128 devices in a mesh: dp: 4 (over y_hi, core), ctx: 2 (over y_lo), tp: 16 (over x, z).
Axes of the slice: x: 4, y: 4 (y_hi: 2, y_lo: 2; y = y_hi * 2 + y_lo), z: 4, core: 2. Of those that a mesh axis runs over, the one named last changes fastest.
Arguments:
- queries: bfloat16 [16384, 4096], P(('dp', 'ctx'), 'tp'), may hold values from -16 to 16
- key_rows: bfloat16 [16384, 512], P(('dp', 'ctx', 'tp')), may hold values from -4 to 4
- value_rows: bfloat16 [16384, 512], P(('dp', 'ctx', 'tp')), may hold values from -6 to 6
- span_order: int32 [4], replicated, may hold values from 0 to 3, each once
- out_proj: bfloat16 [4096, 4096], P('tp'), may hold values from -0.09375 to 0.09375
- residual: bfloat16 [16384, 4096], P(('dp', 'ctx', 'tp')), may hold values from -6 to 6
- norm_gain: float32 [4096], replicated, may hold values from 0.1 to 1.9
- expert_ids: int32 [16384, 8], P(('dp', 'ctx', 'tp')), may hold values from 0 to 127, all different within a row; in each aligned block of 128 rows (0 to 127, 128 to 255, ...) at most 9 rows name the same one
- route_weights: float32 [16384, 8], P(('dp', 'ctx', 'tp')), may hold values from 0.1 to 0.4
- w_up: bfloat16 [128, 4096, 768], P(('dp', 'ctx', 'tp')), may hold values from -0.09375 to 0.09375
- w_down: bfloat16 [128, 768, 4096], P(('dp', 'ctx', 'tp')), may hold values from -0.21875 to 0.21875
Outputs:
- layer_out: bfloat16 [16384, 4096], P(('dp', 'ctx', 'tp'))
The draws below stay inside these ranges and needn't reach their ends.
Inputs may be any that keep to these rules, and one draw needn't show every extreme that they name: `expert_ids`: in the 128 rows of one device no expert is named by more than 9 entries, a bound that some block reaches; a row names 8 different experts. `span_order`: each span appears once.
All inputs are finite; a program needn't handle non-finite values.
Results may differ from the reference program's by a relative error of at most 0.01.
Values may be sent and summed in bfloat16 or wider, within the bound.
No kernel may reach another device: no remote copies, remote signals or barrier semaphores. Data moves between devices by JAX's collectives and lax.ppermute only.
A program may use at most 256 MiB of HBM per device.

```python
import math
import jax
import jax.numpy as jnp
import numpy as np
from jax import lax

D = 4096
HD = 128
QH = 32
KVH = 4
FF = 768
TOPK = 8
TOK_DEV = 128
SEQ = 4096
TOKENS = 16384
CH = 1024
EXPERTS = 128
CAP = 9
N_DP = 4
N_CTX = 2
N_TP = 16


def draw_key_rows(key, part):
    key = jax.random.fold_in(key, 3)
    return jnp.clip(jax.random.normal(key, (TOKENS, KVH * HD), jnp.float32), -4.0, 4.0).astype(jnp.bfloat16)


def draw_queries(key, part):
    key = jax.random.fold_in(key, 5)
    return jnp.clip(jax.random.normal(key, (TOKENS, QH * HD), jnp.float32), -4.0, 4.0).astype(jnp.bfloat16)


def steps_of(rng, extent, split, low, top_value):
    factor_of, own = 1.0, jax.random.fold_in(rng, 6)
    for dim, shards_of in split:
        heights = jnp.exp(jax.random.uniform(jax.random.fold_in(own, dim), (shards_of,), jnp.float32, low / len(split), top_value / len(split)))
        factor_of = factor_of * jnp.repeat(heights, extent[dim] // shards_of).reshape([-1 if axis == dim else 1 for axis in range(len(extent))])
    return factor_of


def routed_block(key, own, number, rows, number_of, top, most, lean):
    sequence = jax.random.permutation(key, number_of)
    crowded, usual = shares(number_of, rows * top, most, lean, True), shares(number_of, rows * top, most, lean, False)
    places = jnp.arange(number_of)

    def named(tallies, turn):
        used = int((tallies > 0).sum())
        fixed = max(1, used // 4)
        moved = fixed + (places - fixed + turn * (used - fixed)) % max(1, number_of - fixed)
        return jnp.zeros((number_of,), jnp.int32).at[sequence[jnp.where(places < fixed, places, moved)]].set(jnp.asarray(tallies, jnp.int32))

    tallies = jnp.where(number % 4 == 0, named(crowded, number // 4), named(usual, number - number // 4 - 1))
    mixed = jax.random.permutation(jax.random.fold_in(own, 3), number_of)
    donor, sink = mixed[0:number_of // 2 * 2:2], mixed[1:number_of // 2 * 2:2]
    slack = jnp.minimum(tallies[donor] - 1, most - tallies[sink]) // 2
    slack = jnp.where((donor == sequence[0]) | (sink == sequence[0]) | (tallies[sink] == 0), 0, jnp.maximum(slack, 0))
    moved = jax.random.randint(jax.random.fold_in(own, 4), (number_of // 2,), 0, 1 << 20) % (slack + 1)
    tallies = tallies.at[donor].add(-moved).at[sink].add(moved)
    members = jnp.searchsorted(jnp.cumsum(tallies), jnp.arange(rows * top), side="right").astype(jnp.int32)
    listing = members.reshape(top, rows).T
    listing = listing[jax.random.permutation(jax.random.fold_in(own, 1), rows)]
    turn = jax.random.randint(jax.random.fold_in(own, 2), (rows, 1), 0, top)
    return jnp.take_along_axis(listing, (jnp.arange(top)[None, :] + turn) % top, axis=1)


def shares(number_of, total, limit, lean, full):
    loads = [(1 << 20) // math.isqrt(standing ** lean) + 1 for standing in range(1, number_of + 1)]
    largest = limit if full else min(limit, max(-(-total // number_of), total * loads[0] // sum(loads)))
    least = 1 if total - largest >= number_of - 1 else 0
    given, rest = [largest] + [least] * (number_of - 1), total - largest - least * (number_of - 1)
    while rest > 0:
        free = [i for i in range(1, number_of) if given[i] < largest] or [i for i in range(1, number_of) if given[i] < limit]
        whole, left = sum([loads[i] for i in free]), rest
        for i in free:
            extra = min(limit - given[i], max(1, left * loads[i] // whole), rest)
            given[i] = given[i] + extra
            rest = rest - extra
    return np.array(given)


def noise(key, dims, deviation, limit, pieces=(), held_as=jnp.bfloat16):
    result = jax.random.normal(key, dims, jnp.float32) * deviation
    if len(pieces) > 0:
        result = steps_of(key, dims, pieces, -0.22, 0.18) * result
    return jnp.clip(result, min=-limit, max=limit).astype(held_as)


def setup_inputs(seed: int = 0) -> dict:
    key_list = jax.random.split(jax.random.key(seed), 12)
    queries = draw_queries(jax.random.fold_in(key_list[11], 71), 0)
    key_rows = draw_key_rows(jax.random.fold_in(key_list[11], 71), 0)
    value_rows = noise(key_list[2], (TOKENS, KVH * HD), 1.0, 6.0, ((0, 128),))
    span_order = jax.random.permutation(key_list[3], 2 * N_CTX).astype(jnp.int32)
    out_proj = noise(key_list[4], (QH * HD, D), (QH * HD) ** -0.5, 0.09375, ((0, 16),))
    residual = noise(key_list[5], (TOKENS, D), 1.0, 6.0, ((0, 128),))
    norm_gain = jnp.clip(1.0 + 0.18 * jax.random.normal(key_list[6], (D,), jnp.float32), 0.1, 1.9)
    expert_ids_keys = jax.random.split(jax.random.fold_in(key_list[7], 1), TOKENS // TOK_DEV)
    expert_ids_turns = jax.random.permutation(jax.random.fold_in(key_list[7], 3), TOKENS // TOK_DEV)
    expert_ids = jax.vmap(lambda own, number: routed_block(jax.random.fold_in(key_list[7], 2), own, number, TOK_DEV, EXPERTS, TOPK, CAP, 2))(expert_ids_keys, expert_ids_turns).reshape((TOKENS, TOPK))
    route_weights = jnp.clip(0.1 + 0.3 * jax.random.uniform(key_list[8], (TOKENS, TOPK), jnp.float32) ** steps_of(key_list[8], (TOKENS, TOPK), ((0, 128),), -0.2, 0.2), 0.1, 0.4)
    w_up = noise(key_list[9], (EXPERTS, D, FF), D ** -0.5, 0.09375, ((0, 128),))
    w_down = noise(key_list[10], (EXPERTS, FF, D), FF ** -0.5, 0.21875, ((0, 128),))
    return dict(queries=queries, key_rows=key_rows, value_rows=value_rows, span_order=span_order, out_proj=out_proj, residual=residual, norm_gain=norm_gain, expert_ids=expert_ids, route_weights=route_weights, w_up=w_up, w_down=w_down)


NEGATIVE = -1e+30

def positions_of(span_order):
    places = jnp.arange(SEQ, dtype=jnp.int32)
    slot_ids = places // CH
    owners = lax.optimization_barrier(jnp.sum(jnp.where(slot_ids[:, None] == jnp.arange(2 * N_CTX, dtype=jnp.int32)[None, :], span_order[None, :], 0), axis=1))
    return (owners * CH + places % CH).astype(jnp.int32)

def attend(query_block, key_block, value_block, visible):
    group = QH // KVH
    query_heads = query_block.reshape(SEQ, QH, HD)
    key_heads = key_block.reshape(SEQ, KVH, HD)
    value_heads = value_block.reshape(SEQ, KVH, HD)
    scale = 1.0 / math.sqrt(HD)

    def one_head(head):
        query_one = lax.dynamic_index_in_dim(query_heads, head, 1, keepdims=False)
        key_one = lax.dynamic_index_in_dim(key_heads, head // group, 1, keepdims=False)
        value_one = lax.dynamic_index_in_dim(value_heads, head // group, 1, keepdims=False)
        scores = jnp.dot(query_one, key_one.T, preferred_element_type=jnp.float32) * scale
        scores = jnp.where(visible, scores, NEGATIVE)
        peak = lax.optimization_barrier(jnp.max(scores, axis=1, keepdims=True))
        weights = jnp.where(visible, jnp.exp(scores - peak), 0.0)
        totals = lax.optimization_barrier(jnp.sum(weights, axis=1, keepdims=True))
        mixed = jnp.dot(weights.astype(jnp.bfloat16), value_one, preferred_element_type=jnp.float32)
        return (mixed / totals).astype(jnp.bfloat16)
    heads = lax.map(one_head, jnp.arange(QH, dtype=jnp.int32))
    return jnp.transpose(heads, (1, 0, 2)).reshape(SEQ, QH * HD)

def route(normed, expert_ids, route_weights, w_up, w_down):
    flat_ids = expert_ids.reshape(-1)
    ordering = jnp.argsort(flat_ids, stable=True).astype(jnp.int32)
    counts = jax.ops.segment_sum(jnp.ones_like(flat_ids), flat_ids, EXPERTS).astype(jnp.int32)
    offsets = (jnp.cumsum(counts) - counts).astype(jnp.int32)
    longest = EXPERTS * CAP
    ordering = jnp.concatenate([ordering, jnp.zeros((longest,), jnp.int32)])
    flat_weights = route_weights.reshape(-1)

    def serve(mixture, expert):
        entries = lax.dynamic_slice_in_dim(ordering, offsets[expert], longest)
        live = jnp.arange(longest, dtype=jnp.int32) < counts[expert]
        token_ids = entries // TOPK
        inputs = normed[token_ids]
        inner = jax.nn.silu(jnp.dot(inputs, w_up[expert], preferred_element_type=jnp.float32)).astype(jnp.bfloat16)
        output = lax.optimization_barrier(jnp.dot(inner, w_down[expert], preferred_element_type=jnp.float32).astype(jnp.bfloat16))
        factor = jnp.where(live, flat_weights[entries], 0.0)
        return (mixture.at[token_ids].add(output.astype(jnp.float32) * factor[:, None]), None)
    mixture, _ = lax.scan(serve, jnp.zeros((TOKENS, D), jnp.float32), jnp.arange(EXPERTS, dtype=jnp.int32))
    return mixture

def reference(queries, key_rows, value_rows, span_order, out_proj, residual, norm_gain, expert_ids, route_weights, w_up, w_down):
    places = positions_of(span_order)
    visible = places[None, :] <= places[:, None]
    width = QH * HD // N_TP
    blocks = []
    for replica in range(N_DP):
        lower = replica * SEQ
        context = attend(queries[lower:lower + SEQ], key_rows[lower:lower + SEQ], value_rows[lower:lower + SEQ], visible)
        projected = jnp.zeros((SEQ, D), jnp.float32)
        for shard in range(N_TP):
            term = jnp.dot(context[:, shard * width:(shard + 1) * width], out_proj[shard * width:(shard + 1) * width], preferred_element_type=jnp.float32)
            rounded = lax.optimization_barrier(term.astype(jnp.bfloat16))
            projected = projected + rounded.astype(jnp.float32)
        blocks.append(projected)
    state = residual.astype(jnp.float32) + jnp.concatenate(blocks, axis=0)
    normed = (state * lax.rsqrt(lax.optimization_barrier(jnp.mean(state * state, axis=1, keepdims=True)) + 1e-06) * norm_gain).astype(jnp.bfloat16)
    mixture = route(normed, expert_ids, route_weights, w_up, w_down)
    return (state + mixture).astype(jnp.bfloat16)
```

```python
import functools
import math

import jax
import jax.numpy as jnp
from jax import lax
from jax.experimental import pallas as pl
from jax.experimental.pallas import tpu as pltpu
from jax.sharding import PartitionSpec as P

HD = 128
KVH = 4
SIDE = 4
TOKENS = 128
SLOTS = 8
SEG = 512
BLOCK = 512
NEGATIVE = -1e30
MIB = 1 << 20
F32 = jnp.float32
BF16 = jnp.bfloat16


def shift_x(value, step):
    return lax.ppermute(
        value,
        "tp",
        [(x * SIDE + z, (x + step) % SIDE * SIDE + z) for x in range(SIDE) for z in range(SIDE)],
    )


def shift_z(value, step):
    return lax.ppermute(
        value,
        "tp",
        [(x * SIDE + z, x * SIDE + (z + step) % SIDE) for x in range(SIDE) for z in range(SIDE)],
    )


def swap_ctx(value):
    return lax.ppermute(value, "ctx", [(0, 1), (1, 0)])


def swap_core(value):
    return lax.ppermute(value, "dp", [(0, 1), (1, 0), (2, 3), (3, 2)])


def gather_ring(shift, rows):
    half = rows.shape[0] // 2
    before, after = shift(rows, 1), shift(rows, -1)
    far_low, far_high = shift(before[:half], 1), shift(after[half:], -1)
    return jnp.concatenate([rows, before, far_low, far_high, after], axis=0)


def exchange(shift, blocks):
    return [blocks[0], shift(blocks[1], 1), shift(blocks[2], 2), shift(blocks[3], -1)]


def call(kernel, name, out_shape, in_specs, out_specs, grid=(), scratch=(), limit=32, cost=None):
    return pl.pallas_call(
        kernel,
        name=name,
        out_shape=out_shape,
        grid=grid,
        in_specs=in_specs,
        out_specs=out_specs,
        scratch_shapes=list(scratch),
        compiler_params=pltpu.CompilerParams(vmem_limit_bytes=limit * MIB),
        cost_estimate=cost,
    )


def smem():
    return pl.BlockSpec(memory_space=pltpu.SMEM)


def vmem():
    return pl.BlockSpec(memory_space=pltpu.VMEM)


def dot(left, right):
    return jnp.dot(left, right, preferred_element_type=F32)


def dot_nt(left, right):
    return lax.dot_general(left, right, (((1,), (1,)), ((), ())), preferred_element_type=F32)


def attention_kernel(meta, q_ref, *refs):
    pieces, refs = refs[:8], refs[8:]
    outs_x, outs_z, (keys, values, sums, context) = refs[:4], refs[4:8], refs[8:]
    ctx, x, z = meta[4], meta[5], meta[6]
    factor = math.log2(math.e) / math.sqrt(HD)

    for number, piece in enumerate(pieces):
        part = lax.rem(ctx + number % 2, 2)
        back = (0, 1, 3, 2)[number // 2]
        z_of = lax.rem(z + SIDE - back, SIDE)
        for block in range(SIDE):
            x_of = lax.rem(x + SIDE - block, SIDE)
            place = meta[part * 2 + x_of // 2] * 8 + lax.rem(x_of, 2) * SIDE + z_of
            rows = pl.ds(pl.multiple_of(place * HD, HD), HD)
            keys[rows, :] = piece[block, :, :HD]
            values[:, rows] = piece[block, :, HD:].T

    def step(chunk, state, heads, masked):
        rows = pl.ds(pl.multiple_of(chunk * BLOCK, BLOCK), BLOCK)
        key_block = keys[rows, :]
        value_block = values[:, rows]
        scores = [dot_nt(key_block, head) for head in heads]
        if masked:
            seen = lax.broadcasted_iota(jnp.int32, (BLOCK, BLOCK), 0) <= lax.broadcasted_iota(
                jnp.int32, (BLOCK, BLOCK), 1
            )
            scores = [jnp.where(seen, score, NEGATIVE) for score in scores]
        later = []
        for head, (peak, total) in enumerate(state):
            new_peak = jnp.maximum(peak, jnp.max(scores[head], axis=0, keepdims=True))
            weights = jnp.exp2(scores[head] * factor - new_peak * factor)
            fading = jnp.exp2((peak - new_peak) * factor)
            new_total = total * fading + jnp.sum(weights, axis=0, keepdims=True)
            sums[head] = sums[head] * fading + dot(value_block, weights.astype(BF16))
            later.append((new_peak, new_total))
        return tuple(later)

    for chunk in range(4):
        mine = meta[ctx * 2 + chunk // 2] * 2 + chunk % 2
        heads = [
            q_ref[chunk * BLOCK : (chunk + 1) * BLOCK, head * HD : (head + 1) * HD]
            for head in range(2)
        ]
        sums[...] = jnp.zeros_like(sums)
        first = (jnp.full((1, BLOCK), NEGATIVE, F32), jnp.zeros((1, BLOCK), F32))
        state = lax.fori_loop(
            0, mine, lambda i, s: step(i, s, heads, False), (first, first)
        )
        state = step(mine, state, heads, True)
        for head, (_, total) in enumerate(state):
            mixed = (sums[head] / total).T.astype(BF16)
            context[chunk * BLOCK : (chunk + 1) * BLOCK, head * HD : (head + 1) * HD] = mixed

    for step_of in range(SIDE):
        to_x = lax.rem(x + step_of, SIDE)
        to_z = lax.rem(z + step_of, SIDE)
        outs_x[step_of][...] = context[pl.ds(pl.multiple_of(to_x * BLOCK, BLOCK), BLOCK), :]
        for block in range(SIDE):
            rows = pl.ds(pl.multiple_of(block * BLOCK + to_z * TOKENS, TOKENS), TOKENS)
            outs_z[step_of][block * TOKENS : (block + 1) * TOKENS, :] = context[rows, :]


def attention(meta, queries, pieces):
    rows, width = queries.shape
    return call(
        attention_kernel,
        "attention",
        [jax.ShapeDtypeStruct((BLOCK, width), BF16)] * 8,
        [smem()] + [vmem()] * 9,
        [vmem()] * 8,
        scratch=[
            pltpu.VMEM((2 * rows, HD), BF16),
            pltpu.VMEM((HD, 2 * rows), BF16),
            pltpu.VMEM((2, HD, BLOCK), F32),
            pltpu.VMEM((rows, width), BF16),
        ],
        cost=pl.CostEstimate(
            flops=7 * 10**9, bytes_accessed=5 * 10**6, transcendentals=14 * 10**6
        ),
    )(meta, queries, *pieces)


def projection_kernel(axis, meta, *refs):
    context, weights, outs, held = refs[:4], refs[4:6], refs[6:10], refs[10]
    me = meta[axis]
    width = context[0].shape[1]
    columns = 256
    for side, weight in enumerate(weights):
        for start in range(0, weight.shape[1], columns):
            total = None
            for number, rows in enumerate(context):
                term = dot(
                    rows[...],
                    weight[number * width : (number + 1) * width, start : start + columns],
                )
                total = term if total is None else total + term
            held[:, side * weight.shape[1] + start : side * weight.shape[1] + start + columns] = (
                total.astype(BF16)
            )
    for number, out in enumerate(outs):
        to = lax.rem(me + number, SIDE)
        out[...] = held[pl.ds(pl.multiple_of(to * TOKENS, TOKENS), TOKENS), :]


def projection(axis, meta, context, weights):
    columns = 2 * weights[0].shape[1]
    return call(
        functools.partial(projection_kernel, axis),
        "projection",
        [jax.ShapeDtypeStruct((TOKENS, columns), BF16)] * 4,
        [smem()] + [vmem()] * 6,
        [vmem()] * 4,
        scratch=[pltpu.VMEM((SIDE * TOKENS, columns), BF16)],
        cost=pl.CostEstimate(
            flops=2 * 512 * 1024 * columns, bytes_accessed=7 * 10**6, transcendentals=0
        ),
    )(meta, *context, *weights)


def dispatch_kernel(meta, *refs):
    terms_z, terms_x, refs = refs[:4], refs[4:8], refs[8:]
    residual, gain, main, over, outgoing, state, normed = refs
    step = pl.program_id(0)
    half = terms_z[0].shape[1]
    quarter = half // 2
    core = meta[7]

    @pl.when(step == 0)
    def _():
        for base, terms in ((0, terms_z), (half, terms_x)):
            for side in range(2):
                place = base + quarter * lax.rem(core + side, 2)
                columns = pl.ds(pl.multiple_of(place, quarter), quarter)
                part = slice(side * quarter, (side + 1) * quarter)
                total = terms[0][:, part].astype(F32)
                for term in terms[1:]:
                    total = total + term[:, part].astype(F32)
                state[:, columns] = residual[:, columns].astype(F32) + total
        value = state[...]
        scale = lax.rsqrt(jnp.mean(value * value, axis=1, keepdims=True) + 1e-06)
        for segment in range(SLOTS):
            columns = slice(segment * SEG, (segment + 1) * SEG)
            normed[segment] = (state[:, columns] * scale * gain[:, columns]).astype(BF16)

    @pl.when(step < SLOTS)
    def _():
        outgoing[...] = dot(main[...], normed[step]).astype(BF16)

    @pl.when(step == SLOTS)
    def _():
        slot = lax.rem(lax.broadcasted_iota(jnp.int32, over.shape, 0), SLOTS)
        total = None
        for segment in range(SLOTS):
            picked = jnp.where(slot == segment, over[...], 0.0).astype(BF16)
            term = dot(picked, normed[segment])
            total = term if total is None else total + term
        outgoing[...] = total.astype(BF16)


def dispatch(meta, terms_z, terms_x, residual, gain, main, over):
    rows, width = main.shape[0], residual.shape[1]
    return call(
        dispatch_kernel,
        "dispatch",
        [
            jax.ShapeDtypeStruct((rows, width + SEG), BF16),
            jax.ShapeDtypeStruct((TOKENS, width), F32),
        ],
        [smem()] + [vmem()] * 12,
        [
            pl.BlockSpec((rows, SEG), lambda i: (0, i)),
            pl.BlockSpec((TOKENS, width), lambda i: (0, 0)),
        ],
        grid=(SLOTS + 1,),
        scratch=[pltpu.VMEM((SLOTS, TOKENS, SEG), BF16)],
        cost=pl.CostEstimate(flops=3 * 10**9, bytes_accessed=16 * 10**6, transcendentals=0),
    )(meta, *terms_z, *terms_x, residual, gain, main, over)


EXPERT_ROWS = 256


def expert_kernel(rows_ref, over_ref, up_ref, down_ref, out_ref, spread):
    step = pl.program_id(0)
    width = down_ref.shape[1]

    def act(value):
        return (value / (1.0 + jnp.exp(-value))).astype(BF16)

    @pl.when(step == 0)
    def _():
        shape = (TOKENS, TOKENS * SLOTS)
        row = lax.broadcasted_iota(jnp.int32, shape, 0)
        column = lax.broadcasted_iota(jnp.int32, shape, 1)
        total = None
        for segment in range(SLOTS):
            pick = (column == row * SLOTS + segment).astype(BF16)
            part = dot(pick, over_ref[...]).astype(BF16)
            term = dot(part, up_ref[0, segment * SEG : (segment + 1) * SEG, :])
            total = term if total is None else total + term
        inner = act(total)
        shape = (TOKENS * SLOTS, TOKENS)
        row = lax.broadcasted_iota(jnp.int32, shape, 0)
        column = lax.broadcasted_iota(jnp.int32, shape, 1)
        total = None
        for segment in range(SLOTS):
            put = (row == column * SLOTS + segment).astype(BF16)
            part = dot(inner, down_ref[0, :, segment * SEG : (segment + 1) * SEG]).astype(BF16)
            term = dot(put, part)
            total = term if total is None else total + term
        spread[...] = total.astype(BF16)

    width = down_ref.shape[2]
    inner = act(dot(rows_ref[:, :width], up_ref[0]))
    for segment in range(SLOTS):
        columns = slice(segment * SEG, (segment + 1) * SEG)
        out_ref[:, columns] = dot(inner, down_ref[0, :, columns]).astype(BF16)
    mine = pl.ds(pl.multiple_of(step * EXPERT_ROWS, EXPERT_ROWS), EXPERT_ROWS)
    out_ref[:, width:] = spread[mine, :]


def experts(arrived, up, down):
    rows, columns = arrived.shape
    inner = up.shape[2]
    return call(
        expert_kernel,
        "experts",
        jax.ShapeDtypeStruct((rows, columns), BF16),
        [
            pl.BlockSpec((EXPERT_ROWS, columns), lambda i: (i, 0)),
            pl.BlockSpec((rows, SEG), lambda i: (0, SLOTS)),
            pl.BlockSpec(up.shape, lambda i: (0, 0, 0), pipeline_mode=pl.Buffered(1)),
            pl.BlockSpec(down.shape, lambda i: (0, 0, 0), pipeline_mode=pl.Buffered(1)),
        ],
        pl.BlockSpec((EXPERT_ROWS, columns), lambda i: (i, 0)),
        grid=(rows // EXPERT_ROWS,),
        scratch=[pltpu.VMEM((rows, SEG), BF16)],
        limit=48,
        cost=pl.CostEstimate(
            flops=4 * rows * columns * inner,
            bytes_accessed=32 * 10**6,
            transcendentals=rows * inner,
        ),
    )(arrived, arrived, up, down)


def combine_kernel(main, over, rows_ref, over_ref, state, out):
    step = pl.program_id(0)
    slot = lax.rem(lax.broadcasted_iota(jnp.int32, over.shape, 1), SLOTS)
    picked = jnp.where(slot == step, over[...], 0.0).astype(BF16)
    total = dot(main[...], rows_ref[...]) + dot(picked, over_ref[...])
    out[...] = (state[...] + (total[:TOKENS] + total[TOKENS:])).astype(BF16)


def combine(main, over, returned, state):
    rows, width = returned.shape[0], state.shape[1]
    return call(
        combine_kernel,
        "combine",
        jax.ShapeDtypeStruct(state.shape, BF16),
        [
            vmem(),
            vmem(),
            pl.BlockSpec((rows, SEG), lambda i: (0, i)),
            pl.BlockSpec((rows, SEG), lambda i: (0, SLOTS)),
            pl.BlockSpec((TOKENS, SEG), lambda i: (0, i)),
        ],
        pl.BlockSpec((TOKENS, SEG), lambda i: (0, i)),
        grid=(width // SEG,),
        cost=pl.CostEstimate(flops=4 * 10**9, bytes_accessed=13 * 10**6, transcendentals=0),
    )(main, over, returned, returned, state)


def routes(expert_ids, route_weights, n_experts):
    tokens = expert_ids.shape[0]
    chosen = expert_ids.T[:, None, :] == jnp.arange(n_experts, dtype=jnp.int32)[None, :, None]
    named = jnp.sum(chosen.astype(F32), axis=0)
    weight = jnp.sum(jnp.where(chosen, route_weights.T[:, None, :], 0.0), axis=0)
    order = jnp.arange(tokens, dtype=jnp.int32)
    earlier = (order[:, None] < order[None, :]).astype(BF16)
    rank = dot(named.astype(BF16), earlier)
    rank = jnp.where(named > 0, rank, -1.0)
    slots = jnp.arange(SLOTS, dtype=jnp.int32).astype(F32)
    hit = rank[:, None, :] == slots[None, :, None]
    late = jnp.broadcast_to((rank == SLOTS)[:, None, :], hit.shape)
    high = lax.reduce_precision(weight, 8, 7)
    low = weight - high

    def rows(mask, value):
        spread = jnp.where(mask, value, 0.0)
        return spread.astype(BF16).reshape(n_experts * SLOTS, tokens)

    def both(mask):
        high_rows = rows(mask, high[:, None, :])
        low_rows = rows(mask, low[:, None, :])
        return jnp.concatenate([high_rows.T, low_rows.T], axis=0)

    return rows(hit, 1.0), rows(late, 1.0), both(hit), both(late)


def local(
    queries,
    key_rows,
    value_rows,
    span_order,
    out_proj,
    residual,
    norm_gain,
    expert_ids,
    route_weights,
    w_up,
    w_down,
):
    n_devices = lax.axis_size("dp") * lax.axis_size("ctx") * lax.axis_size("tp")
    core = lax.axis_index("dp") % 2
    ctx = lax.axis_index("ctx")
    x, z = lax.axis_index("tp") // SIDE, lax.axis_index("tp") % SIDE
    meta = jnp.concatenate([span_order, jnp.stack([ctx, x, z, core]).astype(jnp.int32)])

    def head_block(step):
        start = (x + step) % SIDE * HD
        return jnp.concatenate(
            [
                lax.dynamic_slice_in_dim(key_rows, start, HD, 1),
                lax.dynamic_slice_in_dim(value_rows, start, HD, 1),
            ],
            axis=1,
        )

    own = jnp.stack(exchange(shift_x, [head_block(step) for step in range(SIDE)]))
    other = swap_ctx(own)
    before_own, after_own = shift_z(own, 1), shift_z(own, -1)
    before_other, after_other = shift_z(other, 1), shift_z(other, -1)
    far_own = shift_z(before_own, 1)
    far_other = shift_z(after_other, -1)
    pieces = [
        own,
        other,
        before_own,
        before_other,
        after_own,
        after_other,
        far_own,
        far_other,
    ]

    width = out_proj.shape[1]
    quarter = width // 4

    def weights_of(shift, base):
        part = lax.dynamic_slice_in_dim(out_proj, base + core * quarter, quarter, 1)
        mine = gather_ring(shift, part)
        return [mine, swap_core(mine)]

    weights_x = weights_of(shift_x, 0)
    weights_z = weights_of(shift_z, width // 2)
    main, over, back_main, back_over = routes(expert_ids, route_weights, n_devices)

    parts = attention(meta, queries, pieces)
    terms_z = projection(6, meta, exchange(shift_x, parts[:4]), weights_x)
    terms_x = projection(5, meta, exchange(shift_z, parts[4:]), weights_z)
    terms_z = exchange(shift_z, terms_z)
    terms_x = exchange(shift_x, terms_x)

    outgoing, state = dispatch(
        meta, terms_z, terms_x, residual, norm_gain[None, :], main, over
    )

    def all_to_all(rows):
        blocks = rows.reshape(n_devices, SLOTS, rows.shape[1])
        return lax.all_to_all(
            blocks, ("dp", "ctx", "tp"), split_axis=0, concat_axis=0, tiled=True
        ).reshape(rows.shape)

    arrived = all_to_all(outgoing)
    returned = all_to_all(experts(arrived, w_up, w_down))
    return combine(back_main, back_over, returned, state)


def solution(mesh):
    return jax.shard_map(
        local,
        mesh=mesh,
        in_specs=(
            P(("dp", "ctx"), "tp"),
            P(("dp", "ctx", "tp"), None),
            P(("dp", "ctx", "tp"), None),
            P(),
            P("tp", None),
            P(("dp", "ctx", "tp"), None),
            P(),
            P(("dp", "ctx", "tp"), None),
            P(("dp", "ctx", "tp"), None),
            P(("dp", "ctx", "tp"), None, None),
            P(("dp", "ctx", "tp"), None, None),
        ),
        out_specs=P(("dp", "ctx", "tp"), None),
        check_vma=False,
    )
```

```python
import functools
import math

import jax
import jax.numpy as jnp
from jax import lax
from jax.experimental import pallas as pl
from jax.experimental.pallas import tpu as pltpu
from jax.sharding import PartitionSpec as P

HD = 128
KVH = 4
SIDE = 4
TOKENS = 128
SLOTS = 8
SEG = 512
ROWS = 256
BLOCK = 512
NEGATIVE = -1e30
MIB = 1 << 20
F32 = jnp.float32
BF16 = jnp.bfloat16


def shift_x(value, step):
    return lax.ppermute(
        value,
        "tp",
        [(x * SIDE + z, (x + step) % SIDE * SIDE + z) for x in range(SIDE) for z in range(SIDE)],
    )


def shift_z(value, step):
    return lax.ppermute(
        value,
        "tp",
        [(x * SIDE + z, x * SIDE + (z + step) % SIDE) for x in range(SIDE) for z in range(SIDE)],
    )


def swap_ctx(value):
    return lax.ppermute(value, "ctx", [(0, 1), (1, 0)])


def swap_core(value):
    return lax.ppermute(value, "dp", [(0, 1), (1, 0), (2, 3), (3, 2)])


GROUPS_X = [[x * SIDE + z for x in range(SIDE)] for z in range(SIDE)]
GROUPS_Z = [[x * SIDE + z for z in range(SIDE)] for x in range(SIDE)]


def exchange(shift, blocks):
    return [blocks[0], shift(blocks[1], 1), shift(blocks[2], 2), shift(blocks[3], -1)]


def call(kernel, name, out_shape, in_specs, out_specs, grid=(), scratch=(), limit=56, cost=None):
    return pl.pallas_call(
        kernel,
        name=name,
        out_shape=out_shape,
        grid=grid,
        in_specs=in_specs,
        out_specs=out_specs,
        scratch_shapes=list(scratch),
        compiler_params=pltpu.CompilerParams(vmem_limit_bytes=limit * MIB),
        cost_estimate=cost,
    )


def smem():
    return pl.BlockSpec(memory_space=pltpu.SMEM)


def vmem():
    return pl.BlockSpec(memory_space=pltpu.VMEM)


def whole(array):
    zeros = (0,) * array.ndim
    return pl.BlockSpec(array.shape, lambda *_: zeros, pipeline_mode=pl.Buffered(1))


def dot(left, right):
    return jnp.dot(left, right, preferred_element_type=F32)


def dot_nt(left, right):
    return lax.dot_general(left, right, (((1,), (1,)), ((), ())), preferred_element_type=F32)


def attention_kernel(meta, q_ref, *refs):
    pieces, refs = refs[:8], refs[8:]
    outs_x, outs_z, refs = refs[:4], refs[4:8], refs[8:]
    keys, values, sums, peaks, totals, context = refs[:6]
    even, odd = refs[6:8], refs[8:10]
    ctx, x, z = meta[4], meta[5], meta[6]
    factor = math.log2(math.e) / math.sqrt(HD)

    for number, piece in enumerate(pieces):
        part = lax.rem(ctx + number % 2, 2)
        back = (0, 1, 3, 2)[number // 2]
        z_of = lax.rem(z + SIDE - back, SIDE)
        for block in range(SIDE):
            x_of = lax.rem(x + SIDE - block, SIDE)
            place = meta[part * 2 + x_of // 2] * 8 + lax.rem(x_of, 2) * SIDE + z_of
            rows = pl.ds(pl.multiple_of(place * HD, HD), HD)
            keys[rows, :] = piece[block, :, :HD]
            values[:, rows] = piece[block, :, HD:].T

    def rows_of(chunk):
        return pl.ds(pl.multiple_of(chunk * BLOCK, BLOCK), BLOCK)

    @pl.loop(0, SIDE)
    def _(chunk):
        mine = meta[ctx * 2 + chunk // 2] * 2 + lax.rem(chunk, 2)
        heads = [q_ref[rows_of(chunk), head * HD : (head + 1) * HD] for head in range(2)]
        for head in range(2):
            sums[head] = jnp.zeros((HD, BLOCK), F32)
            peaks[head] = jnp.full((1, BLOCK), NEGATIVE, F32)
            totals[head] = jnp.zeros((1, BLOCK), F32)

        def score(number, held):
            key_block = keys[rows_of(number), :]
            for head in range(2):
                held[head][...] = dot_nt(key_block, heads[head])

        def process(number, held, masked):
            value_block = values[:, rows_of(number)]
            for head in range(2):
                scores = held[head][...]
                if masked:
                    seen = lax.broadcasted_iota(
                        jnp.int32, (BLOCK, BLOCK), 0
                    ) <= lax.broadcasted_iota(jnp.int32, (BLOCK, BLOCK), 1)
                    scores = jnp.where(seen, scores, NEGATIVE)
                peak = peaks[head]
                new_peak = jnp.maximum(peak, jnp.max(scores, axis=0, keepdims=True))
                weights = jnp.exp2(scores * factor - new_peak * factor)
                fading = jnp.exp2((peak - new_peak) * factor)
                peaks[head] = new_peak
                totals[head] = totals[head] * fading + jnp.sum(weights, axis=0, keepdims=True)
                sums[head] = sums[head] * fading + dot(value_block, weights.astype(BF16))

        score(0, even)

        def two(pair, carry):
            score(2 * pair + 1, odd)
            process(2 * pair, even, False)
            score(2 * pair + 2, even)
            process(2 * pair + 1, odd, False)
            return carry

        lax.fori_loop(0, mine // 2, two, 0)

        @pl.when(lax.rem(mine, 2) == 1)
        def _():
            score(mine, odd)
            process(mine - 1, even, False)
            process(mine, odd, True)

        @pl.when(lax.rem(mine, 2) == 0)
        def _():
            process(mine, even, True)

        for head in range(2):
            context[rows_of(chunk), head * HD : (head + 1) * HD] = (
                (sums[head] / totals[head]).T.astype(BF16)
            )

    for step_of in range(SIDE):
        to_x = lax.rem(x + step_of, SIDE)
        to_z = lax.rem(z + step_of, SIDE)
        outs_x[step_of][...] = context[pl.ds(pl.multiple_of(to_x * BLOCK, BLOCK), BLOCK), :]
        for block in range(SIDE):
            rows = pl.ds(pl.multiple_of(block * BLOCK + to_z * TOKENS, TOKENS), TOKENS)
            outs_z[step_of][block * TOKENS : (block + 1) * TOKENS, :] = context[rows, :]


def attention(meta, queries, pieces):
    rows, width = queries.shape
    return call(
        attention_kernel,
        "attention",
        [jax.ShapeDtypeStruct((BLOCK, width), BF16)] * 8,
        [smem(), whole(queries)] + [whole(piece) for piece in pieces],
        [pl.BlockSpec((BLOCK, width), lambda: (0, 0))] * 8,
        scratch=[
            pltpu.VMEM((2 * rows, HD), BF16),
            pltpu.VMEM((HD, 2 * rows), BF16),
            pltpu.VMEM((2, HD, BLOCK), F32),
            pltpu.VMEM((2, 1, BLOCK), F32),
            pltpu.VMEM((2, 1, BLOCK), F32),
            pltpu.VMEM((rows, width), BF16),
        ]
        + [pltpu.VMEM((BLOCK, BLOCK), F32)] * 4,
        cost=pl.CostEstimate(
            flops=7 * 10**9, bytes_accessed=5 * 10**6, transcendentals=14 * 10**6
        ),
    )(meta, queries, *pieces)


def projection_kernel(axis_in, axis_out, meta, *refs):
    context, weights, outs, held = refs[:4], refs[4:6], refs[6:10], refs[10]
    me_in, me = meta[axis_in], meta[axis_out]
    width = context[0].shape[1]
    columns = 256
    for side, weight in enumerate(weights):
        for start in range(0, weight.shape[1], columns):
            total = None
            for number, rows in enumerate(context):
                source = lax.rem(me_in + SIDE - number, SIDE)
                part = pl.ds(pl.multiple_of(source * width, width), width)
                term = dot(rows[...], weight[part, start : start + columns])
                total = term if total is None else total + term
            held[:, side * weight.shape[1] + start : side * weight.shape[1] + start + columns] = (
                total.astype(BF16)
            )
    for number, out in enumerate(outs):
        to = lax.rem(me + number, SIDE)
        out[...] = held[pl.ds(pl.multiple_of(to * TOKENS, TOKENS), TOKENS), :]


def projection(axis_in, axis_out, meta, context, weights):
    columns = 2 * weights[0].shape[1]
    return call(
        functools.partial(projection_kernel, axis_in, axis_out),
        "projection",
        [jax.ShapeDtypeStruct((TOKENS, columns), BF16)] * 4,
        [smem()] + [whole(array) for array in (*context, *weights)],
        [pl.BlockSpec((TOKENS, columns), lambda: (0, 0))] * 4,
        scratch=[pltpu.VMEM((SIDE * TOKENS, columns), BF16)],
        cost=pl.CostEstimate(
            flops=2 * 512 * 1024 * columns, bytes_accessed=7 * 10**6, transcendentals=0
        ),
    )(meta, *context, *weights)


def wide_scratch():
    return pltpu.VMEM((SEG // HD, TOKENS * SLOTS, HD), F32)


def widen(wide, rows_ref):
    for part in range(SEG // HD):
        wide[part] = rows_ref[:, part * HD : (part + 1) * HD].astype(F32)


def narrow(wide):
    return jnp.concatenate([wide[part].astype(BF16) for part in range(SEG // HD)], axis=1)


def gather_rows(wide, segment):
    rows = pl.ds(segment, TOKENS, stride=SLOTS)
    return jnp.concatenate([wide[part, rows, :] for part in range(SEG // HD)], axis=1).astype(BF16)


def scatter_rows(wide, segment, value):
    rows = pl.ds(segment, TOKENS, stride=SLOTS)
    for part in range(SEG // HD):
        wide[part, rows, :] = value[:, part * HD : (part + 1) * HD]


def dispatch_kernel(meta, *refs):
    terms_z, terms_x, refs = refs[:4], refs[4:8], refs[8:]
    residual, gain, main, late, outgoing, state, normed, wide, spread = refs
    step = pl.program_id(0)
    half = terms_z[0].shape[1]
    quarter = half // 2
    core = meta[7]

    @pl.when(step == 0)
    def _():
        for base, terms in ((0, terms_z), (half, terms_x)):
            for side in range(2):
                place = base + quarter * lax.rem(core + side, 2)
                columns = pl.ds(pl.multiple_of(place, quarter), quarter)
                part = slice(side * quarter, (side + 1) * quarter)
                total = terms[0][:, part].astype(F32)
                for term in terms[1:]:
                    total = total + term[:, part].astype(F32)
                state[:, columns] = residual[:, columns].astype(F32) + total
        value = state[...]
        scale = lax.rsqrt(jnp.mean(value * value, axis=1, keepdims=True) + 1e-06)
        for segment in range(SLOTS):
            columns = slice(segment * SEG, (segment + 1) * SEG)
            normed[segment] = (state[:, columns] * scale * gain[:, columns]).astype(BF16)

        for segment in range(SLOTS):
            scatter_rows(wide, segment, dot(late[...], normed[segment]))
        spread[...] = narrow(wide)

    for segment in range(SLOTS):
        columns = slice(segment * SEG, (segment + 1) * SEG)
        outgoing[:, columns] = dot(main[...], normed[segment]).astype(BF16)
    rows = outgoing.shape[0]
    outgoing[:, 2 * half :] = spread[pl.ds(pl.multiple_of(step * rows, rows), rows), :]


def dispatch(meta, terms_z, terms_x, residual, gain, main, late):
    rows, width = main.shape[0], residual.shape[1]
    arrays = (*terms_z, *terms_x, residual, gain)
    return call(
        dispatch_kernel,
        "dispatch",
        [
            jax.ShapeDtypeStruct((rows, width + SEG), BF16),
            jax.ShapeDtypeStruct((TOKENS, width), F32),
        ],
        [smem()]
        + [whole(a) for a in arrays]
        + [pl.BlockSpec((ROWS, TOKENS), lambda i: (i, 0)), whole(late)],
        [
            pl.BlockSpec((ROWS, width + SEG), lambda i: (i, 0)),
            pl.BlockSpec((TOKENS, width), lambda i: (0, 0)),
        ],
        grid=(rows // ROWS,),
        scratch=[
            pltpu.VMEM((SLOTS, TOKENS, SEG), BF16),
            wide_scratch(),
            pltpu.VMEM((rows, SEG), BF16),
        ],
        cost=pl.CostEstimate(flops=3 * 10**9, bytes_accessed=16 * 10**6, transcendentals=0),
    )(meta, *arrays, main, late)


def expert_kernel(rows_ref, over_ref, up_ref, down_ref, out_ref, wide, spread):
    step = pl.program_id(0)
    width = down_ref.shape[2]

    def act(value):
        return (value / (1.0 + jnp.exp(-value))).astype(BF16)

    @pl.when(step == 0)
    def _():
        widen(wide, over_ref)
        total = None
        for segment in range(SLOTS):
            part = up_ref[0, segment * SEG : (segment + 1) * SEG, :]
            term = dot(gather_rows(wide, segment), part)
            total = term if total is None else total + term
        inner = act(total)
        for segment in range(SLOTS):
            part = down_ref[0, :, segment * SEG : (segment + 1) * SEG]
            scatter_rows(wide, segment, dot(inner, part))
        spread[...] = narrow(wide)

    inner = act(dot(rows_ref[:, :width], up_ref[0]))
    for segment in range(SLOTS):
        columns = slice(segment * SEG, (segment + 1) * SEG)
        out_ref[:, columns] = dot(inner, down_ref[0, :, columns]).astype(BF16)
    mine = pl.ds(pl.multiple_of(step * ROWS, ROWS), ROWS)
    out_ref[:, width:] = spread[mine, :]


def experts(arrived, up, down):
    rows, columns = arrived.shape
    inner = up.shape[2]
    return call(
        expert_kernel,
        "experts",
        jax.ShapeDtypeStruct((rows, columns), BF16),
        [
            pl.BlockSpec((ROWS, columns), lambda i: (i, 0)),
            pl.BlockSpec((rows, SEG), lambda i: (0, SLOTS)),
            vmem(),
            vmem(),
        ],
        pl.BlockSpec((ROWS, columns), lambda i: (i, 0)),
        grid=(rows // ROWS,),
        scratch=[wide_scratch(), pltpu.VMEM((rows, SEG), BF16)],
        limit=40,
        cost=pl.CostEstimate(
            flops=4 * rows * columns * inner,
            bytes_accessed=32 * 10**6,
            transcendentals=rows * inner,
        ),
    )(arrived, arrived, up, down)


def combine_kernel(main, late, rows_ref, over_ref, state, out, total, wide):
    step = pl.program_id(0)
    segments = [(i, slice(i * SEG, (i + 1) * SEG)) for i in range(SLOTS)]

    def both(value):
        return value[:TOKENS] + value[TOKENS:]

    @pl.when(step == 0)
    def _():
        widen(wide, over_ref)
        for segment, columns in segments:
            late_part = both(dot(late[...], gather_rows(wide, segment)))
            total[:, columns] = state[:, columns] + late_part

    for segment, columns in segments:
        total[:, columns] += both(dot(main[...], rows_ref[:, columns]))

    @pl.when(step == pl.num_programs(0) - 1)
    def _():
        out[...] = total[...].astype(BF16)


def combine(main, late, returned, state):
    rows, columns = returned.shape
    return call(
        combine_kernel,
        "combine",
        jax.ShapeDtypeStruct(state.shape, BF16),
        [
            pl.BlockSpec((2 * TOKENS, ROWS), lambda i: (0, i)),
            whole(late),
            pl.BlockSpec((ROWS, columns), lambda i: (i, 0)),
            pl.BlockSpec((rows, SEG), lambda i: (0, SLOTS), pipeline_mode=pl.Buffered(1)),
            whole(state),
        ],
        pl.BlockSpec(state.shape, lambda i: (0, 0)),
        grid=(rows // ROWS,),
        scratch=[pltpu.VMEM(state.shape, F32), wide_scratch()],
        cost=pl.CostEstimate(flops=4 * 10**9, bytes_accessed=13 * 10**6, transcendentals=0),
    )(main, late, returned, returned, state)


def routes(expert_ids, route_weights, n_experts):
    tokens = expert_ids.shape[0]
    chosen = expert_ids.T[:, None, :] == jnp.arange(n_experts, dtype=jnp.int32)[None, :, None]
    named = jnp.sum(chosen.astype(F32), axis=0)
    weight = jnp.sum(jnp.where(chosen, route_weights.T[:, None, :], 0.0), axis=0)
    order = jnp.arange(tokens, dtype=jnp.int32)
    earlier = (order[:, None] < order[None, :]).astype(BF16)
    rank = dot(named.astype(BF16), earlier)
    rank = jnp.where(named > 0, rank, -1.0)
    slots = jnp.arange(SLOTS, dtype=jnp.int32).astype(F32)
    hit = rank[:, None, :] == slots[None, :, None]
    late = rank == SLOTS
    high = lax.reduce_precision(weight, 8, 7)
    low = weight - high

    def rows(value):
        spread = jnp.where(hit, value, 0.0)
        return spread.astype(BF16).reshape(n_experts * SLOTS, tokens)

    back_main = jnp.concatenate([rows(high[:, None, :]).T, rows(low[:, None, :]).T], axis=0)
    back_late = jnp.concatenate(
        [jnp.where(late, value, 0.0).astype(BF16).T for value in (high, low)], axis=0
    )
    return rows(1.0), late.astype(BF16), back_main, back_late


def local(
    queries,
    key_rows,
    value_rows,
    span_order,
    out_proj,
    residual,
    norm_gain,
    expert_ids,
    route_weights,
    w_up,
    w_down,
):
    n_devices = lax.axis_size("dp") * lax.axis_size("ctx") * lax.axis_size("tp")
    core = lax.axis_index("dp") % 2
    ctx = lax.axis_index("ctx")
    x, z = lax.axis_index("tp") // SIDE, lax.axis_index("tp") % SIDE
    meta = jnp.concatenate([span_order, jnp.stack([ctx, x, z, core]).astype(jnp.int32)])

    def head_block(step):
        start = (x + step) % SIDE * HD
        return jnp.concatenate(
            [
                lax.dynamic_slice_in_dim(key_rows, start, HD, 1),
                lax.dynamic_slice_in_dim(value_rows, start, HD, 1),
            ],
            axis=1,
        )

    width = out_proj.shape[1]
    quarter = width // 4

    def weights_part(base):
        return lax.dynamic_slice_in_dim(out_proj, base + core * quarter, quarter, 1)

    def gathered(part, groups):
        return lax.all_gather(part, "tp", axis=0, tiled=True, axis_index_groups=groups)

    own = jnp.stack(exchange(shift_x, [head_block(step) for step in range(SIDE)]))
    own, part_x, part_z = lax.optimization_barrier(
        (own, weights_part(0), weights_part(width // 2))
    )
    weights_x = gathered(part_x, GROUPS_X)
    weights_z = gathered(part_z, GROUPS_Z)
    other = swap_ctx(own)
    before_own, after_own = shift_z(own, 1), shift_z(own, -1)
    before_other, after_other = shift_z(other, 1), shift_z(other, -1)
    far_own = shift_z(before_own, 1)
    far_other = shift_z(after_other, -1)
    pieces = [
        own,
        other,
        before_own,
        before_other,
        after_own,
        after_other,
        far_own,
        far_other,
    ]

    maps = routes(expert_ids, route_weights, n_devices)

    parts = attention(meta, queries, pieces)
    parts, weights_x = lax.optimization_barrier((parts, weights_x))
    other_x = swap_core(weights_x)
    context_x = exchange(shift_x, parts[:4])
    context_z = exchange(shift_z, parts[4:])
    context_x, context_z = lax.optimization_barrier((context_x, context_z))
    terms_z = projection(5, 6, meta, context_x, [weights_x, other_x])
    terms_z, weights_z = lax.optimization_barrier((terms_z, weights_z))
    other_z = swap_core(weights_z)
    terms_x = projection(6, 5, meta, context_z, [weights_z, other_z])
    terms_z, terms_x = exchange(shift_z, terms_z), exchange(shift_x, terms_x)
    main, late, back_main, back_late = maps

    outgoing, state = dispatch(
        meta, terms_z, terms_x, residual, norm_gain[None, :], main, late
    )

    def all_to_all(rows):
        blocks = rows.reshape(n_devices, SLOTS, rows.shape[1])
        return lax.all_to_all(
            blocks, ("dp", "ctx", "tp"), split_axis=0, concat_axis=0, tiled=True
        ).reshape(rows.shape)

    arrived = all_to_all(outgoing)
    returned = all_to_all(experts(arrived, w_up, w_down))
    return combine(back_main, back_late, returned, state)


def solution(mesh):
    return jax.shard_map(
        local,
        mesh=mesh,
        in_specs=(
            P(("dp", "ctx"), "tp"),
            P(("dp", "ctx", "tp"), None),
            P(("dp", "ctx", "tp"), None),
            P(),
            P("tp", None),
            P(("dp", "ctx", "tp"), None),
            P(),
            P(("dp", "ctx", "tp"), None),
            P(("dp", "ctx", "tp"), None),
            P(("dp", "ctx", "tp"), None, None),
            P(("dp", "ctx", "tp"), None, None),
        ),
        out_specs=P(("dp", "ctx", "tp"), None),
        check_vma=False,
    )
```

```python
import functools
import math

import jax
import jax.numpy as jnp
from jax import lax
from jax.experimental import pallas as pl
from jax.experimental.pallas import tpu as pltpu
from jax.sharding import PartitionSpec as P

HD = 128
KVH = 4
SIDE = 4
TOKENS = 128
SLOTS = 8
SEG = 512
ROWS = 256
BLOCK = 512
NEGATIVE = -1e30
MIB = 1 << 20
F32 = jnp.float32
BF16 = jnp.bfloat16


def shift_x(value, step):
    return lax.ppermute(
        value,
        "tp",
        [(x * SIDE + z, (x + step) % SIDE * SIDE + z) for x in range(SIDE) for z in range(SIDE)],
    )


def shift_z(value, step):
    return lax.ppermute(
        value,
        "tp",
        [(x * SIDE + z, x * SIDE + (z + step) % SIDE) for x in range(SIDE) for z in range(SIDE)],
    )


def swap_ctx(value):
    return lax.ppermute(value, "ctx", [(0, 1), (1, 0)])


def swap_core(value):
    return lax.ppermute(value, "dp", [(0, 1), (1, 0), (2, 3), (3, 2)])


def gather_rows_of(shift, rows):
    return [rows, shift(rows, 1), shift(rows, 2), shift(rows, -1)]


def exchange(shift, blocks):
    return [blocks[0], shift(blocks[1], 1), shift(blocks[2], 2), shift(blocks[3], -1)]


def call(kernel, name, out_shape, in_specs, out_specs, grid=(), scratch=(), limit=56, cost=None):
    return pl.pallas_call(
        kernel,
        name=name,
        out_shape=out_shape,
        grid=grid,
        in_specs=in_specs,
        out_specs=out_specs,
        scratch_shapes=list(scratch),
        compiler_params=pltpu.CompilerParams(vmem_limit_bytes=limit * MIB),
        cost_estimate=cost,
    )


def smem():
    return pl.BlockSpec(memory_space=pltpu.SMEM)


def vmem():
    return pl.BlockSpec(memory_space=pltpu.VMEM)


def whole(array):
    zeros = (0,) * array.ndim
    return pl.BlockSpec(array.shape, lambda *_: zeros, pipeline_mode=pl.Buffered(1))


def dot(left, right):
    return jnp.dot(left, right, preferred_element_type=F32)


def dot_nt(left, right):
    return lax.dot_general(left, right, (((1,), (1,)), ((), ())), preferred_element_type=F32)


def attention_kernel(meta, q_ref, *refs):
    pieces, refs = refs[:8], refs[8:]
    outs_x, outs_z, refs = refs[:4], refs[4:8], refs[8:]
    keys, values, sums, peaks, totals, context = refs[:6]
    even, odd = refs[6:8], refs[8:10]
    ctx, x, z = meta[4], meta[5], meta[6]
    factor = math.log2(math.e) / math.sqrt(HD)

    for number, piece in enumerate(pieces):
        part = lax.rem(ctx + number % 2, 2)
        back = (0, 1, 3, 2)[number // 2]
        z_of = lax.rem(z + SIDE - back, SIDE)
        for block in range(SIDE):
            x_of = lax.rem(x + SIDE - block, SIDE)
            place = meta[part * 2 + x_of // 2] * 8 + lax.rem(x_of, 2) * SIDE + z_of
            rows = pl.ds(pl.multiple_of(place * HD, HD), HD)
            keys[rows, :] = piece[block, :, :HD]
            values[:, rows] = piece[block, :, HD:].T

    def rows_of(chunk):
        return pl.ds(pl.multiple_of(chunk * BLOCK, BLOCK), BLOCK)

    @pl.loop(0, SIDE)
    def _(chunk):
        mine = meta[ctx * 2 + chunk // 2] * 2 + lax.rem(chunk, 2)
        heads = [q_ref[rows_of(chunk), head * HD : (head + 1) * HD] for head in range(2)]
        for head in range(2):
            sums[head] = jnp.zeros((HD, BLOCK), F32)
            peaks[head] = jnp.full((1, BLOCK), NEGATIVE, F32)
            totals[head] = jnp.zeros((1, BLOCK), F32)

        def score(number, held):
            key_block = keys[rows_of(number), :]
            for head in range(2):
                held[head][...] = dot_nt(key_block, heads[head])

        def process(number, held, masked):
            value_block = values[:, rows_of(number)]
            for head in range(2):
                scores = held[head][...]
                if masked:
                    seen = lax.broadcasted_iota(
                        jnp.int32, (BLOCK, BLOCK), 0
                    ) <= lax.broadcasted_iota(jnp.int32, (BLOCK, BLOCK), 1)
                    scores = jnp.where(seen, scores, NEGATIVE)
                peak = peaks[head]
                new_peak = jnp.maximum(peak, jnp.max(scores, axis=0, keepdims=True))
                weights = jnp.exp2(scores * factor - new_peak * factor)
                fading = jnp.exp2((peak - new_peak) * factor)
                peaks[head] = new_peak
                totals[head] = totals[head] * fading + jnp.sum(weights, axis=0, keepdims=True)
                sums[head] = sums[head] * fading + dot(value_block, weights.astype(BF16))

        score(0, even)

        def two(pair, carry):
            score(2 * pair + 1, odd)
            process(2 * pair, even, False)
            score(2 * pair + 2, even)
            process(2 * pair + 1, odd, False)
            return carry

        lax.fori_loop(0, mine // 2, two, 0)

        @pl.when(lax.rem(mine, 2) == 1)
        def _():
            score(mine, odd)
            process(mine - 1, even, False)
            process(mine, odd, True)

        @pl.when(lax.rem(mine, 2) == 0)
        def _():
            process(mine, even, True)

        for head in range(2):
            context[rows_of(chunk), head * HD : (head + 1) * HD] = (
                (sums[head] / totals[head]).T.astype(BF16)
            )

    for step_of in range(SIDE):
        to_x = lax.rem(x + step_of, SIDE)
        to_z = lax.rem(z + step_of, SIDE)
        outs_x[step_of][...] = context[pl.ds(pl.multiple_of(to_x * BLOCK, BLOCK), BLOCK), :]
        for block in range(SIDE):
            rows = pl.ds(pl.multiple_of(block * BLOCK + to_z * TOKENS, TOKENS), TOKENS)
            outs_z[step_of][block * TOKENS : (block + 1) * TOKENS, :] = context[rows, :]


def attention(meta, queries, pieces):
    rows, width = queries.shape
    return call(
        attention_kernel,
        "attention",
        [jax.ShapeDtypeStruct((BLOCK, width), BF16)] * 8,
        [smem(), whole(queries)] + [whole(piece) for piece in pieces],
        [pl.BlockSpec((BLOCK, width), lambda: (0, 0))] * 8,
        scratch=[
            pltpu.VMEM((2 * rows, HD), BF16),
            pltpu.VMEM((HD, 2 * rows), BF16),
            pltpu.VMEM((2, HD, BLOCK), F32),
            pltpu.VMEM((2, 1, BLOCK), F32),
            pltpu.VMEM((2, 1, BLOCK), F32),
            pltpu.VMEM((rows, width), BF16),
        ]
        + [pltpu.VMEM((BLOCK, BLOCK), F32)] * 4,
        cost=pl.CostEstimate(
            flops=7 * 10**9, bytes_accessed=5 * 10**6, transcendentals=14 * 10**6
        ),
    )(meta, queries, *pieces)


def projection_kernel(axis, n_pieces, meta, *refs):
    context, weights, pieces, refs = refs[:4], refs[4:6], refs[6 : 6 + n_pieces], refs[6 + n_pieces :]
    outs, refs = refs[:4], refs[4:]
    joined, held, done = refs if n_pieces else (None, *refs)
    me = meta[axis]
    width = context[0].shape[1]
    columns = 256
    copies = [
        pltpu.make_async_copy(piece, joined.at[pl.ds(i * width, width), :], done.at[i])
        for i, piece in enumerate(pieces)
    ]
    for copy in copies:
        copy.start()
    for side, weight in enumerate(weights):
        for start in range(0, weight.shape[1], columns):
            total = None
            for number, rows in enumerate(context):
                part = weight[number * width : (number + 1) * width, start : start + columns]
                term = dot(rows[...], part)
                total = term if total is None else total + term
            held[:, side * weight.shape[1] + start : side * weight.shape[1] + start + columns] = (
                total.astype(BF16)
            )
    for number, out in enumerate(outs):
        to = lax.rem(me + number, SIDE)
        out[...] = held[pl.ds(pl.multiple_of(to * TOKENS, TOKENS), TOKENS), :]
    for copy in copies:
        copy.wait()


def projection(axis, meta, context, weights, pieces=()):
    columns = 2 * weights[0].shape[1]
    any_space = pl.BlockSpec(memory_space=pl.ANY)
    joined = [jax.ShapeDtypeStruct(weights[0].shape, BF16)] if pieces else []
    return call(
        functools.partial(projection_kernel, axis, len(pieces)),
        "projection",
        [jax.ShapeDtypeStruct((TOKENS, columns), BF16)] * 4 + joined,
        [smem()]
        + [whole(array) for array in (*context, *weights)]
        + [any_space for _ in pieces],
        [pl.BlockSpec((TOKENS, columns), lambda: (0, 0))] * 4 + [any_space for _ in joined],
        scratch=[
            pltpu.VMEM((SIDE * TOKENS, columns), BF16),
            pltpu.SemaphoreType.DMA((SIDE,)),
        ],
        cost=pl.CostEstimate(
            flops=2 * 512 * 1024 * columns, bytes_accessed=7 * 10**6, transcendentals=0
        ),
    )(meta, *context, *weights, *pieces)


def wide_scratch():
    return pltpu.VMEM((SEG // HD, TOKENS * SLOTS, HD), F32)


def widen(wide, rows_ref):
    for part in range(SEG // HD):
        wide[part] = rows_ref[:, part * HD : (part + 1) * HD].astype(F32)


def narrow(wide):
    return jnp.concatenate([wide[part].astype(BF16) for part in range(SEG // HD)], axis=1)


def gather_rows(wide, segment):
    rows = pl.ds(segment, TOKENS, stride=SLOTS)
    return jnp.concatenate([wide[part, rows, :] for part in range(SEG // HD)], axis=1).astype(BF16)


def scatter_rows(wide, segment, value):
    rows = pl.ds(segment, TOKENS, stride=SLOTS)
    for part in range(SEG // HD):
        wide[part, rows, :] = value[:, part * HD : (part + 1) * HD]


def dispatch_kernel(meta, *refs):
    terms_z, terms_x, refs = refs[:4], refs[4:8], refs[8:]
    residual, gain, main, late, outgoing, state, normed, wide, spread = refs
    step = pl.program_id(0)
    half = terms_z[0].shape[1]
    quarter = half // 2
    core = meta[7]

    @pl.when(step == 0)
    def _():
        for base, terms in ((0, terms_z), (half, terms_x)):
            for side in range(2):
                place = base + quarter * lax.rem(core + side, 2)
                columns = pl.ds(pl.multiple_of(place, quarter), quarter)
                part = slice(side * quarter, (side + 1) * quarter)
                total = terms[0][:, part].astype(F32)
                for term in terms[1:]:
                    total = total + term[:, part].astype(F32)
                state[:, columns] = residual[:, columns].astype(F32) + total
        value = state[...]
        scale = lax.rsqrt(jnp.mean(value * value, axis=1, keepdims=True) + 1e-06)
        for segment in range(SLOTS):
            columns = slice(segment * SEG, (segment + 1) * SEG)
            normed[segment] = (state[:, columns] * scale * gain[:, columns]).astype(BF16)

        for segment in range(SLOTS):
            scatter_rows(wide, segment, dot(late[...], normed[segment]))
        spread[...] = narrow(wide)

    for segment in range(SLOTS):
        columns = slice(segment * SEG, (segment + 1) * SEG)
        outgoing[:, columns] = dot(main[...], normed[segment]).astype(BF16)
    rows = outgoing.shape[0]
    outgoing[:, 2 * half :] = spread[pl.ds(pl.multiple_of(step * rows, rows), rows), :]


def dispatch(meta, terms_z, terms_x, residual, gain, main, late):
    rows, width = main.shape[0], residual.shape[1]
    arrays = (*terms_z, *terms_x, residual, gain)
    return call(
        dispatch_kernel,
        "dispatch",
        [
            jax.ShapeDtypeStruct((rows, width + SEG), BF16),
            jax.ShapeDtypeStruct((TOKENS, width), F32),
        ],
        [smem()]
        + [whole(a) for a in arrays]
        + [pl.BlockSpec((ROWS, TOKENS), lambda i: (i, 0)), whole(late)],
        [
            pl.BlockSpec((ROWS, width + SEG), lambda i: (i, 0)),
            pl.BlockSpec((TOKENS, width), lambda i: (0, 0)),
        ],
        grid=(rows // ROWS,),
        scratch=[
            pltpu.VMEM((SLOTS, TOKENS, SEG), BF16),
            wide_scratch(),
            pltpu.VMEM((rows, SEG), BF16),
        ],
        cost=pl.CostEstimate(flops=3 * 10**9, bytes_accessed=16 * 10**6, transcendentals=0),
    )(meta, *arrays, main, late)


def expert_kernel(rows_ref, over_ref, up_ref, down_hbm, out_ref, wide, spread, down_ref, done):
    step = pl.program_id(0)
    width = down_ref.shape[2]
    fetch = pltpu.make_async_copy(down_hbm, down_ref, done)

    def act(value):
        return (value / (1.0 + jnp.exp(-value))).astype(BF16)

    @pl.when(step == 0)
    def _():
        fetch.start()
        widen(wide, over_ref)
        total = None
        for segment in range(SLOTS):
            part = up_ref[0, segment * SEG : (segment + 1) * SEG, :]
            term = dot(gather_rows(wide, segment), part)
            total = term if total is None else total + term
        inner = act(total)
        fetch.wait()
        for segment in range(SLOTS):
            part = down_ref[0, :, segment * SEG : (segment + 1) * SEG]
            scatter_rows(wide, segment, dot(inner, part))
        spread[...] = narrow(wide)

    inner = act(dot(rows_ref[:, :width], up_ref[0]))
    for segment in range(SLOTS):
        columns = slice(segment * SEG, (segment + 1) * SEG)
        out_ref[:, columns] = dot(inner, down_ref[0, :, columns]).astype(BF16)
    mine = pl.ds(pl.multiple_of(step * ROWS, ROWS), ROWS)
    out_ref[:, width:] = spread[mine, :]


def experts(arrived, up, down):
    rows, columns = arrived.shape
    inner = up.shape[2]
    return call(
        expert_kernel,
        "experts",
        jax.ShapeDtypeStruct((rows, columns), BF16),
        [
            pl.BlockSpec((ROWS, columns), lambda i: (i, 0)),
            pl.BlockSpec((rows, SEG), lambda i: (0, SLOTS)),
            vmem(),
            pl.BlockSpec(memory_space=pl.ANY),
        ],
        pl.BlockSpec((ROWS, columns), lambda i: (i, 0)),
        grid=(rows // ROWS,),
        scratch=[
            wide_scratch(),
            pltpu.VMEM((rows, SEG), BF16),
            pltpu.VMEM(down.shape, BF16),
            pltpu.SemaphoreType.DMA,
        ],
        limit=46,
        cost=pl.CostEstimate(
            flops=4 * rows * columns * inner,
            bytes_accessed=32 * 10**6,
            transcendentals=rows * inner,
        ),
    )(arrived, arrived, up, down)


def combine_kernel(main, late, rows_ref, over_ref, state, out, total, wide):
    step = pl.program_id(0)
    segments = [(i, slice(i * SEG, (i + 1) * SEG)) for i in range(SLOTS)]

    def both(value):
        return value[:TOKENS] + value[TOKENS:]

    @pl.when(step == 0)
    def _():
        widen(wide, over_ref)
        for segment, columns in segments:
            late_part = both(dot(late[...], gather_rows(wide, segment)))
            total[:, columns] = state[:, columns] + late_part

    for segment, columns in segments:
        total[:, columns] += both(dot(main[...], rows_ref[:, columns]))

    @pl.when(step == pl.num_programs(0) - 1)
    def _():
        out[...] = total[...].astype(BF16)


def combine(main, late, returned, state):
    rows, columns = returned.shape
    return call(
        combine_kernel,
        "combine",
        jax.ShapeDtypeStruct(state.shape, BF16),
        [
            pl.BlockSpec((2 * TOKENS, ROWS), lambda i: (0, i)),
            whole(late),
            pl.BlockSpec((ROWS, columns), lambda i: (i, 0)),
            pl.BlockSpec((rows, SEG), lambda i: (0, SLOTS), pipeline_mode=pl.Buffered(1)),
            whole(state),
        ],
        pl.BlockSpec(state.shape, lambda i: (0, 0)),
        grid=(rows // ROWS,),
        scratch=[pltpu.VMEM(state.shape, F32), wide_scratch()],
        cost=pl.CostEstimate(flops=4 * 10**9, bytes_accessed=13 * 10**6, transcendentals=0),
    )(main, late, returned, returned, state)


def routes(expert_ids, route_weights, n_experts):
    tokens = expert_ids.shape[0]
    chosen = expert_ids.T[:, None, :] == jnp.arange(n_experts, dtype=jnp.int32)[None, :, None]
    named = jnp.sum(chosen.astype(F32), axis=0)
    weight = jnp.sum(jnp.where(chosen, route_weights.T[:, None, :], 0.0), axis=0)
    order = jnp.arange(tokens, dtype=jnp.int32)
    earlier = (order[:, None] < order[None, :]).astype(BF16)
    rank = dot(named.astype(BF16), earlier)
    rank = jnp.where(named > 0, rank, -1.0)
    slots = jnp.arange(SLOTS, dtype=jnp.int32).astype(F32)
    hit = rank[:, None, :] == slots[None, :, None]
    late = rank == SLOTS
    high = lax.reduce_precision(weight, 8, 7)
    low = weight - high

    def rows(value):
        spread = jnp.where(hit, value, 0.0)
        return spread.astype(BF16).reshape(n_experts * SLOTS, tokens)

    back_main = jnp.concatenate([rows(high[:, None, :]).T, rows(low[:, None, :]).T], axis=0)
    back_late = jnp.concatenate(
        [jnp.where(late, value, 0.0).astype(BF16).T for value in (high, low)], axis=0
    )
    return rows(1.0), late.astype(BF16), back_main, back_late


def local(
    queries,
    key_rows,
    value_rows,
    span_order,
    out_proj,
    residual,
    norm_gain,
    expert_ids,
    route_weights,
    w_up,
    w_down,
):
    n_devices = lax.axis_size("dp") * lax.axis_size("ctx") * lax.axis_size("tp")
    core = lax.axis_index("dp") % 2
    ctx = lax.axis_index("ctx")
    x, z = lax.axis_index("tp") // SIDE, lax.axis_index("tp") % SIDE
    meta = jnp.concatenate([span_order, jnp.stack([ctx, x, z, core]).astype(jnp.int32)])

    def head_block(step):
        start = (x + step) % SIDE * HD
        return jnp.concatenate(
            [
                lax.dynamic_slice_in_dim(key_rows, start, HD, 1),
                lax.dynamic_slice_in_dim(value_rows, start, HD, 1),
            ],
            axis=1,
        )

    width = out_proj.shape[1]
    quarter = width // 4

    def weights_part(base):
        return lax.dynamic_slice_in_dim(out_proj, base + core * quarter, quarter, 1)

    own = jnp.stack(exchange(shift_x, [head_block(step) for step in range(SIDE)]))
    own, part_x = lax.optimization_barrier((own, weights_part(0)))
    other = swap_ctx(own)
    before_own, after_own = shift_z(own, 1), shift_z(own, -1)
    before_own, after_own, part_z = lax.optimization_barrier(
        (before_own, after_own, weights_part(width // 2))
    )
    before_other, after_other = shift_z(other, 1), shift_z(other, -1)
    far_own = shift_z(before_own, 1)
    far_other = shift_z(after_other, -1)
    weights_x = jnp.concatenate(gather_rows_of(shift_x, part_x), axis=0)
    other_x = swap_core(weights_x)
    weights_z = gather_rows_of(shift_z, part_z)
    pieces = [
        own,
        other,
        before_own,
        before_other,
        after_own,
        after_other,
        far_own,
        far_other,
    ]

    maps = routes(expert_ids, route_weights, n_devices)

    parts = attention(meta, queries, pieces)
    context_x = exchange(shift_x, parts[:4])
    context_z = exchange(shift_z, parts[4:])
    context_x, context_z, weights_z = lax.optimization_barrier((context_x, context_z, weights_z))
    *terms_z, weights_z = projection(6, meta, context_x, [weights_x, other_x], weights_z)
    terms_x = projection(5, meta, context_z, [weights_z, swap_core(weights_z)])
    terms_z, terms_x = exchange(shift_z, terms_z), exchange(shift_x, terms_x)
    main, late, back_main, back_late = maps

    outgoing, state = dispatch(
        meta, terms_z, terms_x, residual, norm_gain[None, :], main, late
    )

    def all_to_all(rows):
        blocks = rows.reshape(n_devices, SLOTS, rows.shape[1])
        return lax.all_to_all(
            blocks, ("dp", "ctx", "tp"), split_axis=0, concat_axis=0, tiled=True
        ).reshape(rows.shape)

    arrived = all_to_all(outgoing)
    returned = all_to_all(experts(arrived, w_up, w_down))
    return combine(back_main, back_late, returned, state)


def solution(mesh):
    return jax.shard_map(
        local,
        mesh=mesh,
        in_specs=(
            P(("dp", "ctx"), "tp"),
            P(("dp", "ctx", "tp"), None),
            P(("dp", "ctx", "tp"), None),
            P(),
            P("tp", None),
            P(("dp", "ctx", "tp"), None),
            P(),
            P(("dp", "ctx", "tp"), None),
            P(("dp", "ctx", "tp"), None),
            P(("dp", "ctx", "tp"), None, None),
            P(("dp", "ctx", "tp"), None, None),
        ),
        out_specs=P(("dp", "ctx", "tp"), None),
        check_vma=False,
    )
```

```python
import functools
import math

import jax
import jax.numpy as jnp
from jax import lax
from jax.experimental import pallas as pl
from jax.experimental.pallas import tpu as pltpu
from jax.sharding import PartitionSpec as P

HD = 128
KVH = 4
SIDE = 4
TOKENS = 128
SLOTS = 8
SEG = 512
ROWS = 256
BLOCK = 512
NEGATIVE = -1e30
MIB = 1 << 20
F32 = jnp.float32
BF16 = jnp.bfloat16


def shift_x(value, step):
    return lax.ppermute(
        value,
        "tp",
        [(x * SIDE + z, (x + step) % SIDE * SIDE + z) for x in range(SIDE) for z in range(SIDE)],
    )


def shift_z(value, step):
    return lax.ppermute(
        value,
        "tp",
        [(x * SIDE + z, x * SIDE + (z + step) % SIDE) for x in range(SIDE) for z in range(SIDE)],
    )


def swap_ctx(value):
    return lax.ppermute(value, "ctx", [(0, 1), (1, 0)])


def swap_core(value):
    return lax.ppermute(value, "dp", [(0, 1), (1, 0), (2, 3), (3, 2)])


def gather_rows_of(shift, rows):
    return [rows, shift(rows, 1), shift(rows, 2), shift(rows, -1)]


def exchange(shift, blocks):
    return [blocks[0], shift(blocks[1], 1), shift(blocks[2], 2), shift(blocks[3], -1)]


def call(kernel, name, out_shape, in_specs, out_specs, grid=(), scratch=(), limit=56, cost=None):
    return pl.pallas_call(
        kernel,
        name=name,
        out_shape=out_shape,
        grid=grid,
        in_specs=in_specs,
        out_specs=out_specs,
        scratch_shapes=list(scratch),
        compiler_params=pltpu.CompilerParams(vmem_limit_bytes=limit * MIB),
        cost_estimate=cost,
    )


def smem():
    return pl.BlockSpec(memory_space=pltpu.SMEM)


def vmem():
    return pl.BlockSpec(memory_space=pltpu.VMEM)


def whole(array):
    zeros = (0,) * array.ndim
    return pl.BlockSpec(array.shape, lambda *_: zeros, pipeline_mode=pl.Buffered(1))


def dot(left, right):
    return jnp.dot(left, right, preferred_element_type=F32)


def dot_nt(left, right):
    return lax.dot_general(left, right, (((1,), (1,)), ((), ())), preferred_element_type=F32)


def rows_of(chunk):
    return pl.ds(pl.multiple_of(chunk * BLOCK, BLOCK), BLOCK)


def attend(meta, chunk, q_ref, keys, values, scratch):
    sums, peaks, totals, even, odd = scratch[0], scratch[1], scratch[2], scratch[3:5], scratch[5:7]
    factor = math.log2(math.e) / math.sqrt(HD)
    mine = meta[meta[4] * 2 + chunk // 2] * 2 + lax.rem(chunk, 2)
    heads = [q_ref[rows_of(chunk), head * HD : (head + 1) * HD] for head in range(2)]
    for head in range(2):
        sums[head] = jnp.zeros((HD, BLOCK), F32)
        peaks[head] = jnp.full((1, BLOCK), NEGATIVE, F32)
        totals[head] = jnp.zeros((1, BLOCK), F32)

    def score(number, held):
        key_block = keys[rows_of(number), :]
        for head in range(2):
            held[head][...] = dot_nt(key_block, heads[head])

    def process(number, held, masked):
        value_block = values[:, rows_of(number)]
        for head in range(2):
            scores = held[head][...]
            if masked:
                seen = lax.broadcasted_iota(
                    jnp.int32, (BLOCK, BLOCK), 0
                ) <= lax.broadcasted_iota(jnp.int32, (BLOCK, BLOCK), 1)
                scores = jnp.where(seen, scores, NEGATIVE)
            peak = peaks[head]
            new_peak = jnp.maximum(peak, jnp.max(scores, axis=0, keepdims=True))
            weights = jnp.exp2(scores * factor - new_peak * factor)
            fading = jnp.exp2((peak - new_peak) * factor)
            peaks[head] = new_peak
            totals[head] = totals[head] * fading + jnp.sum(weights, axis=0, keepdims=True)
            sums[head] = sums[head] * fading + dot(value_block, weights.astype(BF16))

    score(0, even)

    def two(pair, carry):
        score(2 * pair + 1, odd)
        process(2 * pair, even, False)
        score(2 * pair + 2, even)
        process(2 * pair + 1, odd, False)
        return carry

    lax.fori_loop(0, mine // 2, two, 0)

    @pl.when(lax.rem(mine, 2) == 1)
    def _():
        score(mine, odd)
        process(mine - 1, even, False)
        process(mine, odd, True)

    @pl.when(lax.rem(mine, 2) == 0)
    def _():
        process(mine, even, True)

    return jnp.concatenate(
        [(sums[head] / totals[head]).T.astype(BF16) for head in range(2)], axis=1
    )


def attend_scratch():
    return [
        pltpu.VMEM((2, HD, BLOCK), F32),
        pltpu.VMEM((2, 1, BLOCK), F32),
        pltpu.VMEM((2, 1, BLOCK), F32),
    ] + [pltpu.VMEM((BLOCK, BLOCK), F32)] * 4


def join(pieces, joined):
    rows = pieces[0].shape[0]
    for number, piece in enumerate(pieces):
        joined[number * rows : (number + 1) * rows, :] = piece[...]


def attention_kernel(meta, q_ref, *refs):
    pieces, weights, refs = refs[:8], refs[8:12], refs[12:]
    outs, keys, values, joined, context, scratch = refs[:3], *refs[3:7], refs[7:]
    ctx, x, z = meta[4], meta[5], meta[6]

    join(weights, joined)
    for number, piece in enumerate(pieces):
        part = lax.rem(ctx + number % 2, 2)
        back = (0, 1, 3, 2)[number // 2]
        z_of = lax.rem(z + SIDE - back, SIDE)
        for block in range(SIDE):
            x_of = lax.rem(x + SIDE - block, SIDE)
            place = meta[part * 2 + x_of // 2] * 8 + lax.rem(x_of, 2) * SIDE + z_of
            rows = pl.ds(pl.multiple_of(place * HD, HD), HD)
            keys[rows, :] = piece[block, :, :HD]
            values[:, rows] = piece[block, :, HD:].T

    @pl.loop(0, SIDE - 1)
    def _(number):
        chunk = lax.rem(x + 1 + number, SIDE)
        context[number] = attend(meta, chunk, q_ref, keys, values, scratch)

    for number, out in enumerate(outs):
        out[...] = context[number]


def attention(meta, queries, pieces, weights):
    rows, width = queries.shape
    arrays = (queries, *pieces, *weights)
    outs = [jax.ShapeDtypeStruct((BLOCK, width), BF16)] * 3 + [
        jax.ShapeDtypeStruct((2 * rows, HD), BF16),
        jax.ShapeDtypeStruct((HD, 2 * rows), BF16),
        jax.ShapeDtypeStruct((SIDE * weights[0].shape[0], weights[0].shape[1]), BF16),
    ]
    return call(
        attention_kernel,
        "attention",
        outs,
        [smem()] + [whole(array) for array in arrays],
        [pl.BlockSpec(out.shape, lambda: (0, 0)) for out in outs],
        scratch=[pltpu.VMEM((3, BLOCK, width), BF16), *attend_scratch()],
        cost=pl.CostEstimate(
            flops=16 * 10**9, bytes_accessed=7 * 10**6, transcendentals=10 * 10**6
        ),
    )(meta, *arrays)


def attention_end_kernel(meta, q_ref, keys, values, *refs):
    others, weights, out, refs = refs[:3], refs[3:7], refs[7], refs[8:]
    outs_z, joined, scratch = refs[:4], refs[4], refs[5:]
    x, z = meta[5], meta[6]
    join(weights, joined)
    out[...] = attend(meta, x, q_ref, keys, values, scratch)
    for number, context in enumerate((out, *others)):
        x_of = lax.rem(x + number, SIDE)
        rows = pl.ds(pl.multiple_of(x_of * TOKENS, TOKENS), TOKENS)
        for step_of in range(SIDE):
            to_z = lax.rem(z + step_of, SIDE)
            part = pl.ds(pl.multiple_of(to_z * TOKENS, TOKENS), TOKENS)
            outs_z[step_of][rows, :] = context[part, :]


def attention_end(meta, queries, keys, values, others, weights):
    width = queries.shape[1]
    arrays = (queries, keys, values, *others, *weights)
    outs = [jax.ShapeDtypeStruct((BLOCK, width), BF16)] * 5
    outs.append(jax.ShapeDtypeStruct((SIDE * weights[0].shape[0], weights[0].shape[1]), BF16))
    return call(
        attention_end_kernel,
        "attention_end",
        outs,
        [smem()] + [whole(array) for array in arrays],
        [pl.BlockSpec(out.shape, lambda: (0, 0)) for out in outs],
        scratch=attend_scratch(),
        cost=pl.CostEstimate(
            flops=6 * 10**9, bytes_accessed=7 * 10**6, transcendentals=3 * 10**6
        ),
    )(meta, *arrays)


def projection_kernel(axis, meta, *refs):
    context, weights, outs, held = refs[:4], refs[4:6], refs[6:10], refs[10]
    me = meta[axis]
    width = context[0].shape[1]
    columns = 256
    for side, weight in enumerate(weights):
        for start in range(0, weight.shape[1], columns):
            total = None
            for number, rows in enumerate(context):
                part = weight[number * width : (number + 1) * width, start : start + columns]
                term = dot(rows[...], part)
                total = term if total is None else total + term
            held[:, side * weight.shape[1] + start : side * weight.shape[1] + start + columns] = (
                total.astype(BF16)
            )
    for number, out in enumerate(outs):
        to = lax.rem(me + number, SIDE)
        out[...] = held[pl.ds(pl.multiple_of(to * TOKENS, TOKENS), TOKENS), :]


def projection(axis, meta, context, weights):
    columns = 2 * weights[0].shape[1]
    arrays = (*context, *weights)
    return call(
        functools.partial(projection_kernel, axis),
        "projection",
        [jax.ShapeDtypeStruct((TOKENS, columns), BF16)] * 4,
        [smem()] + [whole(array) for array in arrays],
        [pl.BlockSpec((TOKENS, columns), lambda: (0, 0))] * 4,
        scratch=[pltpu.VMEM((SIDE * TOKENS, columns), BF16)],
        cost=pl.CostEstimate(
            flops=2 * 512 * 1024 * columns, bytes_accessed=7 * 10**6, transcendentals=0
        ),
    )(meta, *arrays)


def wide_scratch():
    return pltpu.VMEM((SEG // HD, TOKENS * SLOTS, HD), F32)


def widen(wide, rows_ref):
    for part in range(SEG // HD):
        wide[part] = rows_ref[:, part * HD : (part + 1) * HD].astype(F32)


def narrow(wide):
    return jnp.concatenate([wide[part].astype(BF16) for part in range(SEG // HD)], axis=1)


def gather_rows(wide, segment):
    rows = pl.ds(segment, TOKENS, stride=SLOTS)
    return jnp.concatenate([wide[part, rows, :] for part in range(SEG // HD)], axis=1).astype(BF16)


def scatter_rows(wide, segment, value):
    rows = pl.ds(segment, TOKENS, stride=SLOTS)
    for part in range(SEG // HD):
        wide[part, rows, :] = value[:, part * HD : (part + 1) * HD]


def dispatch_kernel(meta, *refs):
    terms_z, terms_x, refs = refs[:4], refs[4:8], refs[8:]
    residual, gain, main, late, outgoing, state, normed, wide, spread = refs
    step = pl.program_id(0)
    half = terms_z[0].shape[1]
    quarter = half // 2
    core = meta[7]

    @pl.when(step == 0)
    def _():
        for base, terms in ((0, terms_z), (half, terms_x)):
            for side in range(2):
                place = base + quarter * lax.rem(core + side, 2)
                columns = pl.ds(pl.multiple_of(place, quarter), quarter)
                part = slice(side * quarter, (side + 1) * quarter)
                total = terms[0][:, part].astype(F32)
                for term in terms[1:]:
                    total = total + term[:, part].astype(F32)
                state[:, columns] = residual[:, columns].astype(F32) + total
        value = state[...]
        scale = lax.rsqrt(jnp.mean(value * value, axis=1, keepdims=True) + 1e-06)
        for segment in range(SLOTS):
            columns = slice(segment * SEG, (segment + 1) * SEG)
            normed[segment] = (state[:, columns] * scale * gain[:, columns]).astype(BF16)

        for segment in range(SLOTS):
            scatter_rows(wide, segment, dot(late[...], normed[segment]))
        spread[...] = narrow(wide)

    for segment in range(SLOTS):
        columns = slice(segment * SEG, (segment + 1) * SEG)
        outgoing[:, columns] = dot(main[...], normed[segment]).astype(BF16)
    rows = outgoing.shape[0]
    outgoing[:, 2 * half :] = spread[pl.ds(pl.multiple_of(step * rows, rows), rows), :]


def dispatch(meta, terms_z, terms_x, residual, gain, main, late):
    rows, width = main.shape[0], residual.shape[1]
    arrays = (*terms_z, *terms_x, residual, gain)
    return call(
        dispatch_kernel,
        "dispatch",
        [
            jax.ShapeDtypeStruct((rows, width + SEG), BF16),
            jax.ShapeDtypeStruct((TOKENS, width), F32),
        ],
        [smem()]
        + [whole(a) for a in arrays]
        + [pl.BlockSpec((ROWS, TOKENS), lambda i: (i, 0)), whole(late)],
        [
            pl.BlockSpec((ROWS, width + SEG), lambda i: (i, 0)),
            pl.BlockSpec((TOKENS, width), lambda i: (0, 0)),
        ],
        grid=(rows // ROWS,),
        scratch=[
            pltpu.VMEM((SLOTS, TOKENS, SEG), BF16),
            wide_scratch(),
            pltpu.VMEM((rows, SEG), BF16),
        ],
        cost=pl.CostEstimate(flops=3 * 10**9, bytes_accessed=16 * 10**6, transcendentals=0),
    )(meta, *arrays, main, late)


def expert_kernel(rows_ref, over_ref, up_ref, down_hbm, out_ref, wide, spread, down_ref, done):
    step = pl.program_id(0)
    width = down_ref.shape[2]
    fetch = pltpu.make_async_copy(down_hbm, down_ref, done)

    def act(value):
        return (value / (1.0 + jnp.exp(-value))).astype(BF16)

    @pl.when(step == 0)
    def _():
        fetch.start()
        widen(wide, over_ref)
        total = None
        for segment in range(SLOTS):
            part = up_ref[0, segment * SEG : (segment + 1) * SEG, :]
            term = dot(gather_rows(wide, segment), part)
            total = term if total is None else total + term
        inner = act(total)
        fetch.wait()
        for segment in range(SLOTS):
            part = down_ref[0, :, segment * SEG : (segment + 1) * SEG]
            scatter_rows(wide, segment, dot(inner, part))
        spread[...] = narrow(wide)

    inner = act(dot(rows_ref[:, :width], up_ref[0]))
    for segment in range(SLOTS):
        columns = slice(segment * SEG, (segment + 1) * SEG)
        out_ref[:, columns] = dot(inner, down_ref[0, :, columns]).astype(BF16)
    mine = pl.ds(pl.multiple_of(step * ROWS, ROWS), ROWS)
    out_ref[:, width:] = spread[mine, :]


def experts(arrived, up, down):
    rows, columns = arrived.shape
    inner = up.shape[2]
    return call(
        expert_kernel,
        "experts",
        jax.ShapeDtypeStruct((rows, columns), BF16),
        [
            pl.BlockSpec((ROWS, columns), lambda i: (i, 0)),
            pl.BlockSpec((rows, SEG), lambda i: (0, SLOTS)),
            vmem(),
            pl.BlockSpec(memory_space=pl.ANY),
        ],
        pl.BlockSpec((ROWS, columns), lambda i: (i, 0)),
        grid=(rows // ROWS,),
        scratch=[
            wide_scratch(),
            pltpu.VMEM((rows, SEG), BF16),
            pltpu.VMEM(down.shape, BF16),
            pltpu.SemaphoreType.DMA,
        ],
        limit=46,
        cost=pl.CostEstimate(
            flops=4 * rows * columns * inner,
            bytes_accessed=32 * 10**6,
            transcendentals=rows * inner,
        ),
    )(arrived, arrived, up, down)


def combine_kernel(main, late, rows_ref, over_ref, state, out, total, wide):
    step = pl.program_id(0)
    segments = [(i, slice(i * SEG, (i + 1) * SEG)) for i in range(SLOTS)]

    def both(value):
        return value[:TOKENS] + value[TOKENS:]

    @pl.when(step == 0)
    def _():
        widen(wide, over_ref)
        for segment, columns in segments:
            late_part = both(dot(late[...], gather_rows(wide, segment)))
            total[:, columns] = state[:, columns] + late_part

    for segment, columns in segments:
        total[:, columns] += both(dot(main[...], rows_ref[:, columns]))

    @pl.when(step == pl.num_programs(0) - 1)
    def _():
        out[...] = total[...].astype(BF16)


def combine(main, late, returned, state):
    rows, columns = returned.shape
    return call(
        combine_kernel,
        "combine",
        jax.ShapeDtypeStruct(state.shape, BF16),
        [
            pl.BlockSpec((2 * TOKENS, ROWS), lambda i: (0, i)),
            whole(late),
            pl.BlockSpec((ROWS, columns), lambda i: (i, 0)),
            pl.BlockSpec((rows, SEG), lambda i: (0, SLOTS), pipeline_mode=pl.Buffered(1)),
            whole(state),
        ],
        pl.BlockSpec(state.shape, lambda i: (0, 0)),
        grid=(rows // ROWS,),
        scratch=[pltpu.VMEM(state.shape, F32), wide_scratch()],
        cost=pl.CostEstimate(flops=4 * 10**9, bytes_accessed=13 * 10**6, transcendentals=0),
    )(main, late, returned, returned, state)


def routes(expert_ids, route_weights, n_experts):
    tokens = expert_ids.shape[0]
    chosen = expert_ids.T[:, None, :] == jnp.arange(n_experts, dtype=jnp.int32)[None, :, None]
    named = jnp.sum(chosen.astype(F32), axis=0)
    weight = jnp.sum(jnp.where(chosen, route_weights.T[:, None, :], 0.0), axis=0)
    order = jnp.arange(tokens, dtype=jnp.int32)
    earlier = (order[:, None] < order[None, :]).astype(BF16)
    rank = dot(named.astype(BF16), earlier)
    rank = jnp.where(named > 0, rank, -1.0)
    slots = jnp.arange(SLOTS, dtype=jnp.int32).astype(F32)
    hit = rank[:, None, :] == slots[None, :, None]
    late = rank == SLOTS
    high = lax.reduce_precision(weight, 8, 7)
    low = weight - high

    def rows(value):
        spread = jnp.where(hit, value, 0.0)
        return spread.astype(BF16).reshape(n_experts * SLOTS, tokens)

    back_main = jnp.concatenate([rows(high[:, None, :]).T, rows(low[:, None, :]).T], axis=0)
    back_late = jnp.concatenate(
        [jnp.where(late, value, 0.0).astype(BF16).T for value in (high, low)], axis=0
    )
    return rows(1.0), late.astype(BF16), back_main, back_late


def local(
    queries,
    key_rows,
    value_rows,
    span_order,
    out_proj,
    residual,
    norm_gain,
    expert_ids,
    route_weights,
    w_up,
    w_down,
):
    n_devices = lax.axis_size("dp") * lax.axis_size("ctx") * lax.axis_size("tp")
    core = lax.axis_index("dp") % 2
    ctx = lax.axis_index("ctx")
    x, z = lax.axis_index("tp") // SIDE, lax.axis_index("tp") % SIDE
    meta = jnp.concatenate([span_order, jnp.stack([ctx, x, z, core]).astype(jnp.int32)])

    def head_block(step):
        start = (x + step) % SIDE * HD
        return jnp.concatenate(
            [
                lax.dynamic_slice_in_dim(key_rows, start, HD, 1),
                lax.dynamic_slice_in_dim(value_rows, start, HD, 1),
            ],
            axis=1,
        )

    width = out_proj.shape[1]
    quarter = width // 4

    def weights_part(base):
        return lax.dynamic_slice_in_dim(out_proj, base + core * quarter, quarter, 1)

    def after(value, *others):
        return lax.optimization_barrier((value, *others))[0]

    own = jnp.stack(exchange(shift_x, [head_block(step) for step in range(SIDE)]))
    other = swap_ctx(own)
    before_own, after_own = shift_z(own, 1), shift_z(own, -1)
    before_other, after_other = shift_z(other, 1), shift_z(other, -1)
    far_own = shift_z(before_own, 1)
    far_other = shift_z(after_other, -1)
    weights_x = gather_rows_of(shift_x, after(weights_part(0), own))
    weights_z = gather_rows_of(shift_z, after(weights_part(width // 2), far_own, far_other))
    pieces = [
        own,
        other,
        before_own,
        before_other,
        after_own,
        after_other,
        far_own,
        far_other,
    ]

    maps = routes(expert_ids, route_weights, n_devices)

    *far, keys, values, weights_x = attention(meta, queries, pieces, weights_x)
    other_x = swap_core(weights_x)
    mine, *parts, weights_z = attention_end(meta, queries, keys, values, far, weights_z)
    other_z = swap_core(weights_z)
    context_x = exchange(shift_x, [mine, *far])
    context_z = exchange(shift_z, parts)
    terms_z = projection(6, meta, context_x, [weights_x, other_x])
    terms_x = projection(5, meta, context_z, [weights_z, other_z])
    terms_z, terms_x = exchange(shift_z, terms_z), exchange(shift_x, terms_x)
    main, late, back_main, back_late = maps

    outgoing, state = dispatch(
        meta, terms_z, terms_x, residual, norm_gain[None, :], main, late
    )

    def all_to_all(rows):
        blocks = rows.reshape(n_devices, SLOTS, rows.shape[1])
        return lax.all_to_all(
            blocks, ("dp", "ctx", "tp"), split_axis=0, concat_axis=0, tiled=True
        ).reshape(rows.shape)

    arrived = all_to_all(outgoing)
    returned = all_to_all(experts(arrived, w_up, w_down))
    return combine(back_main, back_late, returned, state)


def solution(mesh):
    return jax.shard_map(
        local,
        mesh=mesh,
        in_specs=(
            P(("dp", "ctx"), "tp"),
            P(("dp", "ctx", "tp"), None),
            P(("dp", "ctx", "tp"), None),
            P(),
            P("tp", None),
            P(("dp", "ctx", "tp"), None),
            P(),
            P(("dp", "ctx", "tp"), None),
            P(("dp", "ctx", "tp"), None),
            P(("dp", "ctx", "tp"), None, None),
            P(("dp", "ctx", "tp"), None, None),
        ),
        out_specs=P(("dp", "ctx", "tp"), None),
        check_vma=False,
    )
```

```python
import functools
import math

import jax
import jax.numpy as jnp
from jax import lax
from jax.experimental import pallas as pl
from jax.experimental.pallas import tpu as pltpu
from jax.sharding import PartitionSpec as P

HD = 128
KVH = 4
SIDE = 4
TOKENS = 128
SLOTS = 8
SEG = 512
ROWS = 256
DISPATCH_COLUMNS = 512
DOWN_COLUMNS = 512
COMBINE_COLUMNS = 512
BLOCK = 512
NEGATIVE = -1e30
MIB = 1 << 20
F32 = jnp.float32
BF16 = jnp.bfloat16


def shift_x(value, step):
    return lax.ppermute(
        value,
        "tp",
        [(x * SIDE + z, (x + step) % SIDE * SIDE + z) for x in range(SIDE) for z in range(SIDE)],
    )


def shift_z(value, step):
    return lax.ppermute(
        value,
        "tp",
        [(x * SIDE + z, x * SIDE + (z + step) % SIDE) for x in range(SIDE) for z in range(SIDE)],
    )


def swap_ctx(value):
    return lax.ppermute(value, "ctx", [(0, 1), (1, 0)])


def swap_core(value):
    return lax.ppermute(value, "dp", [(0, 1), (1, 0), (2, 3), (3, 2)])


def gather_rows_of(shift, rows):
    return [rows, shift(rows, 1), shift(rows, 2), shift(rows, -1)]


def exchange(shift, blocks):
    return [blocks[0], shift(blocks[1], 1), shift(blocks[2], 2), shift(blocks[3], -1)]


def call(kernel, name, out_shape, in_specs, out_specs, grid=(), scratch=(), limit=56, cost=None):
    return pl.pallas_call(
        kernel,
        name=name,
        out_shape=out_shape,
        grid=grid,
        in_specs=in_specs,
        out_specs=out_specs,
        scratch_shapes=list(scratch),
        compiler_params=pltpu.CompilerParams(vmem_limit_bytes=limit * MIB),
        cost_estimate=cost,
    )


def smem():
    return pl.BlockSpec(memory_space=pltpu.SMEM)


def vmem():
    return pl.BlockSpec(memory_space=pltpu.VMEM)


def whole(array):
    zeros = (0,) * array.ndim
    return pl.BlockSpec(array.shape, lambda *_: zeros, pipeline_mode=pl.Buffered(1))


def dot(left, right):
    return jnp.dot(left, right, preferred_element_type=F32)


def dot_nt(left, right):
    return lax.dot_general(left, right, (((1,), (1,)), ((), ())), preferred_element_type=F32)


def rows_of(chunk):
    return pl.ds(pl.multiple_of(chunk * BLOCK, BLOCK), BLOCK)


def attend(meta, chunk, q_ref, keys, values, scratch):
    sums, peaks, totals, even, odd = scratch[0], scratch[1], scratch[2], scratch[3:5], scratch[5:7]
    factor = math.log2(math.e) / math.sqrt(HD)
    mine = meta[meta[4] * 2 + chunk // 2] * 2 + lax.rem(chunk, 2)
    heads = [q_ref[rows_of(chunk), head * HD : (head + 1) * HD] for head in range(2)]
    for head in range(2):
        sums[head] = jnp.zeros((HD, BLOCK), F32)
        peaks[head] = jnp.full((1, BLOCK), NEGATIVE, F32)
        totals[head] = jnp.zeros((1, BLOCK), F32)

    def score(number, held):
        key_block = keys[rows_of(number), :]
        for head in range(2):
            held[head][...] = dot_nt(key_block, heads[head])

    def process(number, held, masked):
        value_block = values[:, rows_of(number)]
        for head in range(2):
            scores = held[head][...]
            if masked:
                seen = lax.broadcasted_iota(
                    jnp.int32, (BLOCK, BLOCK), 0
                ) <= lax.broadcasted_iota(jnp.int32, (BLOCK, BLOCK), 1)
                scores = jnp.where(seen, scores, NEGATIVE)
            peak = peaks[head]
            new_peak = jnp.maximum(peak, jnp.max(scores, axis=0, keepdims=True))
            weights = jnp.exp2(scores * factor - new_peak * factor)
            fading = jnp.exp2((peak - new_peak) * factor)
            peaks[head] = new_peak
            totals[head] = totals[head] * fading + jnp.sum(weights, axis=0, keepdims=True)
            sums[head] = sums[head] * fading + dot(value_block, weights.astype(BF16))

    score(0, even)

    def two(pair, carry):
        score(2 * pair + 1, odd)
        process(2 * pair, even, False)
        score(2 * pair + 2, even)
        process(2 * pair + 1, odd, False)
        return carry

    lax.fori_loop(0, mine // 2, two, 0)

    @pl.when(lax.rem(mine, 2) == 1)
    def _():
        score(mine, odd)
        process(mine - 1, even, False)
        process(mine, odd, True)

    @pl.when(lax.rem(mine, 2) == 0)
    def _():
        process(mine, even, True)

    return jnp.concatenate(
        [(sums[head] / totals[head]).T.astype(BF16) for head in range(2)], axis=1
    )


def attend_scratch():
    return [
        pltpu.VMEM((2, HD, BLOCK), F32),
        pltpu.VMEM((2, 1, BLOCK), F32),
        pltpu.VMEM((2, 1, BLOCK), F32),
    ] + [pltpu.VMEM((BLOCK, BLOCK), F32)] * 4


def join(pieces, joined):
    rows = pieces[0].shape[0]
    for number, piece in enumerate(pieces):
        joined[number * rows : (number + 1) * rows, :] = piece[...]


def attention_kernel(meta, q_ref, *refs):
    pieces, weights, refs = refs[:8], refs[8:12], refs[12:]
    outs, keys, values, joined, context, scratch = refs[:3], *refs[3:7], refs[7:]
    ctx, x, z = meta[4], meta[5], meta[6]

    join(weights, joined)
    for number, piece in enumerate(pieces):
        part = lax.rem(ctx + number % 2, 2)
        back = (0, 1, 3, 2)[number // 2]
        z_of = lax.rem(z + SIDE - back, SIDE)
        for block in range(SIDE):
            x_of = lax.rem(x + SIDE - block, SIDE)
            place = meta[part * 2 + x_of // 2] * 8 + lax.rem(x_of, 2) * SIDE + z_of
            rows = pl.ds(pl.multiple_of(place * HD, HD), HD)
            keys[rows, :] = piece[block, :, :HD]
            values[:, rows] = piece[block, :, HD:].T

    @pl.loop(0, SIDE - 1)
    def _(number):
        chunk = lax.rem(x + 1 + number, SIDE)
        context[number] = attend(meta, chunk, q_ref, keys, values, scratch)

    for number, out in enumerate(outs):
        out[...] = context[number]


def attention(meta, queries, pieces, weights):
    rows, width = queries.shape
    arrays = (queries, *pieces, *weights)
    outs = [jax.ShapeDtypeStruct((BLOCK, width), BF16)] * 3 + [
        jax.ShapeDtypeStruct((2 * rows, HD), BF16),
        jax.ShapeDtypeStruct((HD, 2 * rows), BF16),
        jax.ShapeDtypeStruct((SIDE * weights[0].shape[0], weights[0].shape[1]), BF16),
    ]
    return call(
        attention_kernel,
        "attention",
        outs,
        [smem()] + [whole(array) for array in arrays],
        [pl.BlockSpec(out.shape, lambda: (0, 0)) for out in outs],
        scratch=[pltpu.VMEM((3, BLOCK, width), BF16), *attend_scratch()],
        cost=pl.CostEstimate(
            flops=16 * 10**9, bytes_accessed=7 * 10**6, transcendentals=10 * 10**6
        ),
    )(meta, *arrays)


def attention_end_kernel(meta, q_ref, keys, values, *refs):
    others, weights, out, refs = refs[:3], refs[3:7], refs[7], refs[8:]
    outs_z, joined, scratch = refs[:4], refs[4], refs[5:]
    x, z = meta[5], meta[6]
    join(weights, joined)
    out[...] = attend(meta, x, q_ref, keys, values, scratch)
    for number, context in enumerate((out, *others)):
        x_of = lax.rem(x + number, SIDE)
        rows = pl.ds(pl.multiple_of(x_of * TOKENS, TOKENS), TOKENS)
        for step_of in range(SIDE):
            to_z = lax.rem(z + step_of, SIDE)
            part = pl.ds(pl.multiple_of(to_z * TOKENS, TOKENS), TOKENS)
            outs_z[step_of][rows, :] = context[part, :]


def attention_end(meta, queries, keys, values, others, weights):
    width = queries.shape[1]
    arrays = (queries, keys, values, *others, *weights)
    outs = [jax.ShapeDtypeStruct((BLOCK, width), BF16)] * 5
    outs.append(jax.ShapeDtypeStruct((SIDE * weights[0].shape[0], weights[0].shape[1]), BF16))
    return call(
        attention_end_kernel,
        "attention_end",
        outs,
        [smem()] + [whole(array) for array in arrays],
        [pl.BlockSpec(out.shape, lambda: (0, 0)) for out in outs],
        scratch=attend_scratch(),
        cost=pl.CostEstimate(
            flops=6 * 10**9, bytes_accessed=7 * 10**6, transcendentals=3 * 10**6
        ),
    )(meta, *arrays)


def projection_kernel(axis, meta, *refs):
    context, weights, outs, held = refs[:4], refs[4:6], refs[6:10], refs[10]
    step, me = pl.program_id(0), meta[axis]
    width = context[0].shape[1]
    columns = weights[0].shape[1]
    steps = held.shape[1] // (2 * columns)
    for side, weight in enumerate(weights):
        total = None
        for number, rows in enumerate(context):
            term = dot(rows[...], weight[number * width : (number + 1) * width, :])
            total = term if total is None else total + term
        start = pl.multiple_of((side * steps + step) * columns, columns)
        held[:, pl.ds(start, columns)] = total.astype(BF16)

    @pl.when(step == steps - 1)
    def _():
        for number, out in enumerate(outs):
            to = lax.rem(me + number, SIDE)
            out[...] = held[pl.ds(pl.multiple_of(to * TOKENS, TOKENS), TOKENS), :]


def projection(axis, meta, context, weights):
    depth, columns = weights[0].shape
    part = columns // 4
    return call(
        functools.partial(projection_kernel, axis),
        "projection",
        [jax.ShapeDtypeStruct((TOKENS, 2 * columns), BF16)] * 4,
        [smem()]
        + [whole(array) for array in context]
        + [pl.BlockSpec((depth, part), lambda i: (0, i))] * 2,
        [pl.BlockSpec((TOKENS, 2 * columns), lambda i: (0, 0))] * 4,
        grid=(4,),
        scratch=[pltpu.VMEM((SIDE * TOKENS, 2 * columns), BF16)],
        cost=pl.CostEstimate(
            flops=4 * 512 * 1024 * columns, bytes_accessed=7 * 10**6, transcendentals=0
        ),
    )(meta, *context, *weights)


def wide_scratch():
    return pltpu.VMEM((SEG // HD, TOKENS * SLOTS, HD), F32)


def widen(wide, rows_ref):
    for part in range(SEG // HD):
        wide[part] = rows_ref[:, part * HD : (part + 1) * HD].astype(F32)


def narrow(wide):
    return jnp.concatenate([wide[part].astype(BF16) for part in range(SEG // HD)], axis=1)


def gather_rows(wide, segment):
    rows = pl.ds(segment, TOKENS, stride=SLOTS)
    return jnp.concatenate([wide[part, rows, :] for part in range(SEG // HD)], axis=1).astype(BF16)


def scatter_rows(wide, segment, value):
    rows = pl.ds(segment, TOKENS, stride=SLOTS)
    for part in range(SEG // HD):
        wide[part, rows, :] = value[:, part * HD : (part + 1) * HD]


def dispatch_kernel(meta, *refs):
    terms_z, terms_x, refs = refs[:4], refs[4:8], refs[8:]
    residual, gain, main, late, outgoing, state, normed, wide, spread = refs
    step = pl.program_id(0)
    half = terms_z[0].shape[1]
    quarter = half // 2
    core = meta[7]

    @pl.when(step == 0)
    def _():
        for base, terms in ((0, terms_z), (half, terms_x)):
            for side in range(2):
                place = base + quarter * lax.rem(core + side, 2)
                columns = pl.ds(pl.multiple_of(place, quarter), quarter)
                part = slice(side * quarter, (side + 1) * quarter)
                total = terms[0][:, part].astype(F32)
                for term in terms[1:]:
                    total = total + term[:, part].astype(F32)
                state[:, columns] = residual[:, columns].astype(F32) + total
        value = state[...]
        scale = lax.rsqrt(jnp.mean(value * value, axis=1, keepdims=True) + 1e-06)
        for segment in range(SLOTS):
            columns = slice(segment * SEG, (segment + 1) * SEG)
            normed[:, columns] = (state[:, columns] * scale * gain[:, columns]).astype(BF16)

        for segment in range(SLOTS):
            columns = slice(segment * SEG, (segment + 1) * SEG)
            scatter_rows(wide, segment, dot(late[...], normed[:, columns]))
        spread[...] = narrow(wide)

    for start in range(0, 2 * half, DISPATCH_COLUMNS):
        columns = slice(start, start + DISPATCH_COLUMNS)
        outgoing[:, columns] = dot(main[...], normed[:, columns]).astype(BF16)
    rows = outgoing.shape[0]
    outgoing[:, 2 * half :] = spread[pl.ds(pl.multiple_of(step * rows, rows), rows), :]


def dispatch(meta, terms_z, terms_x, residual, gain, main, late):
    rows, width = main.shape[0], residual.shape[1]
    arrays = (*terms_z, *terms_x, residual, gain)
    return call(
        dispatch_kernel,
        "dispatch",
        [
            jax.ShapeDtypeStruct((rows, width + SEG), BF16),
            jax.ShapeDtypeStruct((TOKENS, width), F32),
        ],
        [smem()]
        + [whole(a) for a in arrays]
        + [pl.BlockSpec((ROWS, TOKENS), lambda i: (i, 0)), whole(late)],
        [
            pl.BlockSpec((ROWS, width + SEG), lambda i: (i, 0)),
            pl.BlockSpec((TOKENS, width), lambda i: (0, 0)),
        ],
        grid=(rows // ROWS,),
        scratch=[
            pltpu.VMEM((TOKENS, width), BF16),
            wide_scratch(),
            pltpu.VMEM((rows, SEG), BF16),
        ],
        cost=pl.CostEstimate(flops=3 * 10**9, bytes_accessed=16 * 10**6, transcendentals=0),
    )(meta, *arrays, main, late)


def expert_kernel(rows_ref, over_ref, up_ref, down_hbm, out_ref, wide, spread, down_ref, done):
    step = pl.program_id(0)
    width = down_ref.shape[2]
    fetch = pltpu.make_async_copy(down_hbm, down_ref, done)

    def act(value):
        return (value / (1.0 + jnp.exp(-value))).astype(BF16)

    @pl.when(step == 0)
    def _():
        fetch.start()
        widen(wide, over_ref)
        total = None
        for segment in range(SLOTS):
            part = up_ref[0, segment * SEG : (segment + 1) * SEG, :]
            term = dot(gather_rows(wide, segment), part)
            total = term if total is None else total + term
        inner = act(total)
        fetch.wait()
        for segment in range(SLOTS):
            part = down_ref[0, :, segment * SEG : (segment + 1) * SEG]
            scatter_rows(wide, segment, dot(inner, part))
        spread[...] = narrow(wide)

    inner = act(dot(rows_ref[:, :width], up_ref[0]))
    for start in range(0, width, DOWN_COLUMNS):
        columns = slice(start, start + DOWN_COLUMNS)
        out_ref[:, columns] = dot(inner, down_ref[0, :, columns]).astype(BF16)
    mine = pl.ds(pl.multiple_of(step * ROWS, ROWS), ROWS)
    out_ref[:, width:] = spread[mine, :]


def experts(arrived, up, down):
    rows, columns = arrived.shape
    inner = up.shape[2]
    return call(
        expert_kernel,
        "experts",
        jax.ShapeDtypeStruct((rows, columns), BF16),
        [
            pl.BlockSpec((ROWS, columns), lambda i: (i, 0)),
            pl.BlockSpec((rows, SEG), lambda i: (0, SLOTS)),
            vmem(),
            pl.BlockSpec(memory_space=pl.ANY),
        ],
        pl.BlockSpec((ROWS, columns), lambda i: (i, 0)),
        grid=(rows // ROWS,),
        scratch=[
            wide_scratch(),
            pltpu.VMEM((rows, SEG), BF16),
            pltpu.VMEM(down.shape, BF16),
            pltpu.SemaphoreType.DMA,
        ],
        limit=46,
        cost=pl.CostEstimate(
            flops=4 * rows * columns * inner,
            bytes_accessed=32 * 10**6,
            transcendentals=rows * inner,
        ),
    )(arrived, arrived, up, down)


def combine_kernel(main, late, rows_ref, over_ref, state, out, total, wide):
    step = pl.program_id(0)
    segments = [(i, slice(i * SEG, (i + 1) * SEG)) for i in range(SLOTS)]

    def both(value):
        return value[:TOKENS] + value[TOKENS:]

    @pl.when(step == 0)
    def _():
        widen(wide, over_ref)
        for segment, columns in segments:
            late_part = both(dot(late[...], gather_rows(wide, segment)))
            total[:, columns] = state[:, columns] + late_part

    for start in range(0, total.shape[1], COMBINE_COLUMNS):
        columns = slice(start, start + COMBINE_COLUMNS)
        total[:, columns] += both(dot(main[...], rows_ref[:, columns]))

    @pl.when(step == pl.num_programs(0) - 1)
    def _():
        out[...] = total[...].astype(BF16)


def combine(main, late, returned, state):
    rows, columns = returned.shape
    return call(
        combine_kernel,
        "combine",
        jax.ShapeDtypeStruct(state.shape, BF16),
        [
            pl.BlockSpec((2 * TOKENS, ROWS), lambda i: (0, i)),
            whole(late),
            pl.BlockSpec((ROWS, columns), lambda i: (i, 0)),
            pl.BlockSpec((rows, SEG), lambda i: (0, SLOTS), pipeline_mode=pl.Buffered(1)),
            whole(state),
        ],
        pl.BlockSpec(state.shape, lambda i: (0, 0)),
        grid=(rows // ROWS,),
        scratch=[pltpu.VMEM(state.shape, F32), wide_scratch()],
        cost=pl.CostEstimate(flops=4 * 10**9, bytes_accessed=13 * 10**6, transcendentals=0),
    )(main, late, returned, returned, state)


def routes_kernel(ids, weights, main, late, back_main, back_late):
    square = (TOKENS, TOKENS)
    row = lax.broadcasted_iota(jnp.int32, square, 0)
    column = lax.broadcasted_iota(jnp.int32, square, 1)
    named, weight = jnp.zeros(square, F32), jnp.zeros(square, F32)
    for choice in range(ids.shape[1]):
        chosen = column == ids[:, choice : choice + 1]
        named = named + jnp.where(chosen, 1.0, 0.0)
        weight = weight + jnp.where(chosen, weights[:, choice : choice + 1], 0.0)
    earlier = jnp.where(column < row, 1.0, 0.0).astype(BF16)
    rank = jnp.where(named > 0.0, dot(earlier, named.astype(BF16)), -1.0)
    high = weight.astype(BF16)
    low = (weight - high.astype(F32)).astype(BF16)

    tall = main.shape
    row = lax.broadcasted_iota(jnp.int32, tall, 0)
    column = lax.broadcasted_iota(jnp.int32, tall, 1)
    spread = jnp.where(row // SLOTS == column, 1.0, 0.0).astype(BF16)
    ranks = dot(spread, rank.T.astype(BF16))
    main[...] = jnp.where(ranks == (row % SLOTS).astype(F32), 1.0, 0.0).astype(BF16)
    late[...] = jnp.where(rank.T == SLOTS, 1.0, 0.0).astype(BF16)

    flat = (TOKENS, tall[0])
    hit = dot_nt(rank.astype(BF16), spread) == (
        lax.broadcasted_iota(jnp.int32, flat, 1) % SLOTS
    ).astype(F32)
    for half, part in enumerate((high, low)):
        rows = slice(half * TOKENS, (half + 1) * TOKENS)
        back_main[rows, :] = jnp.where(hit, dot_nt(part, spread), 0.0).astype(BF16)
        back_late[rows, :] = jnp.where(rank == SLOTS, part.astype(F32), 0.0).astype(BF16)


def routes(expert_ids, route_weights, n_experts):
    outs = [
        jax.ShapeDtypeStruct(shape, BF16)
        for shape in (
            (n_experts * SLOTS, TOKENS),
            (n_experts, TOKENS),
            (2 * TOKENS, n_experts * SLOTS),
            (2 * TOKENS, n_experts),
        )
    ]
    return call(
        routes_kernel,
        "routes",
        outs,
        [whole(expert_ids), whole(route_weights)],
        [pl.BlockSpec(out.shape, lambda: (0, 0)) for out in outs],
        cost=pl.CostEstimate(flops=2 * 10**8, bytes_accessed=10**6, transcendentals=0),
    )(expert_ids, route_weights)


def local(
    queries,
    key_rows,
    value_rows,
    span_order,
    out_proj,
    residual,
    norm_gain,
    expert_ids,
    route_weights,
    w_up,
    w_down,
):
    n_devices = lax.axis_size("dp") * lax.axis_size("ctx") * lax.axis_size("tp")
    core = lax.axis_index("dp") % 2
    ctx = lax.axis_index("ctx")
    x, z = lax.axis_index("tp") // SIDE, lax.axis_index("tp") % SIDE
    meta = jnp.concatenate([span_order, jnp.stack([ctx, x, z, core]).astype(jnp.int32)])

    def head_block(step):
        start = (x + step) % SIDE * HD
        return jnp.concatenate(
            [
                lax.dynamic_slice_in_dim(key_rows, start, HD, 1),
                lax.dynamic_slice_in_dim(value_rows, start, HD, 1),
            ],
            axis=1,
        )

    width = out_proj.shape[1]
    quarter = width // 4

    def weights_part(base):
        return lax.dynamic_slice_in_dim(out_proj, base + core * quarter, quarter, 1)

    def after(value, *others):
        return lax.optimization_barrier((value, *others))[0]

    own = jnp.stack(exchange(shift_x, [head_block(step) for step in range(SIDE)]))
    other = swap_ctx(own)
    before_own, after_own = shift_z(own, 1), shift_z(own, -1)
    before_other, after_other = shift_z(other, 1), shift_z(other, -1)
    far_own = shift_z(before_own, 1)
    far_other = shift_z(after_other, -1)
    weights_x = gather_rows_of(shift_x, after(weights_part(0), own))
    weights_z = gather_rows_of(shift_z, after(weights_part(width // 2), far_own, far_other))
    pieces = [
        own,
        other,
        before_own,
        before_other,
        after_own,
        after_other,
        far_own,
        far_other,
    ]

    main, late, back_main, back_late = routes(expert_ids, route_weights, n_devices)
    queries = after(queries, main)

    *far, keys, values, weights_x = attention(meta, queries, pieces, weights_x)
    other_x = swap_core(after(weights_x, *weights_z))
    mine, *parts, weights_z = attention_end(meta, queries, keys, values, far, weights_z)
    mine, *parts, other_x = lax.optimization_barrier((mine, *far, *parts, other_x))
    context_x = exchange(shift_x, [mine, *parts[:3]])
    context_z = exchange(shift_z, parts[3:])
    context_x, context_z = lax.optimization_barrier((context_x, context_z))
    other_z = swap_core(after(weights_z, *context_x))
    terms_z = projection(6, meta, context_x, [weights_x, other_x])
    terms_x = projection(5, meta, context_z, [weights_z, other_z])
    terms_z, terms_x = exchange(shift_z, terms_z), exchange(shift_x, terms_x)
    outgoing, state = dispatch(
        meta, terms_z, terms_x, residual, norm_gain[None, :], main, late
    )

    def all_to_all(rows):
        blocks = rows.reshape(n_devices, SLOTS, rows.shape[1])
        return lax.all_to_all(
            blocks, ("dp", "ctx", "tp"), split_axis=0, concat_axis=0, tiled=True
        ).reshape(rows.shape)

    arrived = all_to_all(outgoing)
    returned = all_to_all(experts(arrived, w_up, w_down))
    return combine(back_main, back_late, returned, state)


def solution(mesh):
    return jax.shard_map(
        local,
        mesh=mesh,
        in_specs=(
            P(("dp", "ctx"), "tp"),
            P(("dp", "ctx", "tp"), None),
            P(("dp", "ctx", "tp"), None),
            P(),
            P("tp", None),
            P(("dp", "ctx", "tp"), None),
            P(),
            P(("dp", "ctx", "tp"), None),
            P(("dp", "ctx", "tp"), None),
            P(("dp", "ctx", "tp"), None, None),
            P(("dp", "ctx", "tp"), None, None),
        ),
        out_specs=P(("dp", "ctx", "tp"), None),
        check_vma=False,
    )
```

```python
import functools
import math

import jax
import jax.numpy as jnp
from jax import lax
from jax.experimental import pallas as pl
from jax.experimental.pallas import tpu as pltpu
from jax.sharding import PartitionSpec as P

HD = 128
KVH = 4
SIDE = 4
TOKENS = 128
SLOTS = 8
SEG = 512
ROWS = 256
DISPATCH_COLUMNS = 512
DOWN_COLUMNS = 512
COMBINE_COLUMNS = 512
BLOCK = 512
NEGATIVE = -1e30
MIB = 1 << 20
F32 = jnp.float32
BF16 = jnp.bfloat16


def shift_x(value, step):
    return lax.ppermute(
        value,
        "tp",
        [(x * SIDE + z, (x + step) % SIDE * SIDE + z) for x in range(SIDE) for z in range(SIDE)],
    )


def shift_z(value, step):
    return lax.ppermute(
        value,
        "tp",
        [(x * SIDE + z, x * SIDE + (z + step) % SIDE) for x in range(SIDE) for z in range(SIDE)],
    )


def swap_ctx(value):
    return lax.ppermute(value, "ctx", [(0, 1), (1, 0)])


def swap_core(value):
    return lax.ppermute(value, "dp", [(0, 1), (1, 0), (2, 3), (3, 2)])


def gather_rows_of(shift, rows):
    return [rows, shift(rows, 1), shift(rows, 2), shift(rows, -1)]


def exchange(shift, blocks):
    return [blocks[0], shift(blocks[1], 1), shift(blocks[2], 2), shift(blocks[3], -1)]


def call(kernel, name, out_shape, in_specs, out_specs, grid=(), scratch=(), limit=56, cost=None):
    return pl.pallas_call(
        kernel,
        name=name,
        out_shape=out_shape,
        grid=grid,
        in_specs=in_specs,
        out_specs=out_specs,
        scratch_shapes=list(scratch),
        compiler_params=pltpu.CompilerParams(vmem_limit_bytes=limit * MIB),
        cost_estimate=cost,
    )


def smem():
    return pl.BlockSpec(memory_space=pltpu.SMEM)


def vmem():
    return pl.BlockSpec(memory_space=pltpu.VMEM)


def whole(array):
    zeros = (0,) * array.ndim
    return pl.BlockSpec(array.shape, lambda *_: zeros, pipeline_mode=pl.Buffered(1))


def dot(left, right):
    return jnp.dot(left, right, preferred_element_type=F32)


def dot_nt(left, right):
    return lax.dot_general(left, right, (((1,), (1,)), ((), ())), preferred_element_type=F32)


def rows_of(chunk):
    return pl.ds(pl.multiple_of(chunk * BLOCK, BLOCK), BLOCK)


def attend(meta, chunk, q_ref, keys, values, scratch):
    sums, peaks, totals, even, odd = scratch[0], scratch[1], scratch[2], scratch[3:5], scratch[5:7]
    factor = math.log2(math.e) / math.sqrt(HD)
    mine = meta[meta[4] * 2 + chunk // 2] * 2 + lax.rem(chunk, 2)
    heads = [q_ref[rows_of(chunk), head * HD : (head + 1) * HD] for head in range(2)]
    for head in range(2):
        sums[head] = jnp.zeros((HD, BLOCK), F32)
        peaks[head] = jnp.full((1, BLOCK), NEGATIVE, F32)
        totals[head] = jnp.zeros((1, BLOCK), F32)

    def score(number, held):
        key_block = keys[rows_of(number), :]
        for head in range(2):
            held[head][...] = dot_nt(key_block, heads[head])

    def process(number, held, masked):
        value_block = values[:, rows_of(number)]
        for head in range(2):
            scores = held[head][...]
            if masked:
                seen = lax.broadcasted_iota(
                    jnp.int32, (BLOCK, BLOCK), 0
                ) <= lax.broadcasted_iota(jnp.int32, (BLOCK, BLOCK), 1)
                scores = jnp.where(seen, scores, NEGATIVE)
            peak = peaks[head]
            new_peak = jnp.maximum(peak, jnp.max(scores, axis=0, keepdims=True))
            weights = jnp.exp2(scores * factor - new_peak * factor)
            fading = jnp.exp2((peak - new_peak) * factor)
            peaks[head] = new_peak
            totals[head] = totals[head] * fading + jnp.sum(weights, axis=0, keepdims=True)
            sums[head] = sums[head] * fading + dot(value_block, weights.astype(BF16))

    score(0, even)

    def two(pair, carry):
        score(2 * pair + 1, odd)
        process(2 * pair, even, False)
        score(2 * pair + 2, even)
        process(2 * pair + 1, odd, False)
        return carry

    lax.fori_loop(0, mine // 2, two, 0)

    @pl.when(lax.rem(mine, 2) == 1)
    def _():
        score(mine, odd)
        process(mine - 1, even, False)
        process(mine, odd, True)

    @pl.when(lax.rem(mine, 2) == 0)
    def _():
        process(mine, even, True)

    return jnp.concatenate(
        [(sums[head] / totals[head]).T.astype(BF16) for head in range(2)], axis=1
    )


def attend_scratch():
    return [
        pltpu.VMEM((2, HD, BLOCK), F32),
        pltpu.VMEM((2, 1, BLOCK), F32),
        pltpu.VMEM((2, 1, BLOCK), F32),
    ] + [pltpu.VMEM((BLOCK, BLOCK), F32)] * 4


def join(pieces, joined):
    rows = pieces[0].shape[0]
    for number, piece in enumerate(pieces):
        joined[number * rows : (number + 1) * rows, :] = piece[...]


def attention_kernel(meta, q_ref, *refs):
    pieces, refs = refs[:8], refs[8:]
    outs, keys, values, context, scratch = refs[:3], *refs[3:6], refs[6:]
    ctx, x, z = meta[4], meta[5], meta[6]

    for number, piece in enumerate(pieces):
        part = lax.rem(ctx + number % 2, 2)
        back = (0, 1, 3, 2)[number // 2]
        z_of = lax.rem(z + SIDE - back, SIDE)
        for block in range(SIDE):
            x_of = lax.rem(x + SIDE - block, SIDE)
            place = meta[part * 2 + x_of // 2] * 8 + lax.rem(x_of, 2) * SIDE + z_of
            rows = pl.ds(pl.multiple_of(place * HD, HD), HD)
            keys[rows, :] = piece[block, :, :HD]
            values[:, rows] = piece[block, :, HD:].T

    @pl.loop(0, SIDE - 1)
    def _(number):
        chunk = lax.rem(x + 1 + number, SIDE)
        context[number] = attend(meta, chunk, q_ref, keys, values, scratch)

    for number, out in enumerate(outs):
        out[...] = context[number]


def attention(meta, queries, pieces):
    rows, width = queries.shape
    arrays = (queries, *pieces)
    outs = [jax.ShapeDtypeStruct((BLOCK, width), BF16)] * 3 + [
        jax.ShapeDtypeStruct((2 * rows, HD), BF16),
        jax.ShapeDtypeStruct((HD, 2 * rows), BF16),
    ]
    return call(
        attention_kernel,
        "attention",
        outs,
        [smem()] + [whole(array) for array in arrays],
        [pl.BlockSpec(out.shape, lambda: (0, 0)) for out in outs],
        scratch=[pltpu.VMEM((3, BLOCK, width), BF16), *attend_scratch()],
        cost=pl.CostEstimate(
            flops=16 * 10**9, bytes_accessed=7 * 10**6, transcendentals=10 * 10**6
        ),
    )(meta, *arrays)


def attention_end_kernel(meta, q_ref, keys, values, *refs):
    others, weights, out, refs = refs[:3], refs[3:11], refs[11], refs[12:]
    outs_z, joined, scratch = refs[:4], refs[4:6], refs[6:]
    x, z = meta[5], meta[6]
    join(weights[:4], joined[0])
    join(weights[4:], joined[1])
    out[...] = attend(meta, x, q_ref, keys, values, scratch)
    for number, context in enumerate((out, *others)):
        x_of = lax.rem(x + number, SIDE)
        rows = pl.ds(pl.multiple_of(x_of * TOKENS, TOKENS), TOKENS)
        for step_of in range(SIDE):
            to_z = lax.rem(z + step_of, SIDE)
            part = pl.ds(pl.multiple_of(to_z * TOKENS, TOKENS), TOKENS)
            outs_z[step_of][rows, :] = context[part, :]


def attention_end(meta, queries, keys, values, others, weights):
    width = queries.shape[1]
    arrays = (queries, keys, values, *others, *weights)
    outs = [jax.ShapeDtypeStruct((BLOCK, width), BF16)] * 5
    outs += [jax.ShapeDtypeStruct((SIDE * weights[0].shape[0], weights[0].shape[1]), BF16)] * 2
    return call(
        attention_end_kernel,
        "attention_end",
        outs,
        [smem()] + [whole(array) for array in arrays],
        [pl.BlockSpec(out.shape, lambda: (0, 0)) for out in outs],
        scratch=attend_scratch(),
        cost=pl.CostEstimate(
            flops=6 * 10**9, bytes_accessed=7 * 10**6, transcendentals=3 * 10**6
        ),
    )(meta, *arrays)


def projection_kernel(axis, meta, *refs):
    context, weights, outs, held = refs[:4], refs[4:6], refs[6:10], refs[10]
    step, me = pl.program_id(0), meta[axis]
    width = context[0].shape[1]
    columns = weights[0].shape[1]
    steps = held.shape[1] // (2 * columns)
    for side, weight in enumerate(weights):
        total = None
        for number, rows in enumerate(context):
            term = dot(rows[...], weight[number * width : (number + 1) * width, :])
            total = term if total is None else total + term
        start = pl.multiple_of((side * steps + step) * columns, columns)
        held[:, pl.ds(start, columns)] = total.astype(BF16)

    @pl.when(step == steps - 1)
    def _():
        for number, out in enumerate(outs):
            to = lax.rem(me + number, SIDE)
            out[...] = held[pl.ds(pl.multiple_of(to * TOKENS, TOKENS), TOKENS), :]


def projection(axis, meta, context, weights):
    depth, columns = weights[0].shape
    part = columns // 4
    return call(
        functools.partial(projection_kernel, axis),
        "projection",
        [jax.ShapeDtypeStruct((TOKENS, 2 * columns), BF16)] * 4,
        [smem()]
        + [whole(array) for array in context]
        + [pl.BlockSpec((depth, part), lambda i: (0, i))] * 2,
        [pl.BlockSpec((TOKENS, 2 * columns), lambda i: (0, 0))] * 4,
        grid=(4,),
        scratch=[pltpu.VMEM((SIDE * TOKENS, 2 * columns), BF16)],
        cost=pl.CostEstimate(
            flops=4 * 512 * 1024 * columns, bytes_accessed=7 * 10**6, transcendentals=0
        ),
    )(meta, *context, *weights)


def wide_scratch():
    return pltpu.VMEM((SEG // HD, TOKENS * SLOTS, HD), F32)


def widen(wide, rows_ref):
    for part in range(SEG // HD):
        wide[part] = rows_ref[:, part * HD : (part + 1) * HD].astype(F32)


def narrow(wide):
    return jnp.concatenate([wide[part].astype(BF16) for part in range(SEG // HD)], axis=1)


def gather_rows(wide, segment):
    rows = pl.ds(segment, TOKENS, stride=SLOTS)
    return jnp.concatenate([wide[part, rows, :] for part in range(SEG // HD)], axis=1).astype(BF16)


def scatter_rows(wide, segment, value):
    rows = pl.ds(segment, TOKENS, stride=SLOTS)
    for part in range(SEG // HD):
        wide[part, rows, :] = value[:, part * HD : (part + 1) * HD]


def add_terms(core, terms, residual, state, base):
    quarter = terms[0].shape[1] // 2
    for side in range(2):
        place = base + quarter * lax.rem(core + side, 2)
        columns = pl.ds(pl.multiple_of(place, quarter), quarter)
        part = slice(side * quarter, (side + 1) * quarter)
        total = terms[0][:, part].astype(F32)
        for term in terms[1:]:
            total = total + term[:, part].astype(F32)
        state[:, columns] = residual[:, columns].astype(F32) + total


def settle_kernel(meta, *refs):
    terms, (residual, state) = refs[:4], refs[4:]
    add_terms(meta[7], terms, residual, state, 0)


def settle(meta, terms, residual):
    half = terms[0].shape[1]
    return call(
        settle_kernel,
        "settle",
        jax.ShapeDtypeStruct((TOKENS, half), F32),
        [smem()]
        + [whole(term) for term in terms]
        + [pl.BlockSpec((TOKENS, half), lambda i: (0, 0))],
        pl.BlockSpec((TOKENS, half), lambda i: (0, 0)),
        grid=(1,),
        cost=pl.CostEstimate(flops=2 * 10**10, bytes_accessed=4 * 10**6, transcendentals=0),
    )(meta, *terms, residual)


def dispatch_kernel(meta, *refs):
    terms, refs = refs[:4], refs[4:]
    first, residual, gain, main, late, outgoing, state, normed, wide, spread = refs
    step = pl.program_id(0)
    half = first.shape[1]

    @pl.when(step == 0)
    def _():
        state[:, :half] = first[...]
        add_terms(meta[7], terms, residual, state, half)
        value = state[...]
        scale = lax.rsqrt(jnp.mean(value * value, axis=1, keepdims=True) + 1e-06)
        for segment in range(SLOTS):
            columns = slice(segment * SEG, (segment + 1) * SEG)
            normed[:, columns] = (state[:, columns] * scale * gain[:, columns]).astype(BF16)

        for segment in range(SLOTS):
            columns = slice(segment * SEG, (segment + 1) * SEG)
            scatter_rows(wide, segment, dot(late[...], normed[:, columns]))
        spread[...] = narrow(wide)

    for start in range(0, 2 * half, DISPATCH_COLUMNS):
        columns = slice(start, start + DISPATCH_COLUMNS)
        outgoing[:, columns] = dot(main[...], normed[:, columns]).astype(BF16)
    rows = outgoing.shape[0]
    outgoing[:, 2 * half :] = spread[pl.ds(pl.multiple_of(step * rows, rows), rows), :]


def dispatch(meta, terms, first, residual, gain, main, late):
    rows, width = main.shape[0], residual.shape[1]
    arrays = (*terms, first, residual, gain)
    return call(
        dispatch_kernel,
        "dispatch",
        [
            jax.ShapeDtypeStruct((rows, width + SEG), BF16),
            jax.ShapeDtypeStruct((TOKENS, width), F32),
        ],
        [smem()]
        + [whole(a) for a in arrays]
        + [pl.BlockSpec((ROWS, TOKENS), lambda i: (i, 0)), whole(late)],
        [
            pl.BlockSpec((ROWS, width + SEG), lambda i: (i, 0)),
            pl.BlockSpec((TOKENS, width), lambda i: (0, 0)),
        ],
        grid=(rows // ROWS,),
        scratch=[
            pltpu.VMEM((TOKENS, width), BF16),
            wide_scratch(),
            pltpu.VMEM((rows, SEG), BF16),
        ],
        cost=pl.CostEstimate(flops=3 * 10**9, bytes_accessed=16 * 10**6, transcendentals=0),
    )(meta, *arrays, main, late)


def expert_kernel(rows_ref, over_ref, up_ref, down_hbm, out_ref, wide, spread, down_ref, done):
    step = pl.program_id(0)
    width = down_ref.shape[2]
    fetch = pltpu.make_async_copy(down_hbm, down_ref, done)

    def act(value):
        return (value / (1.0 + jnp.exp(-value))).astype(BF16)

    @pl.when(step == 0)
    def _():
        fetch.start()
        widen(wide, over_ref)
        total = None
        for segment in range(SLOTS):
            part = up_ref[0, segment * SEG : (segment + 1) * SEG, :]
            term = dot(gather_rows(wide, segment), part)
            total = term if total is None else total + term
        inner = act(total)
        fetch.wait()
        for segment in range(SLOTS):
            part = down_ref[0, :, segment * SEG : (segment + 1) * SEG]
            scatter_rows(wide, segment, dot(inner, part))
        spread[...] = narrow(wide)

    inner = act(dot(rows_ref[:, :width], up_ref[0]))
    for start in range(0, width, DOWN_COLUMNS):
        columns = slice(start, start + DOWN_COLUMNS)
        out_ref[:, columns] = dot(inner, down_ref[0, :, columns]).astype(BF16)
    mine = pl.ds(pl.multiple_of(step * ROWS, ROWS), ROWS)
    out_ref[:, width:] = spread[mine, :]


def experts(arrived, up, down):
    rows, columns = arrived.shape
    inner = up.shape[2]
    return call(
        expert_kernel,
        "experts",
        jax.ShapeDtypeStruct((rows, columns), BF16),
        [
            pl.BlockSpec((ROWS, columns), lambda i: (i, 0)),
            pl.BlockSpec((rows, SEG), lambda i: (0, SLOTS)),
            vmem(),
            pl.BlockSpec(memory_space=pl.ANY),
        ],
        pl.BlockSpec((ROWS, columns), lambda i: (i, 0)),
        grid=(rows // ROWS,),
        scratch=[
            wide_scratch(),
            pltpu.VMEM((rows, SEG), BF16),
            pltpu.VMEM(down.shape, BF16),
            pltpu.SemaphoreType.DMA,
        ],
        limit=46,
        cost=pl.CostEstimate(
            flops=4 * rows * columns * inner,
            bytes_accessed=32 * 10**6,
            transcendentals=rows * inner,
        ),
    )(arrived, arrived, up, down)


def combine_kernel(main, late, rows_ref, over_ref, state, out, total, wide):
    step = pl.program_id(0)
    segments = [(i, slice(i * SEG, (i + 1) * SEG)) for i in range(SLOTS)]

    def both(value):
        return value[:TOKENS] + value[TOKENS:]

    @pl.when(step == 0)
    def _():
        widen(wide, over_ref)
        for segment, columns in segments:
            late_part = both(dot(late[...], gather_rows(wide, segment)))
            total[:, columns] = state[:, columns] + late_part

    for start in range(0, total.shape[1], COMBINE_COLUMNS):
        columns = slice(start, start + COMBINE_COLUMNS)
        total[:, columns] += both(dot(main[...], rows_ref[:, columns]))

    @pl.when(step == pl.num_programs(0) - 1)
    def _():
        out[...] = total[...].astype(BF16)


def combine(main, late, returned, state):
    rows, columns = returned.shape
    return call(
        combine_kernel,
        "combine",
        jax.ShapeDtypeStruct(state.shape, BF16),
        [
            pl.BlockSpec((2 * TOKENS, ROWS), lambda i: (0, i)),
            whole(late),
            pl.BlockSpec((ROWS, columns), lambda i: (i, 0)),
            pl.BlockSpec((rows, SEG), lambda i: (0, SLOTS), pipeline_mode=pl.Buffered(1)),
            whole(state),
        ],
        pl.BlockSpec(state.shape, lambda i: (0, 0)),
        grid=(rows // ROWS,),
        scratch=[pltpu.VMEM(state.shape, F32), wide_scratch()],
        cost=pl.CostEstimate(flops=4 * 10**9, bytes_accessed=13 * 10**6, transcendentals=0),
    )(main, late, returned, returned, state)


def routes_kernel(ids, weights, main, late, back_main, back_late):
    square = (TOKENS, TOKENS)
    row = lax.broadcasted_iota(jnp.int32, square, 0)
    column = lax.broadcasted_iota(jnp.int32, square, 1)
    named, weight = jnp.zeros(square, F32), jnp.zeros(square, F32)
    for choice in range(ids.shape[1]):
        chosen = column == ids[:, choice : choice + 1]
        named = named + jnp.where(chosen, 1.0, 0.0)
        weight = weight + jnp.where(chosen, weights[:, choice : choice + 1], 0.0)
    earlier = jnp.where(column < row, 1.0, 0.0).astype(BF16)
    rank = jnp.where(named > 0.0, dot(earlier, named.astype(BF16)), -1.0)
    high = weight.astype(BF16)
    low = (weight - high.astype(F32)).astype(BF16)

    tall = main.shape
    row = lax.broadcasted_iota(jnp.int32, tall, 0)
    column = lax.broadcasted_iota(jnp.int32, tall, 1)
    spread = jnp.where(row // SLOTS == column, 1.0, 0.0).astype(BF16)
    ranks = dot(spread, rank.T.astype(BF16))
    main[...] = jnp.where(ranks == (row % SLOTS).astype(F32), 1.0, 0.0).astype(BF16)
    late[...] = jnp.where(rank.T == SLOTS, 1.0, 0.0).astype(BF16)

    flat = (TOKENS, tall[0])
    hit = dot_nt(rank.astype(BF16), spread) == (
        lax.broadcasted_iota(jnp.int32, flat, 1) % SLOTS
    ).astype(F32)
    for half, part in enumerate((high, low)):
        rows = slice(half * TOKENS, (half + 1) * TOKENS)
        back_main[rows, :] = jnp.where(hit, dot_nt(part, spread), 0.0).astype(BF16)
        back_late[rows, :] = jnp.where(rank == SLOTS, part.astype(F32), 0.0).astype(BF16)


def routes(expert_ids, route_weights, n_experts):
    outs = [
        jax.ShapeDtypeStruct(shape, BF16)
        for shape in (
            (n_experts * SLOTS, TOKENS),
            (n_experts, TOKENS),
            (2 * TOKENS, n_experts * SLOTS),
            (2 * TOKENS, n_experts),
        )
    ]
    return call(
        routes_kernel,
        "routes",
        outs,
        [whole(expert_ids), whole(route_weights)],
        [pl.BlockSpec(out.shape, lambda: (0, 0)) for out in outs],
        cost=pl.CostEstimate(flops=2 * 10**8, bytes_accessed=10**6, transcendentals=0),
    )(expert_ids, route_weights)


def local(
    queries,
    key_rows,
    value_rows,
    span_order,
    out_proj,
    residual,
    norm_gain,
    expert_ids,
    route_weights,
    w_up,
    w_down,
):
    n_devices = lax.axis_size("dp") * lax.axis_size("ctx") * lax.axis_size("tp")
    core = lax.axis_index("dp") % 2
    ctx = lax.axis_index("ctx")
    x, z = lax.axis_index("tp") // SIDE, lax.axis_index("tp") % SIDE
    meta = jnp.concatenate([span_order, jnp.stack([ctx, x, z, core]).astype(jnp.int32)])

    def head_block(step):
        start = (x + step) % SIDE * HD
        return jnp.concatenate(
            [
                lax.dynamic_slice_in_dim(key_rows, start, HD, 1),
                lax.dynamic_slice_in_dim(value_rows, start, HD, 1),
            ],
            axis=1,
        )

    width = out_proj.shape[1]
    quarter = width // 4

    def weights_part(base):
        return lax.dynamic_slice_in_dim(out_proj, base + core * quarter, quarter, 1)

    def after(value, *others):
        return lax.optimization_barrier((value, *others))[0]

    own = jnp.stack(exchange(shift_x, [head_block(step) for step in range(SIDE)]))
    other = swap_ctx(own)
    before_own, after_own = shift_z(own, 1), shift_z(own, -1)
    before_other, after_other = shift_z(other, 1), shift_z(other, -1)
    far_own = shift_z(before_own, 1)
    far_other = shift_z(after_other, -1)
    weights_x = gather_rows_of(shift_x, after(weights_part(0), own))
    weights_z = gather_rows_of(shift_z, after(weights_part(width // 2), far_own, far_other))
    pieces = [
        own,
        other,
        before_own,
        before_other,
        after_own,
        after_other,
        far_own,
        far_other,
    ]

    main, late, back_main, back_late = routes(expert_ids, route_weights, n_devices)
    queries = after(queries, main)

    *far, keys, values = attention(meta, queries, pieces)
    mine, *parts, weights_x, weights_z = attention_end(
        meta, queries, keys, values, far, [*weights_x, *weights_z]
    )
    context_x = exchange(shift_x, [mine, *far])
    other_x = swap_core(after(weights_x, *context_x[1:]))
    context_z = exchange(shift_z, [after(part, *context_x) for part in parts])
    other_z = swap_core(after(weights_z, *context_x))
    terms_z = projection(6, meta, context_x, [weights_x, other_x])
    terms_x = projection(5, meta, context_z, [after(weights_z, terms_z[0]), other_z])
    terms_z, terms_x = exchange(shift_z, terms_z), exchange(shift_x, terms_x)
    outgoing, state = dispatch(
        meta, terms_x, settle(meta, terms_z, residual), residual, norm_gain[None, :], main, late
    )

    def all_to_all(rows):
        blocks = rows.reshape(n_devices, SLOTS, rows.shape[1])
        return lax.all_to_all(
            blocks, ("dp", "ctx", "tp"), split_axis=0, concat_axis=0, tiled=True
        ).reshape(rows.shape)

    arrived = all_to_all(outgoing)
    returned = all_to_all(experts(arrived, w_up, w_down))
    return combine(back_main, back_late, returned, state)


def solution(mesh):
    return jax.shard_map(
        local,
        mesh=mesh,
        in_specs=(
            P(("dp", "ctx"), "tp"),
            P(("dp", "ctx", "tp"), None),
            P(("dp", "ctx", "tp"), None),
            P(),
            P("tp", None),
            P(("dp", "ctx", "tp"), None),
            P(),
            P(("dp", "ctx", "tp"), None),
            P(("dp", "ctx", "tp"), None),
            P(("dp", "ctx", "tp"), None, None),
            P(("dp", "ctx", "tp"), None, None),
        ),
        out_specs=P(("dp", "ctx", "tp"), None),
        check_vma=False,
    )
```

```python
import functools
import math

import jax
import jax.numpy as jnp
from jax import lax
from jax.experimental import pallas as pl
from jax.experimental.pallas import tpu as pltpu
from jax.sharding import PartitionSpec as P

HD = 128
KVH = 4
SIDE = 4
TOKENS = 128
SLOTS = 8
SEG = 512
ROWS = 256
DISPATCH_COLUMNS = 512
DOWN_COLUMNS = 512
COMBINE_COLUMNS = 512
BLOCK = 512
NEGATIVE = -1e30
MIB = 1 << 20
F32 = jnp.float32
BF16 = jnp.bfloat16


def shift_x(value, step):
    return lax.ppermute(
        value,
        "tp",
        [(x * SIDE + z, (x + step) % SIDE * SIDE + z) for x in range(SIDE) for z in range(SIDE)],
    )


def shift_z(value, step):
    return lax.ppermute(
        value,
        "tp",
        [(x * SIDE + z, x * SIDE + (z + step) % SIDE) for x in range(SIDE) for z in range(SIDE)],
    )


def swap_ctx(value):
    return lax.ppermute(value, "ctx", [(0, 1), (1, 0)])


def swap_core(value):
    return lax.ppermute(value, "dp", [(0, 1), (1, 0), (2, 3), (3, 2)])


def gather_rows_of(shift, rows):
    return [rows, shift(rows, 1), shift(rows, 2), shift(rows, -1)]


def exchange(shift, blocks):
    return [blocks[0], shift(blocks[1], 1), shift(blocks[2], 2), shift(blocks[3], -1)]


def call(kernel, name, out_shape, in_specs, out_specs, grid=(), scratch=(), limit=56, cost=None):
    return pl.pallas_call(
        kernel,
        name=name,
        out_shape=out_shape,
        grid=grid,
        in_specs=in_specs,
        out_specs=out_specs,
        scratch_shapes=list(scratch),
        compiler_params=pltpu.CompilerParams(vmem_limit_bytes=limit * MIB),
        cost_estimate=cost,
    )


def smem():
    return pl.BlockSpec(memory_space=pltpu.SMEM)


def vmem():
    return pl.BlockSpec(memory_space=pltpu.VMEM)


def whole(array):
    zeros = (0,) * array.ndim
    return pl.BlockSpec(array.shape, lambda *_: zeros, pipeline_mode=pl.Buffered(1))


def dot(left, right):
    return jnp.dot(left, right, preferred_element_type=F32)


def dot_nt(left, right):
    return lax.dot_general(left, right, (((1,), (1,)), ((), ())), preferred_element_type=F32)


def rows_of(chunk):
    return pl.ds(pl.multiple_of(chunk * BLOCK, BLOCK), BLOCK)


def attend(meta, chunk, q_ref, keys, values, scratch):
    sums, peaks, totals, even, odd = scratch[0], scratch[1], scratch[2], scratch[3:5], scratch[5:7]
    factor = math.log2(math.e) / math.sqrt(HD)
    mine = meta[meta[4] * 2 + chunk // 2] * 2 + lax.rem(chunk, 2)
    heads = [q_ref[rows_of(chunk), head * HD : (head + 1) * HD] for head in range(2)]
    for head in range(2):
        sums[head] = jnp.zeros((HD, BLOCK), F32)
        peaks[head] = jnp.full((1, BLOCK), NEGATIVE, F32)
        totals[head] = jnp.zeros((1, BLOCK), F32)

    def score(number, held):
        key_block = keys[rows_of(number), :]
        for head in range(2):
            held[head][...] = dot_nt(key_block, heads[head])

    def process(number, held, masked):
        value_block = values[:, rows_of(number)]
        for head in range(2):
            scores = held[head][...]
            if masked:
                seen = lax.broadcasted_iota(
                    jnp.int32, (BLOCK, BLOCK), 0
                ) <= lax.broadcasted_iota(jnp.int32, (BLOCK, BLOCK), 1)
                scores = jnp.where(seen, scores, NEGATIVE)
            peak = peaks[head]
            new_peak = jnp.maximum(peak, jnp.max(scores, axis=0, keepdims=True))
            weights = jnp.exp2(scores * factor - new_peak * factor)
            fading = jnp.exp2((peak - new_peak) * factor)
            peaks[head] = new_peak
            totals[head] = totals[head] * fading + jnp.sum(weights, axis=0, keepdims=True)
            sums[head] = sums[head] * fading + dot(value_block, weights.astype(BF16))

    score(0, even)

    def two(pair, carry):
        score(2 * pair + 1, odd)
        process(2 * pair, even, False)
        score(2 * pair + 2, even)
        process(2 * pair + 1, odd, False)
        return carry

    lax.fori_loop(0, mine // 2, two, 0)

    @pl.when(lax.rem(mine, 2) == 1)
    def _():
        score(mine, odd)
        process(mine - 1, even, False)
        process(mine, odd, True)

    @pl.when(lax.rem(mine, 2) == 0)
    def _():
        process(mine, even, True)

    return jnp.concatenate(
        [(sums[head] / totals[head]).T.astype(BF16) for head in range(2)], axis=1
    )


def attend_scratch():
    return [
        pltpu.VMEM((2, HD, BLOCK), F32),
        pltpu.VMEM((2, 1, BLOCK), F32),
        pltpu.VMEM((2, 1, BLOCK), F32),
    ] + [pltpu.VMEM((BLOCK, BLOCK), F32)] * 4


def join(pieces, joined):
    rows = pieces[0].shape[0]
    for number, piece in enumerate(pieces):
        joined[number * rows : (number + 1) * rows, :] = piece[...]


def attention_kernel(meta, q_ref, *refs):
    pieces, refs = refs[:8], refs[8:]
    outs, keys, values, context, scratch = refs[:3], *refs[3:6], refs[6:]
    ctx, x, z = meta[4], meta[5], meta[6]

    for number, piece in enumerate(pieces):
        part = lax.rem(ctx + number % 2, 2)
        back = (0, 1, 3, 2)[number // 2]
        z_of = lax.rem(z + SIDE - back, SIDE)
        for block in range(SIDE):
            x_of = lax.rem(x + SIDE - block, SIDE)
            place = meta[part * 2 + x_of // 2] * 8 + lax.rem(x_of, 2) * SIDE + z_of
            rows = pl.ds(pl.multiple_of(place * HD, HD), HD)
            keys[rows, :] = piece[block, :, :HD]
            values[:, rows] = piece[block, :, HD:].T

    @pl.loop(0, SIDE - 1)
    def _(number):
        chunk = lax.rem(x + 1 + number, SIDE)
        context[number] = attend(meta, chunk, q_ref, keys, values, scratch)

    for number, out in enumerate(outs):
        out[...] = context[number]


def attention(meta, queries, pieces):
    rows, width = queries.shape
    arrays = (queries, *pieces)
    outs = [jax.ShapeDtypeStruct((BLOCK, width), BF16)] * 3 + [
        jax.ShapeDtypeStruct((2 * rows, HD), BF16),
        jax.ShapeDtypeStruct((HD, 2 * rows), BF16),
    ]
    return call(
        attention_kernel,
        "attention",
        outs,
        [smem()] + [whole(array) for array in arrays],
        [pl.BlockSpec(out.shape, lambda: (0, 0)) for out in outs],
        scratch=[pltpu.VMEM((3, BLOCK, width), BF16), *attend_scratch()],
        cost=pl.CostEstimate(
            flops=16 * 10**9, bytes_accessed=7 * 10**6, transcendentals=10 * 10**6
        ),
    )(meta, *arrays)


def attention_end_kernel(meta, q_ref, keys, values, *refs):
    others, weights, out, refs = refs[:3], refs[3:11], refs[11], refs[12:]
    outs_z, joined, scratch = refs[:4], refs[4:6], refs[6:]
    x, z = meta[5], meta[6]
    join(weights[:4], joined[0])
    join(weights[4:], joined[1])
    out[...] = attend(meta, x, q_ref, keys, values, scratch)
    for number, context in enumerate((out, *others)):
        x_of = lax.rem(x + number, SIDE)
        rows = pl.ds(pl.multiple_of(x_of * TOKENS, TOKENS), TOKENS)
        for step_of in range(SIDE):
            to_z = lax.rem(z + step_of, SIDE)
            part = pl.ds(pl.multiple_of(to_z * TOKENS, TOKENS), TOKENS)
            outs_z[step_of][rows, :] = context[part, :]


def attention_end(meta, queries, keys, values, others, weights):
    width = queries.shape[1]
    arrays = (queries, keys, values, *others, *weights)
    outs = [jax.ShapeDtypeStruct((BLOCK, width), BF16)] * 5
    outs += [jax.ShapeDtypeStruct((SIDE * weights[0].shape[0], weights[0].shape[1]), BF16)] * 2
    return call(
        attention_end_kernel,
        "attention_end",
        outs,
        [smem()] + [whole(array) for array in arrays],
        [pl.BlockSpec(out.shape, lambda: (0, 0)) for out in outs],
        scratch=attend_scratch(),
        cost=pl.CostEstimate(
            flops=6 * 10**9, bytes_accessed=7 * 10**6, transcendentals=3 * 10**6
        ),
    )(meta, *arrays)


def projection_kernel(axis, meta, *refs):
    context, weights, outs, held = refs[:4], refs[4:6], refs[6:10], refs[10]
    step, me = pl.program_id(0), meta[axis]
    width = context[0].shape[1]
    columns = weights[0].shape[1]
    steps = held.shape[1] // (2 * columns)
    for side, weight in enumerate(weights):
        total = None
        for number, rows in enumerate(context):
            term = dot(rows[...], weight[number * width : (number + 1) * width, :])
            total = term if total is None else total + term
        start = pl.multiple_of((side * steps + step) * columns, columns)
        held[:, pl.ds(start, columns)] = total.astype(BF16)

    @pl.when(step == steps - 1)
    def _():
        for number, out in enumerate(outs):
            to = lax.rem(me + number, SIDE)
            out[...] = held[pl.ds(pl.multiple_of(to * TOKENS, TOKENS), TOKENS), :]


def projection(axis, meta, context, weights):
    depth, columns = weights[0].shape
    part = columns // 4
    return call(
        functools.partial(projection_kernel, axis),
        "projection",
        [jax.ShapeDtypeStruct((TOKENS, 2 * columns), BF16)] * 4,
        [smem()]
        + [whole(array) for array in context]
        + [pl.BlockSpec((depth, part), lambda i: (0, i))] * 2,
        [pl.BlockSpec((TOKENS, 2 * columns), lambda i: (0, 0))] * 4,
        grid=(4,),
        scratch=[pltpu.VMEM((SIDE * TOKENS, 2 * columns), BF16)],
        cost=pl.CostEstimate(
            flops=4 * 512 * 1024 * columns, bytes_accessed=7 * 10**6, transcendentals=0
        ),
    )(meta, *context, *weights)


def wide_scratch():
    return pltpu.VMEM((SEG // HD, TOKENS * SLOTS, HD), F32)


def widen(wide, rows_ref):
    for part in range(SEG // HD):
        wide[part] = rows_ref[:, part * HD : (part + 1) * HD].astype(F32)


def narrow(wide):
    return jnp.concatenate([wide[part].astype(BF16) for part in range(SEG // HD)], axis=1)


def gather_rows(wide, segment):
    rows = pl.ds(segment, TOKENS, stride=SLOTS)
    return jnp.concatenate([wide[part, rows, :] for part in range(SEG // HD)], axis=1).astype(BF16)


def scatter_rows(wide, segment, value):
    rows = pl.ds(segment, TOKENS, stride=SLOTS)
    for part in range(SEG // HD):
        wide[part, rows, :] = value[:, part * HD : (part + 1) * HD]


def add_terms(core, terms, residual, state, base):
    quarter = terms[0].shape[1] // 2
    for side in range(2):
        place = base + quarter * lax.rem(core + side, 2)
        columns = pl.ds(pl.multiple_of(place, quarter), quarter)
        part = slice(side * quarter, (side + 1) * quarter)
        total = terms[0][:, part].astype(F32)
        for term in terms[1:]:
            total = total + term[:, part].astype(F32)
        state[:, columns] = residual[:, columns].astype(F32) + total


def settle_kernel(meta, *refs):
    terms, (residual, state) = refs[:4], refs[4:]
    add_terms(meta[7], terms, residual, state, 0)


def settle(meta, terms, residual):
    half = terms[0].shape[1]
    return call(
        settle_kernel,
        "settle",
        jax.ShapeDtypeStruct((TOKENS, half), F32),
        [smem()]
        + [whole(term) for term in terms]
        + [pl.BlockSpec((TOKENS, half), lambda i: (0, 0))],
        pl.BlockSpec((TOKENS, half), lambda i: (0, 0)),
        grid=(1,),
        cost=pl.CostEstimate(flops=2 * 10**10, bytes_accessed=4 * 10**6, transcendentals=0),
    )(meta, *terms, residual)


def dispatch_kernel(meta, *refs):
    terms, refs = refs[:4], refs[4:]
    first, residual, gain, main, late, outgoing, state, normed, wide, spread = refs
    step = pl.program_id(0)
    half = first.shape[1]

    @pl.when(step == 0)
    def _():
        state[:, :half] = first[...]
        add_terms(meta[7], terms, residual, state, half)
        value = state[...]
        scale = lax.rsqrt(jnp.mean(value * value, axis=1, keepdims=True) + 1e-06)
        for segment in range(SLOTS):
            columns = slice(segment * SEG, (segment + 1) * SEG)
            normed[:, columns] = (state[:, columns] * scale * gain[:, columns]).astype(BF16)

        for segment in range(SLOTS):
            columns = slice(segment * SEG, (segment + 1) * SEG)
            scatter_rows(wide, segment, dot(late[...], normed[:, columns]))
        spread[...] = narrow(wide)

    for start in range(0, 2 * half, DISPATCH_COLUMNS):
        columns = slice(start, start + DISPATCH_COLUMNS)
        outgoing[:, columns] = dot(main[...], normed[:, columns]).astype(BF16)
    rows = outgoing.shape[0]
    outgoing[:, 2 * half :] = spread[pl.ds(pl.multiple_of(step * rows, rows), rows), :]


def dispatch(meta, terms, first, residual, gain, main, late):
    rows, width = main.shape[0], residual.shape[1]
    arrays = (*terms, first, residual, gain)
    return call(
        dispatch_kernel,
        "dispatch",
        [
            jax.ShapeDtypeStruct((rows, width + SEG), BF16),
            jax.ShapeDtypeStruct((TOKENS, width), F32),
        ],
        [smem()]
        + [whole(a) for a in arrays]
        + [pl.BlockSpec((ROWS, TOKENS), lambda i: (i, 0)), whole(late)],
        [
            pl.BlockSpec((ROWS, width + SEG), lambda i: (i, 0)),
            pl.BlockSpec((TOKENS, width), lambda i: (0, 0)),
        ],
        grid=(rows // ROWS,),
        scratch=[
            pltpu.VMEM((TOKENS, width), BF16),
            wide_scratch(),
            pltpu.VMEM((rows, SEG), BF16),
        ],
        cost=pl.CostEstimate(flops=3 * 10**9, bytes_accessed=16 * 10**6, transcendentals=0),
    )(meta, *arrays, main, late)


def expert_kernel(rows_ref, over_ref, up_ref, down_hbm, out_ref, wide, spread, down_ref, done):
    step = pl.program_id(0)
    width = down_ref.shape[2]
    fetch = pltpu.make_async_copy(down_hbm, down_ref, done)

    def act(value):
        return (value / (1.0 + jnp.exp(-value))).astype(BF16)

    @pl.when(step == 0)
    def _():
        fetch.start()
        widen(wide, over_ref)
        total = None
        for segment in range(SLOTS):
            part = up_ref[0, segment * SEG : (segment + 1) * SEG, :]
            term = dot(gather_rows(wide, segment), part)
            total = term if total is None else total + term
        inner = act(total)
        fetch.wait()
        for segment in range(SLOTS):
            part = down_ref[0, :, segment * SEG : (segment + 1) * SEG]
            scatter_rows(wide, segment, dot(inner, part))
        spread[...] = narrow(wide)

    inner = act(dot(rows_ref[:, :width], up_ref[0]))
    for start in range(0, width, DOWN_COLUMNS):
        columns = slice(start, start + DOWN_COLUMNS)
        out_ref[:, columns] = dot(inner, down_ref[0, :, columns]).astype(BF16)
    mine = pl.ds(pl.multiple_of(step * ROWS, ROWS), ROWS)
    out_ref[:, width:] = spread[mine, :]


def experts(arrived, up, down):
    rows, columns = arrived.shape
    inner = up.shape[2]
    return call(
        expert_kernel,
        "experts",
        jax.ShapeDtypeStruct((rows, columns), BF16),
        [
            pl.BlockSpec((ROWS, columns), lambda i: (i, 0)),
            pl.BlockSpec((rows, SEG), lambda i: (0, SLOTS)),
            vmem(),
            pl.BlockSpec(memory_space=pl.ANY),
        ],
        pl.BlockSpec((ROWS, columns), lambda i: (i, 0)),
        grid=(rows // ROWS,),
        scratch=[
            wide_scratch(),
            pltpu.VMEM((rows, SEG), BF16),
            pltpu.VMEM(down.shape, BF16),
            pltpu.SemaphoreType.DMA,
        ],
        limit=46,
        cost=pl.CostEstimate(
            flops=4 * rows * columns * inner,
            bytes_accessed=32 * 10**6,
            transcendentals=rows * inner,
        ),
    )(arrived, arrived, up, down)


def combine_kernel(main, late, rows_ref, over_ref, state, out, total, wide):
    step = pl.program_id(0)
    segments = [(i, slice(i * SEG, (i + 1) * SEG)) for i in range(SLOTS)]

    def both(value):
        return value[:TOKENS] + value[TOKENS:]

    @pl.when(step == 0)
    def _():
        widen(wide, over_ref)
        for segment, columns in segments:
            late_part = both(dot(late[...], gather_rows(wide, segment)))
            total[:, columns] = state[:, columns] + late_part

    for start in range(0, total.shape[1], COMBINE_COLUMNS):
        columns = slice(start, start + COMBINE_COLUMNS)
        total[:, columns] += both(dot(main[...], rows_ref[:, columns]))

    @pl.when(step == pl.num_programs(0) - 1)
    def _():
        out[...] = total[...].astype(BF16)


def combine(main, late, returned, state):
    rows, columns = returned.shape
    return call(
        combine_kernel,
        "combine",
        jax.ShapeDtypeStruct(state.shape, BF16),
        [
            pl.BlockSpec((2 * TOKENS, ROWS), lambda i: (0, i)),
            whole(late),
            pl.BlockSpec((ROWS, columns), lambda i: (i, 0)),
            pl.BlockSpec((rows, SEG), lambda i: (0, SLOTS), pipeline_mode=pl.Buffered(1)),
            whole(state),
        ],
        pl.BlockSpec(state.shape, lambda i: (0, 0)),
        grid=(rows // ROWS,),
        scratch=[pltpu.VMEM(state.shape, F32), wide_scratch()],
        cost=pl.CostEstimate(flops=4 * 10**9, bytes_accessed=13 * 10**6, transcendentals=0),
    )(main, late, returned, returned, state)


def routes_kernel(ids, weights, main, late, back_main, back_late):
    square = (TOKENS, TOKENS)
    row = lax.broadcasted_iota(jnp.int32, square, 0)
    column = lax.broadcasted_iota(jnp.int32, square, 1)
    named, weight = jnp.zeros(square, F32), jnp.zeros(square, F32)
    for choice in range(ids.shape[1]):
        chosen = column == ids[:, choice : choice + 1]
        named = named + jnp.where(chosen, 1.0, 0.0)
        weight = weight + jnp.where(chosen, weights[:, choice : choice + 1], 0.0)
    earlier = jnp.where(column < row, 1.0, 0.0).astype(BF16)
    rank = jnp.where(named > 0.0, dot(earlier, named.astype(BF16)), -1.0)
    high = weight.astype(BF16)
    low = (weight - high.astype(F32)).astype(BF16)

    tall = main.shape
    row = lax.broadcasted_iota(jnp.int32, tall, 0)
    column = lax.broadcasted_iota(jnp.int32, tall, 1)
    spread = jnp.where(row // SLOTS == column, 1.0, 0.0).astype(BF16)
    ranks = dot(spread, rank.T.astype(BF16))
    main[...] = jnp.where(ranks == (row % SLOTS).astype(F32), 1.0, 0.0).astype(BF16)
    late[...] = jnp.where(rank.T == SLOTS, 1.0, 0.0).astype(BF16)

    flat = (TOKENS, tall[0])
    hit = dot_nt(rank.astype(BF16), spread) == (
        lax.broadcasted_iota(jnp.int32, flat, 1) % SLOTS
    ).astype(F32)
    for half, part in enumerate((high, low)):
        rows = slice(half * TOKENS, (half + 1) * TOKENS)
        back_main[rows, :] = jnp.where(hit, dot_nt(part, spread), 0.0).astype(BF16)
        back_late[rows, :] = jnp.where(rank == SLOTS, part.astype(F32), 0.0).astype(BF16)


def routes(expert_ids, route_weights, n_experts):
    outs = [
        jax.ShapeDtypeStruct(shape, BF16)
        for shape in (
            (n_experts * SLOTS, TOKENS),
            (n_experts, TOKENS),
            (2 * TOKENS, n_experts * SLOTS),
            (2 * TOKENS, n_experts),
        )
    ]
    return call(
        routes_kernel,
        "routes",
        outs,
        [whole(expert_ids), whole(route_weights)],
        [pl.BlockSpec(out.shape, lambda: (0, 0)) for out in outs],
        cost=pl.CostEstimate(flops=2 * 10**8, bytes_accessed=10**6, transcendentals=0),
    )(expert_ids, route_weights)


def local(
    queries,
    key_rows,
    value_rows,
    span_order,
    out_proj,
    residual,
    norm_gain,
    expert_ids,
    route_weights,
    w_up,
    w_down,
):
    n_devices = lax.axis_size("dp") * lax.axis_size("ctx") * lax.axis_size("tp")
    core = lax.axis_index("dp") % 2
    ctx = lax.axis_index("ctx")
    x, z = lax.axis_index("tp") // SIDE, lax.axis_index("tp") % SIDE
    meta = jnp.concatenate([span_order, jnp.stack([ctx, x, z, core]).astype(jnp.int32)])

    def head_block(step):
        start = (x + step) % SIDE * HD
        return jnp.concatenate(
            [
                lax.dynamic_slice_in_dim(key_rows, start, HD, 1),
                lax.dynamic_slice_in_dim(value_rows, start, HD, 1),
            ],
            axis=1,
        )

    width = out_proj.shape[1]
    quarter = width // 4

    def weights_part(base):
        return lax.dynamic_slice_in_dim(out_proj, base + core * quarter, quarter, 1)

    def after(value, *others):
        return lax.optimization_barrier((value, *others))[0]

    own = jnp.stack(exchange(shift_x, [head_block(step) for step in range(SIDE)]))
    other = swap_ctx(own)
    before_own, after_own = shift_z(own, 1), shift_z(own, -1)
    before_other, after_other = shift_z(other, 1), shift_z(other, -1)
    far_own = shift_z(before_own, 1)
    far_other = shift_z(after_other, -1)
    weights_x = gather_rows_of(shift_x, after(weights_part(0), own))
    weights_z = gather_rows_of(shift_z, after(weights_part(width // 2), far_own, far_other))
    pieces = [
        own,
        other,
        before_own,
        before_other,
        after_own,
        after_other,
        far_own,
        far_other,
    ]

    main, late, back_main, back_late = routes(expert_ids, route_weights, n_devices)
    queries = after(queries, main)

    *far, keys, values = attention(meta, queries, pieces)
    mine, *parts, weights_x, weights_z = attention_end(
        meta, queries, keys, values, far, [*weights_x, *weights_z]
    )
    context_x = exchange(shift_x, [mine, *far])
    other_x = swap_core(after(weights_x, *context_x[1:]))
    context_z = exchange(shift_z, [after(part, *context_x) for part in parts])
    terms_z = projection(6, meta, context_x, [weights_x, other_x])
    terms_z = [after(term, *context_z[1:]) for term in terms_z]
    weights_z = after(weights_z, *terms_z)
    terms_x = projection(5, meta, context_z, [weights_z, swap_core(weights_z)])
    terms_z, terms_x = exchange(shift_z, terms_z), exchange(shift_x, terms_x)
    outgoing, state = dispatch(
        meta, terms_x, settle(meta, terms_z, residual), residual, norm_gain[None, :], main, late
    )

    def all_to_all(rows):
        blocks = rows.reshape(n_devices, SLOTS, rows.shape[1])
        return lax.all_to_all(
            blocks, ("dp", "ctx", "tp"), split_axis=0, concat_axis=0, tiled=True
        ).reshape(rows.shape)

    arrived = all_to_all(outgoing)
    returned = all_to_all(experts(arrived, w_up, w_down))
    return combine(back_main, back_late, returned, state)


def solution(mesh):
    return jax.shard_map(
        local,
        mesh=mesh,
        in_specs=(
            P(("dp", "ctx"), "tp"),
            P(("dp", "ctx", "tp"), None),
            P(("dp", "ctx", "tp"), None),
            P(),
            P("tp", None),
            P(("dp", "ctx", "tp"), None),
            P(),
            P(("dp", "ctx", "tp"), None),
            P(("dp", "ctx", "tp"), None),
            P(("dp", "ctx", "tp"), None, None),
            P(("dp", "ctx", "tp"), None, None),
        ),
        out_specs=P(("dp", "ctx", "tp"), None),
        check_vma=False,
    )
```

```python
import functools
import math

import jax
import jax.numpy as jnp
from jax import lax
from jax.experimental import pallas as pl
from jax.experimental.pallas import tpu as pltpu
from jax.sharding import PartitionSpec as P

HD = 128
KVH = 4
SIDE = 4
TOKENS = 128
SLOTS = 8
SEG = 512
ROWS = 256
COMBINE_ROWS = 512
DISPATCH_COLUMNS = 512
DOWN_COLUMNS = 512
COMBINE_COLUMNS = 512
BLOCK = 512
NEGATIVE = -1e30
MIB = 1 << 20
F32 = jnp.float32
BF16 = jnp.bfloat16


def shift_x(value, step):
    return lax.ppermute(
        value,
        "tp",
        [(x * SIDE + z, (x + step) % SIDE * SIDE + z) for x in range(SIDE) for z in range(SIDE)],
    )


def shift_z(value, step):
    return lax.ppermute(
        value,
        "tp",
        [(x * SIDE + z, x * SIDE + (z + step) % SIDE) for x in range(SIDE) for z in range(SIDE)],
    )


def swap_ctx(value):
    return lax.ppermute(value, "ctx", [(0, 1), (1, 0)])


def swap_core(value):
    return lax.ppermute(value, "dp", [(0, 1), (1, 0), (2, 3), (3, 2)])


def gather_rows_of(shift, rows):
    return [rows, shift(rows, 1), shift(rows, 2), shift(rows, -1)]


def exchange(shift, blocks):
    return [blocks[0], shift(blocks[1], 1), shift(blocks[2], 2), shift(blocks[3], -1)]


def call(kernel, name, out_shape, in_specs, out_specs, grid=(), scratch=(), limit=56, cost=None):
    return pl.pallas_call(
        kernel,
        name=name,
        out_shape=out_shape,
        grid=grid,
        in_specs=in_specs,
        out_specs=out_specs,
        scratch_shapes=list(scratch),
        compiler_params=pltpu.CompilerParams(vmem_limit_bytes=limit * MIB),
        cost_estimate=cost,
    )


def smem():
    return pl.BlockSpec(memory_space=pltpu.SMEM)


def vmem():
    return pl.BlockSpec(memory_space=pltpu.VMEM)


def whole(array):
    zeros = (0,) * array.ndim
    return pl.BlockSpec(array.shape, lambda *_: zeros, pipeline_mode=pl.Buffered(1))


def dot(left, right):
    return jnp.dot(left, right, preferred_element_type=F32)


def dot_nt(left, right):
    return lax.dot_general(left, right, (((1,), (1,)), ((), ())), preferred_element_type=F32)


def rows_of(chunk):
    return pl.ds(pl.multiple_of(chunk * BLOCK, BLOCK), BLOCK)


def attend(meta, chunk, q_ref, keys, values, scratch):
    sums, peaks, totals, even, odd = scratch[0], scratch[1], scratch[2], scratch[3:5], scratch[5:7]
    factor = math.log2(math.e) / math.sqrt(HD)
    mine = meta[meta[4] * 2 + chunk // 2] * 2 + lax.rem(chunk, 2)
    heads = [q_ref[rows_of(chunk), head * HD : (head + 1) * HD] for head in range(2)]
    for head in range(2):
        sums[head] = jnp.zeros((HD, BLOCK), F32)
        peaks[head] = jnp.full((1, BLOCK), NEGATIVE, F32)
        totals[head] = jnp.zeros((1, BLOCK), F32)

    def score(number, held):
        key_block = keys[rows_of(number), :]
        for head in range(2):
            held[head][...] = dot_nt(key_block, heads[head])

    def process(number, held, masked):
        value_block = values[:, rows_of(number)]
        for head in range(2):
            scores = held[head][...]
            if masked:
                seen = lax.broadcasted_iota(
                    jnp.int32, (BLOCK, BLOCK), 0
                ) <= lax.broadcasted_iota(jnp.int32, (BLOCK, BLOCK), 1)
                scores = jnp.where(seen, scores, NEGATIVE)
            peak = peaks[head]
            new_peak = jnp.maximum(peak, jnp.max(scores, axis=0, keepdims=True))
            weights = jnp.exp2(scores * factor - new_peak * factor)
            fading = jnp.exp2((peak - new_peak) * factor)
            peaks[head] = new_peak
            totals[head] = totals[head] * fading + jnp.sum(weights, axis=0, keepdims=True)
            sums[head] = sums[head] * fading + dot(value_block, weights.astype(BF16))

    score(0, even)

    def two(pair, carry):
        score(2 * pair + 1, odd)
        process(2 * pair, even, False)
        score(2 * pair + 2, even)
        process(2 * pair + 1, odd, False)
        return carry

    lax.fori_loop(0, mine // 2, two, 0)

    @pl.when(lax.rem(mine, 2) == 1)
    def _():
        score(mine, odd)
        process(mine - 1, even, False)
        process(mine, odd, True)

    @pl.when(lax.rem(mine, 2) == 0)
    def _():
        process(mine, even, True)

    return jnp.concatenate(
        [(sums[head] / totals[head]).T.astype(BF16) for head in range(2)], axis=1
    )


def attend_scratch():
    return [
        pltpu.VMEM((2, HD, BLOCK), F32),
        pltpu.VMEM((2, 1, BLOCK), F32),
        pltpu.VMEM((2, 1, BLOCK), F32),
    ] + [pltpu.VMEM((BLOCK, BLOCK), F32)] * 4


def attention_kernel(meta, q_ref, *refs):
    pieces, refs = refs[:8], refs[8:]
    outs, keys, values, context, scratch = refs[:3], *refs[3:6], refs[6:]
    ctx, x, z = meta[4], meta[5], meta[6]

    for number, piece in enumerate(pieces):
        part = lax.rem(ctx + number % 2, 2)
        back = (0, 1, 3, 2)[number // 2]
        z_of = lax.rem(z + SIDE - back, SIDE)
        for block in range(SIDE):
            x_of = lax.rem(x + SIDE - block, SIDE)
            place = meta[part * 2 + x_of // 2] * 8 + lax.rem(x_of, 2) * SIDE + z_of
            rows = pl.ds(pl.multiple_of(place * HD, HD), HD)
            keys[rows, :] = piece[block, :, :HD]
            values[:, rows] = piece[block, :, HD:].T

    @pl.loop(0, SIDE - 1)
    def _(number):
        chunk = lax.rem(x + 1 + number, SIDE)
        context[number] = attend(meta, chunk, q_ref, keys, values, scratch)

    for number, out in enumerate(outs):
        out[...] = context[number]


def attention(meta, queries, pieces):
    rows, width = queries.shape
    arrays = (queries, *pieces)
    outs = [jax.ShapeDtypeStruct((BLOCK, width), BF16)] * 3 + [
        jax.ShapeDtypeStruct((2 * rows, HD), BF16),
        jax.ShapeDtypeStruct((HD, 2 * rows), BF16),
    ]
    return call(
        attention_kernel,
        "attention",
        outs,
        [smem()] + [whole(array) for array in arrays],
        [pl.BlockSpec(out.shape, lambda: (0, 0)) for out in outs],
        scratch=[pltpu.VMEM((3, BLOCK, width), BF16), *attend_scratch()],
        cost=pl.CostEstimate(
            flops=16 * 10**9, bytes_accessed=7 * 10**6, transcendentals=10 * 10**6
        ),
    )(meta, *arrays)


def attention_end_kernel(meta, q_ref, keys, values, *refs):
    others, weights, out, refs = refs[:3], refs[3:11], refs[11], refs[12:]
    outs_z, joined, held, came, went, scratch = refs[:4], refs[4:6], *refs[6:9], refs[9:]
    x, z = meta[5], meta[6]
    depth = weights[0].shape[0]
    arriving = [
        pltpu.make_async_copy(
            piece,
            held.at[number // SIDE, pl.ds(number % SIDE * depth, depth), :],
            came.at[number],
        )
        for number, piece in enumerate(weights)
    ]
    leaving = [
        pltpu.make_async_copy(held.at[number], whole_of, went.at[number])
        for number, whole_of in enumerate(joined)
    ]
    for copy in arriving:
        copy.start()
    out[...] = attend(meta, x, q_ref, keys, values, scratch)
    for copy in arriving:
        copy.wait()
    for copy in leaving:
        copy.start()
    for number, context in enumerate((out, *others)):
        x_of = lax.rem(x + number, SIDE)
        rows = pl.ds(pl.multiple_of(x_of * TOKENS, TOKENS), TOKENS)
        for step_of in range(SIDE):
            to_z = lax.rem(z + step_of, SIDE)
            part = pl.ds(pl.multiple_of(to_z * TOKENS, TOKENS), TOKENS)
            outs_z[step_of][rows, :] = context[part, :]
    for copy in leaving:
        copy.wait()


def attention_end(meta, queries, keys, values, others, weights):
    width = queries.shape[1]
    arrays = (queries, keys, values, *others)
    depth, columns = weights[0].shape
    outs = [jax.ShapeDtypeStruct((BLOCK, width), BF16)] * 5
    joined = [jax.ShapeDtypeStruct((SIDE * depth, columns), BF16)] * 2
    anywhere = pl.BlockSpec(memory_space=pl.ANY)
    return call(
        attention_end_kernel,
        "attention_end",
        outs + joined,
        [smem()] + [whole(array) for array in arrays] + [anywhere] * len(weights),
        [pl.BlockSpec(out.shape, lambda: (0, 0)) for out in outs] + [anywhere] * 2,
        scratch=[
            pltpu.VMEM((2, SIDE * depth, columns), BF16),
            pltpu.SemaphoreType.DMA((2 * SIDE,)),
            pltpu.SemaphoreType.DMA((2,)),
            *attend_scratch(),
        ],
        cost=pl.CostEstimate(
            flops=6 * 10**9, bytes_accessed=7 * 10**6, transcendentals=3 * 10**6
        ),
    )(meta, *arrays, *weights)


def projection_kernel(axis, meta, *refs):
    context, weights, outs, held = refs[:4], refs[4:6], refs[6:10], refs[10]
    step, me = pl.program_id(0), meta[axis]
    width = context[0].shape[1]
    columns = weights[0].shape[1]
    steps = held.shape[1] // (2 * columns)
    for side, weight in enumerate(weights):
        total = None
        for number, rows in enumerate(context):
            term = dot(rows[...], weight[number * width : (number + 1) * width, :])
            total = term if total is None else total + term
        start = pl.multiple_of((side * steps + step) * columns, columns)
        held[:, pl.ds(start, columns)] = total.astype(BF16)

    @pl.when(step == steps - 1)
    def _():
        for number, out in enumerate(outs):
            to = lax.rem(me + number, SIDE)
            out[...] = held[pl.ds(pl.multiple_of(to * TOKENS, TOKENS), TOKENS), :]


def projection(axis, meta, context, weights):
    depth, columns = weights[0].shape
    part = columns // 4
    return call(
        functools.partial(projection_kernel, axis),
        "projection",
        [jax.ShapeDtypeStruct((TOKENS, 2 * columns), BF16)] * 4,
        [smem()]
        + [whole(array) for array in context]
        + [pl.BlockSpec((depth, part), lambda i: (0, i))] * 2,
        [pl.BlockSpec((TOKENS, 2 * columns), lambda i: (0, 0))] * 4,
        grid=(4,),
        scratch=[pltpu.VMEM((SIDE * TOKENS, 2 * columns), BF16)],
        cost=pl.CostEstimate(
            flops=4 * 512 * 1024 * columns, bytes_accessed=7 * 10**6, transcendentals=0
        ),
    )(meta, *context, *weights)


def wide_scratch():
    return pltpu.VMEM((SEG // HD, TOKENS * SLOTS, HD), F32)


def widen(wide, rows_ref):
    for part in range(SEG // HD):
        wide[part] = rows_ref[:, part * HD : (part + 1) * HD].astype(F32)


def narrow(wide):
    return jnp.concatenate([wide[part].astype(BF16) for part in range(SEG // HD)], axis=1)


def gather_rows(wide, segment):
    rows = pl.ds(segment, TOKENS, stride=SLOTS)
    return jnp.concatenate([wide[part, rows, :] for part in range(SEG // HD)], axis=1).astype(BF16)


def scatter_rows(wide, segment, value):
    rows = pl.ds(segment, TOKENS, stride=SLOTS)
    for part in range(SEG // HD):
        wide[part, rows, :] = value[:, part * HD : (part + 1) * HD]


def add_terms(core, terms, residual, state, base):
    quarter = terms[0].shape[1] // 2
    for side in range(2):
        place = base + quarter * lax.rem(core + side, 2)
        columns = pl.ds(pl.multiple_of(place, quarter), quarter)
        part = slice(side * quarter, (side + 1) * quarter)
        total = terms[0][:, part].astype(F32)
        for term in terms[1:]:
            total = total + term[:, part].astype(F32)
        state[:, columns] = residual[:, columns].astype(F32) + total


def settle_kernel(meta, *refs):
    terms, (residual, state) = refs[:4], refs[4:]
    add_terms(meta[7], terms, residual, state, 0)


def settle(meta, terms, residual):
    half = terms[0].shape[1]
    return call(
        settle_kernel,
        "settle",
        jax.ShapeDtypeStruct((TOKENS, half), F32),
        [smem()]
        + [whole(term) for term in terms]
        + [pl.BlockSpec((TOKENS, half), lambda i: (0, 0))],
        pl.BlockSpec((TOKENS, half), lambda i: (0, 0)),
        grid=(1,),
        cost=pl.CostEstimate(flops=2 * 10**10, bytes_accessed=4 * 10**6, transcendentals=0),
    )(meta, *terms, residual)


def dispatch_kernel(meta, *refs):
    terms, refs = refs[:4], refs[4:]
    first, residual, gain, main, late, outgoing, state, normed, wide, spread = refs
    step = pl.program_id(0)
    half = first.shape[1]

    @pl.when(step == 0)
    def _():
        state[:, :half] = first[...]
        add_terms(meta[7], terms, residual, state, half)
        value = state[...]
        scale = lax.rsqrt(jnp.mean(value * value, axis=1, keepdims=True) + 1e-06)
        for segment in range(SLOTS):
            columns = slice(segment * SEG, (segment + 1) * SEG)
            normed[:, columns] = (state[:, columns] * scale * gain[:, columns]).astype(BF16)

        for segment in range(SLOTS):
            columns = slice(segment * SEG, (segment + 1) * SEG)
            scatter_rows(wide, segment, dot(late[...], normed[:, columns]))
        spread[...] = narrow(wide)

    for start in range(0, 2 * half, DISPATCH_COLUMNS):
        columns = slice(start, start + DISPATCH_COLUMNS)
        outgoing[:, columns] = dot(main[...], normed[:, columns]).astype(BF16)
    rows = outgoing.shape[0]
    outgoing[:, 2 * half :] = spread[pl.ds(pl.multiple_of(step * rows, rows), rows), :]


def dispatch(meta, terms, first, residual, gain, main, late):
    rows, width = main.shape[0], residual.shape[1]
    arrays = (*terms, first, residual, gain)
    return call(
        dispatch_kernel,
        "dispatch",
        [
            jax.ShapeDtypeStruct((rows, width + SEG), BF16),
            jax.ShapeDtypeStruct((TOKENS, width), F32),
        ],
        [smem()]
        + [whole(a) for a in arrays]
        + [pl.BlockSpec((ROWS, TOKENS), lambda i: (i, 0)), whole(late)],
        [
            pl.BlockSpec((ROWS, width + SEG), lambda i: (i, 0)),
            pl.BlockSpec((TOKENS, width), lambda i: (0, 0)),
        ],
        grid=(rows // ROWS,),
        scratch=[
            pltpu.VMEM((TOKENS, width), BF16),
            wide_scratch(),
            pltpu.VMEM((rows, SEG), BF16),
        ],
        cost=pl.CostEstimate(flops=3 * 10**9, bytes_accessed=16 * 10**6, transcendentals=0),
    )(meta, *arrays, main, late)


def expert_kernel(rows_ref, over_ref, up_ref, down_hbm, out_ref, wide, spread, down_ref, mixed, done):
    step = pl.program_id(0)
    width = down_ref.shape[2]
    fetch = pltpu.make_async_copy(down_hbm, down_ref, done)

    def act(value):
        return (value / (1.0 + jnp.exp(-value))).astype(BF16)

    first = step == 0

    @pl.when(first)
    def _():
        fetch.start()
        widen(wide, over_ref)
        for segment in range(SLOTS):
            columns = slice(segment * SEG, (segment + 1) * SEG)
            mixed[:ROWS, columns] = rows_ref[:, columns]
            mixed[ROWS:, columns] = gather_rows(wide, segment)
        inner = act(dot(mixed[...], up_ref[0]))
        fetch.wait()
        for segment in range(SLOTS):
            columns = slice(segment * SEG, (segment + 1) * SEG)
            made = dot(inner, down_ref[0, :, columns])
            out_ref[:, columns] = made[:ROWS].astype(BF16)
            scatter_rows(wide, segment, made[ROWS:])
        spread[...] = narrow(wide)

    @pl.when(jnp.logical_not(first))
    def _():
        inner = act(dot(rows_ref[:, :width], up_ref[0]))
        for start in range(0, width, DOWN_COLUMNS):
            columns = slice(start, start + DOWN_COLUMNS)
            out_ref[:, columns] = dot(inner, down_ref[0, :, columns]).astype(BF16)

    mine = pl.ds(pl.multiple_of(step * ROWS, ROWS), ROWS)
    out_ref[:, width:] = spread[mine, :]


def experts(arrived, up, down):
    rows, columns = arrived.shape
    inner = up.shape[2]
    return call(
        expert_kernel,
        "experts",
        jax.ShapeDtypeStruct((rows, columns), BF16),
        [
            pl.BlockSpec((ROWS, columns), lambda i: (i, 0)),
            pl.BlockSpec((rows, SEG), lambda i: (0, SLOTS)),
            vmem(),
            pl.BlockSpec(memory_space=pl.ANY),
        ],
        pl.BlockSpec((ROWS, columns), lambda i: (i, 0)),
        grid=(rows // ROWS,),
        scratch=[
            wide_scratch(),
            pltpu.VMEM((rows, SEG), BF16),
            pltpu.VMEM(down.shape, BF16),
            pltpu.VMEM((ROWS + TOKENS, down.shape[2]), BF16),
            pltpu.SemaphoreType.DMA,
        ],
        limit=46,
        cost=pl.CostEstimate(
            flops=4 * rows * columns * inner,
            bytes_accessed=32 * 10**6,
            transcendentals=rows * inner,
        ),
    )(arrived, arrived, up, down)


def combine_kernel(main, late, rows_ref, over_ref, state, out, total, wide):
    step = pl.program_id(0)
    segments = [(i, slice(i * SEG, (i + 1) * SEG)) for i in range(SLOTS)]

    def both(value):
        return value[:TOKENS] + value[TOKENS:]

    @pl.when(step == 0)
    def _():
        widen(wide, over_ref)
        for segment, columns in segments:
            late_part = both(dot(late[...], gather_rows(wide, segment)))
            total[:, columns] = state[:, columns] + late_part

    for start in range(0, total.shape[1], COMBINE_COLUMNS):
        columns = slice(start, start + COMBINE_COLUMNS)
        total[:, columns] += both(dot(main[...], rows_ref[:, columns]))

    @pl.when(step == pl.num_programs(0) - 1)
    def _():
        out[...] = total[...].astype(BF16)


def combine(main, late, returned, state):
    rows, columns = returned.shape
    return call(
        combine_kernel,
        "combine",
        jax.ShapeDtypeStruct(state.shape, BF16),
        [
            pl.BlockSpec((2 * TOKENS, COMBINE_ROWS), lambda i: (0, i)),
            whole(late),
            pl.BlockSpec((COMBINE_ROWS, columns), lambda i: (i, 0)),
            pl.BlockSpec((rows, SEG), lambda i: (0, SLOTS), pipeline_mode=pl.Buffered(1)),
            whole(state),
        ],
        pl.BlockSpec(state.shape, lambda i: (0, 0)),
        grid=(rows // COMBINE_ROWS,),
        scratch=[pltpu.VMEM(state.shape, F32), wide_scratch()],
        cost=pl.CostEstimate(flops=4 * 10**9, bytes_accessed=13 * 10**6, transcendentals=0),
    )(main, late, returned, returned, state)


def routes_kernel(ids, weights, main, late, back_main, back_late):
    square = (TOKENS, TOKENS)
    row = lax.broadcasted_iota(jnp.int32, square, 0)
    column = lax.broadcasted_iota(jnp.int32, square, 1)
    named, weight = jnp.zeros(square, F32), jnp.zeros(square, F32)
    for choice in range(ids.shape[1]):
        chosen = column == ids[:, choice : choice + 1]
        named = named + jnp.where(chosen, 1.0, 0.0)
        weight = weight + jnp.where(chosen, weights[:, choice : choice + 1], 0.0)
    earlier = jnp.where(column < row, 1.0, 0.0).astype(BF16)
    rank = jnp.where(named > 0.0, dot(earlier, named.astype(BF16)), -1.0)
    high = weight.astype(BF16)
    low = (weight - high.astype(F32)).astype(BF16)

    tall = main.shape
    row = lax.broadcasted_iota(jnp.int32, tall, 0)
    column = lax.broadcasted_iota(jnp.int32, tall, 1)
    spread = jnp.where(row // SLOTS == column, 1.0, 0.0).astype(BF16)
    ranks = dot(spread, rank.T.astype(BF16))
    main[...] = jnp.where(ranks == (row % SLOTS).astype(F32), 1.0, 0.0).astype(BF16)
    late[...] = jnp.where(rank.T == SLOTS, 1.0, 0.0).astype(BF16)

    flat = (TOKENS, tall[0])
    hit = dot_nt(rank.astype(BF16), spread) == (
        lax.broadcasted_iota(jnp.int32, flat, 1) % SLOTS
    ).astype(F32)
    for half, part in enumerate((high, low)):
        rows = slice(half * TOKENS, (half + 1) * TOKENS)
        back_main[rows, :] = jnp.where(hit, dot_nt(part, spread), 0.0).astype(BF16)
        back_late[rows, :] = jnp.where(rank == SLOTS, part.astype(F32), 0.0).astype(BF16)


def routes(expert_ids, route_weights, n_experts):
    outs = [
        jax.ShapeDtypeStruct(shape, BF16)
        for shape in (
            (n_experts * SLOTS, TOKENS),
            (n_experts, TOKENS),
            (2 * TOKENS, n_experts * SLOTS),
            (2 * TOKENS, n_experts),
        )
    ]
    return call(
        routes_kernel,
        "routes",
        outs,
        [whole(expert_ids), whole(route_weights)],
        [pl.BlockSpec(out.shape, lambda: (0, 0)) for out in outs],
        cost=pl.CostEstimate(flops=2 * 10**8, bytes_accessed=10**6, transcendentals=0),
    )(expert_ids, route_weights)


def local(
    queries,
    key_rows,
    value_rows,
    span_order,
    out_proj,
    residual,
    norm_gain,
    expert_ids,
    route_weights,
    w_up,
    w_down,
):
    n_devices = lax.axis_size("dp") * lax.axis_size("ctx") * lax.axis_size("tp")
    core = lax.axis_index("dp") % 2
    ctx = lax.axis_index("ctx")
    x, z = lax.axis_index("tp") // SIDE, lax.axis_index("tp") % SIDE
    meta = jnp.concatenate([span_order, jnp.stack([ctx, x, z, core]).astype(jnp.int32)])

    def head_block(step):
        start = (x + step) % SIDE * HD
        return jnp.concatenate(
            [
                lax.dynamic_slice_in_dim(key_rows, start, HD, 1),
                lax.dynamic_slice_in_dim(value_rows, start, HD, 1),
            ],
            axis=1,
        )

    width = out_proj.shape[1]
    quarter = width // 4

    def weights_part(base):
        return lax.dynamic_slice_in_dim(out_proj, base + core * quarter, quarter, 1)

    def after(value, *others):
        return lax.optimization_barrier((value, *others))[0]

    own = jnp.stack(exchange(shift_x, [head_block(step) for step in range(SIDE)]))
    other = swap_ctx(own)
    before_own, after_own = shift_z(own, 1), shift_z(own, -1)
    before_other, after_other = shift_z(other, 1), shift_z(other, -1)
    far_own = shift_z(before_own, 1)
    far_other = shift_z(after_other, -1)
    weights_x = gather_rows_of(shift_x, after(weights_part(0), own))
    weights_z = gather_rows_of(shift_z, after(weights_part(width // 2), far_own, far_other))
    pieces = [
        own,
        other,
        before_own,
        before_other,
        after_own,
        after_other,
        far_own,
        far_other,
    ]


    *far, keys, values = attention(meta, queries, pieces)
    mine, *parts, weights_x, weights_z = attention_end(
        meta, queries, keys, values, far, [*weights_x, *weights_z]
    )
    context_x = exchange(shift_x, [mine, *far])
    other_x = swap_core(after(weights_x, *context_x[1:]))
    context_z = exchange(shift_z, [after(part, *context_x) for part in parts])
    terms_z = projection(6, meta, context_x, [weights_x, other_x])
    terms_z = [after(term, *context_z[1:]) for term in terms_z]
    weights_z = after(weights_z, *terms_z)
    terms_x = projection(5, meta, context_z, [weights_z, swap_core(weights_z)])
    main, late, back_main, back_late = routes(
        after(expert_ids, terms_x[0]), route_weights, n_devices
    )
    terms_z, terms_x = exchange(shift_z, terms_z), exchange(shift_x, terms_x)
    outgoing, state = dispatch(
        meta, terms_x, settle(meta, terms_z, residual), residual, norm_gain[None, :], main, late
    )

    def all_to_all(rows):
        blocks = rows.reshape(n_devices, SLOTS, rows.shape[1])
        return lax.all_to_all(
            blocks, ("dp", "ctx", "tp"), split_axis=0, concat_axis=0, tiled=True
        ).reshape(rows.shape)

    arrived = all_to_all(outgoing)
    returned = all_to_all(experts(arrived, w_up, w_down))
    return combine(back_main, back_late, returned, state)


def solution(mesh):
    return jax.shard_map(
        local,
        mesh=mesh,
        in_specs=(
            P(("dp", "ctx"), "tp"),
            P(("dp", "ctx", "tp"), None),
            P(("dp", "ctx", "tp"), None),
            P(),
            P("tp", None),
            P(("dp", "ctx", "tp"), None),
            P(),
            P(("dp", "ctx", "tp"), None),
            P(("dp", "ctx", "tp"), None),
            P(("dp", "ctx", "tp"), None, None),
            P(("dp", "ctx", "tp"), None, None),
        ),
        out_specs=P(("dp", "ctx", "tp"), None),
        check_vma=False,
    )
```

```python
import functools
import math

import jax
import jax.numpy as jnp
from jax import lax
from jax.experimental import pallas as pl
from jax.experimental.pallas import tpu as pltpu
from jax.sharding import PartitionSpec as P

HD = 128
KVH = 4
SIDE = 4
TOKENS = 128
SLOTS = 8
SEG = 512
ROWS = 256
COMBINE_ROWS = 512
DOWN_COLUMNS = 512
COMBINE_COLUMNS = 512
BLOCK = 512
NEGATIVE = -1e30
MIB = 1 << 20
F32 = jnp.float32
BF16 = jnp.bfloat16


def shift_x(value, step):
    return lax.ppermute(
        value,
        "tp",
        [(x * SIDE + z, (x + step) % SIDE * SIDE + z) for x in range(SIDE) for z in range(SIDE)],
    )


def shift_z(value, step):
    return lax.ppermute(
        value,
        "tp",
        [(x * SIDE + z, x * SIDE + (z + step) % SIDE) for x in range(SIDE) for z in range(SIDE)],
    )


def swap_ctx(value):
    return lax.ppermute(value, "ctx", [(0, 1), (1, 0)])


def swap_core(value):
    return lax.ppermute(value, "dp", [(0, 1), (1, 0), (2, 3), (3, 2)])


def gather_rows_of(shift, rows):
    return [rows, shift(rows, 1), shift(rows, 2), shift(rows, -1)]


def exchange(shift, blocks):
    return [blocks[0], shift(blocks[1], 1), shift(blocks[2], 2), shift(blocks[3], -1)]


def call(kernel, name, out_shape, in_specs, out_specs, grid=(), scratch=(), limit=56, cost=None):
    return pl.pallas_call(
        kernel,
        name=name,
        out_shape=out_shape,
        grid=grid,
        in_specs=in_specs,
        out_specs=out_specs,
        scratch_shapes=list(scratch),
        compiler_params=pltpu.CompilerParams(vmem_limit_bytes=limit * MIB),
        cost_estimate=cost,
    )


def smem():
    return pl.BlockSpec(memory_space=pltpu.SMEM)


def vmem():
    return pl.BlockSpec(memory_space=pltpu.VMEM)


def whole(array):
    zeros = (0,) * array.ndim
    return pl.BlockSpec(array.shape, lambda *_: zeros, pipeline_mode=pl.Buffered(1))


def dot(left, right):
    return jnp.dot(left, right, preferred_element_type=F32)


def dot_nt(left, right):
    return lax.dot_general(left, right, (((1,), (1,)), ((), ())), preferred_element_type=F32)


def rows_of(chunk):
    return pl.ds(pl.multiple_of(chunk * BLOCK, BLOCK), BLOCK)


def attend(meta, chunk, q_ref, keys, values, scratch):
    sums, peaks, totals, even, odd = scratch[0], scratch[1], scratch[2], scratch[3:5], scratch[5:7]
    factor = math.log2(math.e) / math.sqrt(HD)
    mine = meta[meta[4] * 2 + chunk // 2] * 2 + lax.rem(chunk, 2)
    heads = [q_ref[rows_of(chunk), head * HD : (head + 1) * HD] for head in range(2)]
    for head in range(2):
        sums[head] = jnp.zeros((HD, BLOCK), F32)
        peaks[head] = jnp.full((1, BLOCK), NEGATIVE, F32)
        totals[head] = jnp.zeros((1, BLOCK), F32)

    def score(number, held):
        key_block = keys[rows_of(number), :]
        for head in range(2):
            held[head][...] = dot_nt(key_block, heads[head])

    def process(number, held, masked):
        value_block = values[:, rows_of(number)]
        for head in range(2):
            scores = held[head][...]
            if masked:
                seen = lax.broadcasted_iota(
                    jnp.int32, (BLOCK, BLOCK), 0
                ) <= lax.broadcasted_iota(jnp.int32, (BLOCK, BLOCK), 1)
                scores = jnp.where(seen, scores, NEGATIVE)
            peak = peaks[head]
            new_peak = jnp.maximum(peak, jnp.max(scores, axis=0, keepdims=True))
            weights = jnp.exp2(scores * factor - new_peak * factor)
            fading = jnp.exp2((peak - new_peak) * factor)
            peaks[head] = new_peak
            totals[head] = totals[head] * fading + jnp.sum(weights, axis=0, keepdims=True)
            sums[head] = sums[head] * fading + dot(value_block, weights.astype(BF16))

    score(0, even)

    def two(pair, carry):
        score(2 * pair + 1, odd)
        process(2 * pair, even, False)
        score(2 * pair + 2, even)
        process(2 * pair + 1, odd, False)
        return carry

    lax.fori_loop(0, mine // 2, two, 0)

    @pl.when(lax.rem(mine, 2) == 1)
    def _():
        score(mine, odd)
        process(mine - 1, even, False)
        process(mine, odd, True)

    @pl.when(lax.rem(mine, 2) == 0)
    def _():
        process(mine, even, True)

    return jnp.concatenate(
        [(sums[head] / totals[head]).T.astype(BF16) for head in range(2)], axis=1
    )


def attend_scratch():
    return [
        pltpu.VMEM((2, HD, BLOCK), F32),
        pltpu.VMEM((2, 1, BLOCK), F32),
        pltpu.VMEM((2, 1, BLOCK), F32),
    ] + [pltpu.VMEM((BLOCK, BLOCK), F32)] * 4


def attention_kernel(meta, q_ref, *refs):
    pieces, refs = refs[:8], refs[8:]
    outs, keys, values, context, scratch = refs[:3], *refs[3:6], refs[6:]
    ctx, x, z = meta[4], meta[5], meta[6]

    for number, piece in enumerate(pieces):
        part = lax.rem(ctx + number % 2, 2)
        back = (0, 1, 3, 2)[number // 2]
        z_of = lax.rem(z + SIDE - back, SIDE)
        for block in range(SIDE):
            x_of = lax.rem(x + SIDE - block, SIDE)
            place = meta[part * 2 + x_of // 2] * 8 + lax.rem(x_of, 2) * SIDE + z_of
            rows = pl.ds(pl.multiple_of(place * HD, HD), HD)
            keys[rows, :] = piece[block, :, :HD]
            values[:, rows] = piece[block, :, HD:].T

    @pl.loop(0, SIDE - 1)
    def _(number):
        chunk = lax.rem(x + 1 + number, SIDE)
        context[number] = attend(meta, chunk, q_ref, keys, values, scratch)

    for number, out in enumerate(outs):
        out[...] = context[number]


def attention(meta, queries, pieces):
    rows, width = queries.shape
    arrays = (queries, *pieces)
    outs = [jax.ShapeDtypeStruct((BLOCK, width), BF16)] * 3 + [
        jax.ShapeDtypeStruct((2 * rows, HD), BF16),
        jax.ShapeDtypeStruct((HD, 2 * rows), BF16),
    ]
    return call(
        attention_kernel,
        "attention",
        outs,
        [smem()] + [whole(array) for array in arrays],
        [pl.BlockSpec(out.shape, lambda: (0, 0)) for out in outs],
        scratch=[pltpu.VMEM((3, BLOCK, width), BF16), *attend_scratch()],
        cost=pl.CostEstimate(
            flops=16 * 10**9, bytes_accessed=7 * 10**6, transcendentals=10 * 10**6
        ),
    )(meta, *arrays)


def attention_end_kernel(meta, q_ref, keys, values, *refs):
    others, weights, out, refs = refs[:3], refs[3:11], refs[11], refs[12:]
    outs_z, joined, held, refs = refs[:4], refs[4:6], refs[6:8], refs[8:]
    came, went, scratch = refs[0], refs[1], refs[2:]
    x, z = meta[5], meta[6]
    depth = weights[0].shape[0]
    arriving = [
        pltpu.make_async_copy(
            piece,
            held[number // SIDE].at[pl.ds(number % SIDE * depth, depth), :],
            came.at[number],
        )
        for number, piece in enumerate(weights)
    ]
    leaving = [
        pltpu.make_async_copy(held[number], whole_of, went.at[number])
        for number, whole_of in enumerate(joined)
    ]
    for copy in arriving:
        copy.start()
    out[...] = attend(meta, x, q_ref, keys, values, scratch)
    for copy in arriving:
        copy.wait()
    for copy in leaving:
        copy.start()
    for number, context in enumerate((out, *others)):
        x_of = lax.rem(x + number, SIDE)
        rows = pl.ds(pl.multiple_of(x_of * TOKENS, TOKENS), TOKENS)
        for step_of in range(SIDE):
            to_z = lax.rem(z + step_of, SIDE)
            part = pl.ds(pl.multiple_of(to_z * TOKENS, TOKENS), TOKENS)
            outs_z[step_of][rows, :] = context[part, :]
    for copy in leaving:
        copy.wait()


def attention_end(meta, queries, keys, values, others, weights):
    width = queries.shape[1]
    arrays = (queries, keys, values, *others)
    outs = [jax.ShapeDtypeStruct((BLOCK, width), BF16)] * 5
    joined = [
        jax.ShapeDtypeStruct((SIDE * piece.shape[0], piece.shape[1]), BF16)
        for piece in weights[::SIDE]
    ]
    anywhere = pl.BlockSpec(memory_space=pl.ANY)
    return call(
        attention_end_kernel,
        "attention_end",
        outs + joined,
        [smem()] + [whole(array) for array in arrays] + [anywhere] * len(weights),
        [pl.BlockSpec(out.shape, lambda: (0, 0)) for out in outs] + [anywhere] * 2,
        scratch=[
            *[pltpu.VMEM(whole_of.shape, BF16) for whole_of in joined],
            pltpu.SemaphoreType.DMA((2 * SIDE,)),
            pltpu.SemaphoreType.DMA((2,)),
            *attend_scratch(),
        ],
        cost=pl.CostEstimate(
            flops=6 * 10**9, bytes_accessed=7 * 10**6, transcendentals=3 * 10**6
        ),
    )(meta, *arrays, *weights)


def projection_kernel(axis, meta, *refs):
    context, weights, outs, held = refs[:4], refs[4:6], refs[6:10], refs[10]
    step, me = pl.program_id(0), meta[axis]
    width = context[0].shape[1]
    columns = weights[0].shape[1]
    steps = held.shape[1] // (2 * columns)
    for side, weight in enumerate(weights):
        total = None
        for number, rows in enumerate(context):
            term = dot(rows[...], weight[number * width : (number + 1) * width, :])
            total = term if total is None else total + term
        start = pl.multiple_of((side * steps + step) * columns, columns)
        held[:, pl.ds(start, columns)] = total.astype(BF16)

    @pl.when(step == steps - 1)
    def _():
        for number, out in enumerate(outs):
            to = lax.rem(me + number, SIDE)
            out[...] = held[pl.ds(pl.multiple_of(to * TOKENS, TOKENS), TOKENS), :]


def projection(axis, meta, context, weights):
    depth, columns = weights[0].shape
    part = 256
    return call(
        functools.partial(projection_kernel, axis),
        "projection",
        [jax.ShapeDtypeStruct((TOKENS, 2 * columns), BF16)] * 4,
        [smem()]
        + [whole(array) for array in context]
        + [pl.BlockSpec((depth, part), lambda i: (0, i))] * 2,
        [pl.BlockSpec((TOKENS, 2 * columns), lambda i: (0, 0))] * 4,
        grid=(columns // part,),
        scratch=[pltpu.VMEM((SIDE * TOKENS, 2 * columns), BF16)],
        cost=pl.CostEstimate(
            flops=4 * 512 * 1024 * columns, bytes_accessed=7 * 10**6, transcendentals=0
        ),
    )(meta, *context, *weights)


def wide_scratch(rows=TOKENS * SLOTS):
    return pltpu.VMEM((SEG // HD, rows, HD), F32)


def widen(wide, rows_ref):
    for part in range(SEG // HD):
        wide[part] = rows_ref[:, part * HD : (part + 1) * HD].astype(F32)


def narrow(wide):
    return jnp.concatenate([wide[part].astype(BF16) for part in range(SEG // HD)], axis=1)


def gather_rows(wide, segment):
    rows = pl.ds(segment, wide.shape[1] // SLOTS, stride=SLOTS)
    return jnp.concatenate([wide[part, rows, :] for part in range(SEG // HD)], axis=1).astype(BF16)


def scatter_rows(wide, segment, value):
    rows = pl.ds(segment, value.shape[0], stride=SLOTS)
    for part in range(SEG // HD):
        wide[part, rows, :] = value[:, part * HD : (part + 1) * HD]


def add_terms(core, terms, residual, state, base):
    quarter = terms[0].shape[1] // 2
    for side in range(2):
        place = base + quarter * lax.rem(core + side, 2)
        columns = pl.ds(pl.multiple_of(place, quarter), quarter)
        part = slice(side * quarter, (side + 1) * quarter)
        total = terms[0][:, part].astype(F32)
        for term in terms[1:]:
            total = total + term[:, part].astype(F32)
        state[:, columns] = residual[:, columns].astype(F32) + total


def settle_kernel(meta, *refs):
    terms, (residual, state) = refs[:4], refs[4:]
    add_terms(meta[7], terms, residual, state, 0)


def settle(meta, terms, residual):
    half = terms[0].shape[1]
    return call(
        settle_kernel,
        "settle",
        jax.ShapeDtypeStruct((TOKENS, half), F32),
        [smem()]
        + [whole(term) for term in terms]
        + [pl.BlockSpec((TOKENS, half), lambda i: (0, 0))],
        pl.BlockSpec((TOKENS, half), lambda i: (0, 0)),
        grid=(1,),
        cost=pl.CostEstimate(flops=2 * 10**10, bytes_accessed=4 * 10**6, transcendentals=0),
    )(meta, *terms, residual)


def dispatch_kernel(meta, *refs):
    terms, refs = refs[:4], refs[4:]
    first, residual, gain, main, late, outgoing, state, normed, wide = refs
    step = pl.program_id(0)
    half = first.shape[1]

    @pl.when(step == 0)
    def _():
        state[:, :half] = first[...]
        add_terms(meta[7], terms, residual, state, half)
        value = state[...]
        scale = lax.rsqrt(jnp.mean(value * value, axis=1, keepdims=True) + 1e-06)
        for segment in range(SLOTS):
            columns = slice(segment * SEG, (segment + 1) * SEG)
            normed[:, columns] = (state[:, columns] * scale * gain[:, columns]).astype(BF16)

    rows = outgoing.shape[0]
    picks = jnp.concatenate([main[...], late[...]], axis=0)
    for segment in range(SLOTS):
        columns = slice(segment * SEG, (segment + 1) * SEG)
        picked = dot(picks, normed[:, columns])
        outgoing[:, columns] = picked[:rows].astype(BF16)
        scatter_rows(wide, segment, picked[rows:])
    outgoing[:, state.shape[1] :] = narrow(wide)


def dispatch(meta, terms, first, residual, gain, main, late):
    rows, width = main.shape[0], residual.shape[1]
    arrays = (*terms, first, residual, gain)
    return call(
        dispatch_kernel,
        "dispatch",
        [
            jax.ShapeDtypeStruct((rows, width + SEG), BF16),
            jax.ShapeDtypeStruct((TOKENS, width), F32),
        ],
        [smem()]
        + [whole(a) for a in arrays]
        + [pl.BlockSpec((count, TOKENS), lambda i: (i, 0)) for count in (ROWS, ROWS // SLOTS)],
        [
            pl.BlockSpec((ROWS, width + SEG), lambda i: (i, 0)),
            pl.BlockSpec((TOKENS, width), lambda i: (0, 0)),
        ],
        grid=(rows // ROWS,),
        scratch=[
            pltpu.VMEM((TOKENS, width), BF16),
            wide_scratch(ROWS),
        ],
        cost=pl.CostEstimate(flops=3 * 10**9, bytes_accessed=16 * 10**6, transcendentals=0),
    )(meta, *arrays, main, late)


def expert_kernel(rows_ref, over_ref, up_ref, down_hbm, out_ref, wide, spread, down_ref, mixed, done):
    step = pl.program_id(0)
    width = down_ref.shape[2]
    fetch = pltpu.make_async_copy(down_hbm, down_ref, done)

    def act(value):
        return (value / (1.0 + jnp.exp(-value))).astype(BF16)

    first = step == 0

    @pl.when(first)
    def _():
        fetch.start()
        widen(wide, over_ref)
        for segment in range(SLOTS):
            columns = slice(segment * SEG, (segment + 1) * SEG)
            mixed[:ROWS, columns] = rows_ref[:, columns]
            mixed[ROWS:, columns] = gather_rows(wide, segment)
        inner = act(dot(mixed[...], up_ref[0]))
        fetch.wait()
        for segment in range(SLOTS):
            columns = slice(segment * SEG, (segment + 1) * SEG)
            made = dot(inner, down_ref[0, :, columns])
            out_ref[:, columns] = made[:ROWS].astype(BF16)
            scatter_rows(wide, segment, made[ROWS:])
        spread[...] = narrow(wide)

    @pl.when(jnp.logical_not(first))
    def _():
        inner = act(dot(rows_ref[:, :width], up_ref[0]))
        for start in range(0, width, DOWN_COLUMNS):
            columns = slice(start, start + DOWN_COLUMNS)
            out_ref[:, columns] = dot(inner, down_ref[0, :, columns]).astype(BF16)

    mine = pl.ds(pl.multiple_of(step * ROWS, ROWS), ROWS)
    out_ref[:, width:] = spread[mine, :]


def experts(arrived, up, down):
    rows, columns = arrived.shape
    inner = up.shape[2]
    return call(
        expert_kernel,
        "experts",
        jax.ShapeDtypeStruct((rows, columns), BF16),
        [
            pl.BlockSpec((ROWS, columns), lambda i: (i, 0)),
            pl.BlockSpec((rows, SEG), lambda i: (0, SLOTS)),
            vmem(),
            pl.BlockSpec(memory_space=pl.ANY),
        ],
        pl.BlockSpec((ROWS, columns), lambda i: (i, 0)),
        grid=(rows // ROWS,),
        scratch=[
            wide_scratch(),
            pltpu.VMEM((rows, SEG), BF16),
            pltpu.VMEM(down.shape, BF16),
            pltpu.VMEM((ROWS + TOKENS, down.shape[2]), BF16),
            pltpu.SemaphoreType.DMA,
        ],
        limit=46,
        cost=pl.CostEstimate(
            flops=4 * rows * columns * inner,
            bytes_accessed=32 * 10**6,
            transcendentals=rows * inner,
        ),
    )(arrived, arrived, up, down)


def combine_kernel(main, late, rows_ref, over_ref, state, out, total, wide):
    step = pl.program_id(0)
    segments = [(i, slice(i * SEG, (i + 1) * SEG)) for i in range(SLOTS)]

    def both(value):
        return value[:TOKENS] + value[TOKENS:]

    @pl.when(step == 0)
    def _():
        widen(wide, over_ref)
        for segment, columns in segments:
            late_part = both(dot(late[...], gather_rows(wide, segment)))
            total[:, columns] = state[:, columns] + late_part

    for start in range(0, total.shape[1], COMBINE_COLUMNS):
        columns = slice(start, start + COMBINE_COLUMNS)
        total[:, columns] += both(dot(main[...], rows_ref[:, columns]))

    @pl.when(step == pl.num_programs(0) - 1)
    def _():
        out[...] = total[...].astype(BF16)


def combine(main, late, returned, state):
    rows, columns = returned.shape
    return call(
        combine_kernel,
        "combine",
        jax.ShapeDtypeStruct(state.shape, BF16),
        [
            pl.BlockSpec((2 * TOKENS, COMBINE_ROWS), lambda i: (0, i)),
            whole(late),
            pl.BlockSpec((COMBINE_ROWS, columns), lambda i: (i, 0)),
            pl.BlockSpec((rows, SEG), lambda i: (0, SLOTS), pipeline_mode=pl.Buffered(1)),
            whole(state),
        ],
        pl.BlockSpec(state.shape, lambda i: (0, 0)),
        grid=(rows // COMBINE_ROWS,),
        scratch=[pltpu.VMEM(state.shape, F32), wide_scratch()],
        cost=pl.CostEstimate(flops=4 * 10**9, bytes_accessed=13 * 10**6, transcendentals=0),
    )(main, late, returned, returned, state)


def routes_kernel(ids, weights, main, late, back_main, back_late):
    square = (TOKENS, TOKENS)
    row = lax.broadcasted_iota(jnp.int32, square, 0)
    column = lax.broadcasted_iota(jnp.int32, square, 1)
    named, weight = jnp.zeros(square, F32), jnp.zeros(square, F32)
    for choice in range(ids.shape[1]):
        chosen = column == ids[:, choice : choice + 1]
        named = named + jnp.where(chosen, 1.0, 0.0)
        weight = weight + jnp.where(chosen, weights[:, choice : choice + 1], 0.0)
    earlier = jnp.where(column < row, 1.0, 0.0).astype(BF16)
    rank = jnp.where(named > 0.0, dot(earlier, named.astype(BF16)), -1.0)
    high = weight.astype(BF16)
    low = (weight - high.astype(F32)).astype(BF16)

    tall = main.shape
    row = lax.broadcasted_iota(jnp.int32, tall, 0)
    column = lax.broadcasted_iota(jnp.int32, tall, 1)
    spread = jnp.where(row // SLOTS == column, 1.0, 0.0).astype(BF16)
    ranks = dot(spread, rank.T.astype(BF16))
    main[...] = jnp.where(ranks == (row % SLOTS).astype(F32), 1.0, 0.0).astype(BF16)
    late[...] = jnp.where(rank.T == SLOTS, 1.0, 0.0).astype(BF16)

    flat = (TOKENS, tall[0])
    hit = dot_nt(rank.astype(BF16), spread) == (
        lax.broadcasted_iota(jnp.int32, flat, 1) % SLOTS
    ).astype(F32)
    for half, part in enumerate((high, low)):
        rows = slice(half * TOKENS, (half + 1) * TOKENS)
        back_main[rows, :] = jnp.where(hit, dot_nt(part, spread), 0.0).astype(BF16)
        back_late[rows, :] = jnp.where(rank == SLOTS, part.astype(F32), 0.0).astype(BF16)


def routes(expert_ids, route_weights, n_experts):
    outs = [
        jax.ShapeDtypeStruct(shape, BF16)
        for shape in (
            (n_experts * SLOTS, TOKENS),
            (n_experts, TOKENS),
            (2 * TOKENS, n_experts * SLOTS),
            (2 * TOKENS, n_experts),
        )
    ]
    return call(
        routes_kernel,
        "routes",
        outs,
        [whole(expert_ids), whole(route_weights)],
        [pl.BlockSpec(out.shape, lambda: (0, 0)) for out in outs],
        cost=pl.CostEstimate(flops=2 * 10**8, bytes_accessed=10**6, transcendentals=0),
    )(expert_ids, route_weights)


def local(
    queries,
    key_rows,
    value_rows,
    span_order,
    out_proj,
    residual,
    norm_gain,
    expert_ids,
    route_weights,
    w_up,
    w_down,
):
    n_devices = lax.axis_size("dp") * lax.axis_size("ctx") * lax.axis_size("tp")
    core = lax.axis_index("dp") % 2
    ctx = lax.axis_index("ctx")
    x, z = lax.axis_index("tp") // SIDE, lax.axis_index("tp") % SIDE
    meta = jnp.concatenate([span_order, jnp.stack([ctx, x, z, core]).astype(jnp.int32)])

    def head_block(step):
        start = (x + step) % SIDE * HD
        return jnp.concatenate(
            [
                lax.dynamic_slice_in_dim(key_rows, start, HD, 1),
                lax.dynamic_slice_in_dim(value_rows, start, HD, 1),
            ],
            axis=1,
        )

    width = out_proj.shape[1]
    columns_z = width // 256 * 5 // 8 * 128
    columns_x = width // 2 - columns_z

    def weights_part(base, columns):
        return lax.dynamic_slice_in_dim(out_proj, base + core * columns, columns, 1)

    def after(value, *others):
        return lax.optimization_barrier((value, *others))[0]

    own = jnp.stack(exchange(shift_x, [head_block(step) for step in range(SIDE)]))
    other = swap_ctx(own)
    before_own, after_own = shift_z(own, 1), shift_z(own, -1)
    before_other, after_other = shift_z(other, 1), shift_z(other, -1)
    far_own = shift_z(before_own, 1)
    far_other = shift_z(after_other, -1)
    weights_x = gather_rows_of(shift_x, after(weights_part(0, columns_z), own))
    weights_z = gather_rows_of(shift_z, after(weights_part(2 * columns_z, columns_x), far_own, far_other))
    pieces = [
        own,
        other,
        before_own,
        before_other,
        after_own,
        after_other,
        far_own,
        far_other,
    ]


    *far, keys, values = attention(meta, queries, pieces)
    mine, *parts, weights_x, weights_z = attention_end(
        meta, queries, keys, values, far, [*weights_x, *weights_z]
    )
    context_x = exchange(shift_x, [mine, *far])
    other_x = swap_core(after(weights_x, *context_x[1:]))
    context_z = exchange(shift_z, [after(part, *context_x) for part in parts])
    terms_z = projection(6, meta, context_x, [weights_x, other_x])
    terms_z = [after(term, *context_z[1:]) for term in terms_z]
    weights_z = after(weights_z, *terms_z)
    terms_x = projection(5, meta, context_z, [weights_z, swap_core(weights_z)])
    main, late, back_main, back_late = routes(
        after(expert_ids, terms_x[0]), route_weights, n_devices
    )
    terms_z, terms_x = exchange(shift_z, terms_z), exchange(shift_x, terms_x)
    outgoing, state = dispatch(
        meta, terms_x, settle(meta, terms_z, residual), residual, norm_gain[None, :], main, late
    )

    def all_to_all(rows):
        blocks = rows.reshape(n_devices, SLOTS, rows.shape[1])
        return lax.all_to_all(
            blocks, ("dp", "ctx", "tp"), split_axis=0, concat_axis=0, tiled=True
        ).reshape(rows.shape)

    arrived = all_to_all(outgoing)
    returned = all_to_all(experts(arrived, w_up, w_down))
    return combine(back_main, back_late, returned, state)


def solution(mesh):
    return jax.shard_map(
        local,
        mesh=mesh,
        in_specs=(
            P(("dp", "ctx"), "tp"),
            P(("dp", "ctx", "tp"), None),
            P(("dp", "ctx", "tp"), None),
            P(),
            P("tp", None),
            P(("dp", "ctx", "tp"), None),
            P(),
            P(("dp", "ctx", "tp"), None),
            P(("dp", "ctx", "tp"), None),
            P(("dp", "ctx", "tp"), None, None),
            P(("dp", "ctx", "tp"), None, None),
        ),
        out_specs=P(("dp", "ctx", "tp"), None),
        check_vma=False,
    )
```

```python
import functools
import math

import jax
import jax.numpy as jnp
from jax import lax
from jax.experimental import pallas as pl
from jax.experimental.pallas import tpu as pltpu
from jax.sharding import PartitionSpec as P

HD = 128
KVH = 4
SIDE = 4
TOKENS = 128
SLOTS = 8
SEG = 512
ROWS = 256
COMBINE_ROWS = 512
DOWN_COLUMNS = 512
COMBINE_COLUMNS = 512
BLOCK = 512
NEGATIVE = -1e30
MIB = 1 << 20
F32 = jnp.float32
BF16 = jnp.bfloat16


def shift_x(value, step):
    return lax.ppermute(
        value,
        "tp",
        [(x * SIDE + z, (x + step) % SIDE * SIDE + z) for x in range(SIDE) for z in range(SIDE)],
    )


def shift_z(value, step):
    return lax.ppermute(
        value,
        "tp",
        [(x * SIDE + z, x * SIDE + (z + step) % SIDE) for x in range(SIDE) for z in range(SIDE)],
    )


def swap_ctx(value):
    return lax.ppermute(value, "ctx", [(0, 1), (1, 0)])


def swap_core(value):
    return lax.ppermute(value, "dp", [(0, 1), (1, 0), (2, 3), (3, 2)])


def gather_rows_of(shift, rows):
    return [rows, shift(rows, 1), shift(rows, 2), shift(rows, -1)]


def exchange(shift, blocks):
    return [blocks[0], shift(blocks[1], 1), shift(blocks[2], 2), shift(blocks[3], -1)]


def call(kernel, name, out_shape, in_specs, out_specs, grid=(), scratch=(), limit=56, cost=None):
    return pl.pallas_call(
        kernel,
        name=name,
        out_shape=out_shape,
        grid=grid,
        in_specs=in_specs,
        out_specs=out_specs,
        scratch_shapes=list(scratch),
        compiler_params=pltpu.CompilerParams(vmem_limit_bytes=limit * MIB),
        cost_estimate=cost,
    )


def smem():
    return pl.BlockSpec(memory_space=pltpu.SMEM)


def vmem():
    return pl.BlockSpec(memory_space=pltpu.VMEM)


def whole(array):
    zeros = (0,) * array.ndim
    return pl.BlockSpec(array.shape, lambda *_: zeros, pipeline_mode=pl.Buffered(1))


def dot(left, right):
    return jnp.dot(left, right, preferred_element_type=F32)


def dot_nt(left, right):
    return lax.dot_general(left, right, (((1,), (1,)), ((), ())), preferred_element_type=F32)


def rows_of(chunk):
    return pl.ds(pl.multiple_of(chunk * BLOCK, BLOCK), BLOCK)


def attend(meta, chunk, q_ref, keys, values, scratch):
    sums, peaks, totals, even, odd = scratch[0], scratch[1], scratch[2], scratch[3:5], scratch[5:7]
    factor = math.log2(math.e) / math.sqrt(HD)
    mine = meta[meta[4] * 2 + chunk // 2] * 2 + lax.rem(chunk, 2)
    heads = [q_ref[rows_of(chunk), head * HD : (head + 1) * HD] for head in range(2)]
    for head in range(2):
        sums[head] = jnp.zeros((HD, BLOCK), F32)
        peaks[head] = jnp.full((1, BLOCK), NEGATIVE, F32)
        totals[head] = jnp.zeros((1, BLOCK), F32)

    def score(number, held):
        key_block = keys[rows_of(number), :]
        for head in range(2):
            held[head][...] = dot_nt(key_block, heads[head])

    def update(head, scores, value_block, start):
        peak = peaks[head, :, start:]
        new_peak = jnp.maximum(peak, jnp.max(scores, axis=0, keepdims=True))
        weights = jnp.exp2(scores * factor - new_peak * factor)
        fading = jnp.exp2((peak - new_peak) * factor)
        peaks[head, :, start:] = new_peak
        totals[head, :, start:] = totals[head, :, start:] * fading + jnp.sum(
            weights, axis=0, keepdims=True
        )
        sums[head, :, start:] = sums[head, :, start:] * fading + dot(
            value_block, weights.astype(BF16)
        )

    def process(number, held):
        value_block = values[:, rows_of(number)]
        for head in range(2):
            update(head, held[head][...], value_block, 0)

    def process_last(number, held):
        half = BLOCK // 2
        for part in range(2):
            start = part * half
            columns = pl.ds(pl.multiple_of(number * BLOCK + start, half), half)
            value_block = values[:, columns]
            shape = (half, BLOCK - start)
            seen = lax.broadcasted_iota(jnp.int32, shape, 0) <= lax.broadcasted_iota(
                jnp.int32, shape, 1
            )
            for head in range(2):
                scores = held[head][start : start + half, start:]
                update(head, jnp.where(seen, scores, NEGATIVE), value_block, start)

    score(0, even)

    def two(pair, carry):
        score(2 * pair + 1, odd)
        process(2 * pair, even)
        score(2 * pair + 2, even)
        process(2 * pair + 1, odd)
        return carry

    lax.fori_loop(0, mine // 2, two, 0)

    @pl.when(lax.rem(mine, 2) == 1)
    def _():
        score(mine, odd)
        process(mine - 1, even)
        process_last(mine, odd)

    @pl.when(lax.rem(mine, 2) == 0)
    def _():
        process_last(mine, even)

    return jnp.concatenate(
        [(sums[head] / totals[head]).T.astype(BF16) for head in range(2)], axis=1
    )


def attend_scratch():
    return [
        pltpu.VMEM((2, HD, BLOCK), F32),
        pltpu.VMEM((2, 1, BLOCK), F32),
        pltpu.VMEM((2, 1, BLOCK), F32),
    ] + [pltpu.VMEM((BLOCK, BLOCK), F32)] * 4


def attention_kernel(meta, q_ref, *refs):
    pieces, refs = refs[:8], refs[8:]
    outs, keys, values, context, scratch = refs[:3], *refs[3:6], refs[6:]
    ctx, x, z = meta[4], meta[5], meta[6]

    for number, piece in enumerate(pieces):
        part = lax.rem(ctx + number % 2, 2)
        back = (0, 1, 3, 2)[number // 2]
        z_of = lax.rem(z + SIDE - back, SIDE)
        for block in range(SIDE):
            x_of = lax.rem(x + SIDE - block, SIDE)
            place = meta[part * 2 + x_of // 2] * 8 + lax.rem(x_of, 2) * SIDE + z_of
            rows = pl.ds(pl.multiple_of(place * HD, HD), HD)
            keys[rows, :] = piece[block, :, :HD]
            values[:, rows] = piece[block, :, HD:].T

    @pl.loop(0, SIDE - 1)
    def _(number):
        chunk = lax.rem(x + 1 + number, SIDE)
        context[number] = attend(meta, chunk, q_ref, keys, values, scratch)

    for number, out in enumerate(outs):
        out[...] = context[number]


def attention(meta, queries, pieces):
    rows, width = queries.shape
    arrays = (queries, *pieces)
    outs = [jax.ShapeDtypeStruct((BLOCK, width), BF16)] * 3 + [
        jax.ShapeDtypeStruct((2 * rows, HD), BF16),
        jax.ShapeDtypeStruct((HD, 2 * rows), BF16),
    ]
    return call(
        attention_kernel,
        "attention",
        outs,
        [smem()] + [whole(array) for array in arrays],
        [pl.BlockSpec(out.shape, lambda: (0, 0)) for out in outs],
        scratch=[pltpu.VMEM((3, BLOCK, width), BF16), *attend_scratch()],
        cost=pl.CostEstimate(
            flops=16 * 10**9, bytes_accessed=7 * 10**6, transcendentals=10 * 10**6
        ),
    )(meta, *arrays)


def attention_end_kernel(meta, q_ref, keys, values, *refs):
    others, weights, out, refs = refs[:3], refs[3:11], refs[11], refs[12:]
    outs_z, joined, held, refs = refs[:4], refs[4:6], refs[6:8], refs[8:]
    came, went, scratch = refs[0], refs[1], refs[2:]
    x, z = meta[5], meta[6]
    depth = weights[0].shape[0]
    arriving = [
        pltpu.make_async_copy(
            piece,
            held[number // SIDE].at[pl.ds(number % SIDE * depth, depth), :],
            came.at[number],
        )
        for number, piece in enumerate(weights)
    ]
    leaving = [
        pltpu.make_async_copy(held[number], whole_of, went.at[number])
        for number, whole_of in enumerate(joined)
    ]
    for copy in arriving:
        copy.start()
    out[...] = attend(meta, x, q_ref, keys, values, scratch)
    for copy in arriving:
        copy.wait()
    for copy in leaving:
        copy.start()
    for number, context in enumerate((out, *others)):
        x_of = lax.rem(x + number, SIDE)
        rows = pl.ds(pl.multiple_of(x_of * TOKENS, TOKENS), TOKENS)
        for step_of in range(SIDE):
            to_z = lax.rem(z + step_of, SIDE)
            part = pl.ds(pl.multiple_of(to_z * TOKENS, TOKENS), TOKENS)
            outs_z[step_of][rows, :] = context[part, :]
    for copy in leaving:
        copy.wait()


def attention_end(meta, queries, keys, values, others, weights):
    width = queries.shape[1]
    arrays = (queries, keys, values, *others)
    outs = [jax.ShapeDtypeStruct((BLOCK, width), BF16)] * 5
    joined = [
        jax.ShapeDtypeStruct((SIDE * piece.shape[0], piece.shape[1]), BF16)
        for piece in weights[::SIDE]
    ]
    anywhere = pl.BlockSpec(memory_space=pl.ANY)
    return call(
        attention_end_kernel,
        "attention_end",
        outs + joined,
        [smem()] + [whole(array) for array in arrays] + [anywhere] * len(weights),
        [pl.BlockSpec(out.shape, lambda: (0, 0)) for out in outs] + [anywhere] * 2,
        scratch=[
            *[pltpu.VMEM(whole_of.shape, BF16) for whole_of in joined],
            pltpu.SemaphoreType.DMA((2 * SIDE,)),
            pltpu.SemaphoreType.DMA((2,)),
            *attend_scratch(),
        ],
        cost=pl.CostEstimate(
            flops=6 * 10**9, bytes_accessed=7 * 10**6, transcendentals=3 * 10**6
        ),
    )(meta, *arrays, *weights)


def projection_kernel(axis, meta, *refs):
    context, weights, outs, held = refs[:4], refs[4:6], refs[6:10], refs[10]
    step, me = pl.program_id(0), meta[axis]
    width = context[0].shape[1]
    columns = weights[0].shape[1]
    steps = held.shape[1] // (2 * columns)
    for side, weight in enumerate(weights):
        total = None
        for number, rows in enumerate(context):
            term = dot(rows[...], weight[number * width : (number + 1) * width, :])
            total = term if total is None else total + term
        start = pl.multiple_of((side * steps + step) * columns, columns)
        held[:, pl.ds(start, columns)] = total.astype(BF16)

    @pl.when(step == steps - 1)
    def _():
        for number, out in enumerate(outs):
            to = lax.rem(me + number, SIDE)
            out[...] = held[pl.ds(pl.multiple_of(to * TOKENS, TOKENS), TOKENS), :]


def projection(axis, meta, context, weights):
    depth, columns = weights[0].shape
    part = 256
    return call(
        functools.partial(projection_kernel, axis),
        "projection",
        [jax.ShapeDtypeStruct((TOKENS, 2 * columns), BF16)] * 4,
        [smem()]
        + [whole(array) for array in context]
        + [pl.BlockSpec((depth, part), lambda i: (0, i))] * 2,
        [pl.BlockSpec((TOKENS, 2 * columns), lambda i: (0, 0))] * 4,
        grid=(columns // part,),
        scratch=[pltpu.VMEM((SIDE * TOKENS, 2 * columns), BF16)],
        cost=pl.CostEstimate(
            flops=4 * 512 * 1024 * columns, bytes_accessed=7 * 10**6, transcendentals=0
        ),
    )(meta, *context, *weights)


def wide_scratch(rows=TOKENS * SLOTS):
    return pltpu.VMEM((SEG // HD, rows, HD), F32)


def widen(wide, rows_ref):
    for part in range(SEG // HD):
        wide[part] = rows_ref[:, part * HD : (part + 1) * HD].astype(F32)


def narrow(wide):
    return jnp.concatenate([wide[part].astype(BF16) for part in range(SEG // HD)], axis=1)


def gather_rows(wide, segment):
    rows = pl.ds(segment, wide.shape[1] // SLOTS, stride=SLOTS)
    return jnp.concatenate([wide[part, rows, :] for part in range(SEG // HD)], axis=1).astype(BF16)


def scatter_rows(wide, segment, value):
    rows = pl.ds(segment, value.shape[0], stride=SLOTS)
    for part in range(SEG // HD):
        wide[part, rows, :] = value[:, part * HD : (part + 1) * HD]


def add_terms(core, terms, residual, state, base):
    quarter = terms[0].shape[1] // 2
    for side in range(2):
        place = base + quarter * lax.rem(core + side, 2)
        columns = pl.ds(pl.multiple_of(place, quarter), quarter)
        part = slice(side * quarter, (side + 1) * quarter)
        total = terms[0][:, part].astype(F32)
        for term in terms[1:]:
            total = total + term[:, part].astype(F32)
        state[:, columns] = residual[:, columns].astype(F32) + total


def settle_kernel(meta, *refs):
    terms, (residual, state) = refs[:4], refs[4:]
    add_terms(meta[7], terms, residual, state, 0)


def settle(meta, terms, residual):
    half = terms[0].shape[1]
    return call(
        settle_kernel,
        "settle",
        jax.ShapeDtypeStruct((TOKENS, half), F32),
        [smem()]
        + [whole(term) for term in terms]
        + [pl.BlockSpec((TOKENS, half), lambda i: (0, 0))],
        pl.BlockSpec((TOKENS, half), lambda i: (0, 0)),
        grid=(1,),
        cost=pl.CostEstimate(flops=2 * 10**10, bytes_accessed=4 * 10**6, transcendentals=0),
    )(meta, *terms, residual)


def dispatch_kernel(meta, *refs):
    terms, refs = refs[:4], refs[4:]
    first, residual, gain, main, late, outgoing, state, normed, wide = refs
    step = pl.program_id(0)
    half = first.shape[1]

    @pl.when(step == 0)
    def _():
        state[:, :half] = first[...]
        add_terms(meta[7], terms, residual, state, half)
        value = state[...]
        scale = lax.rsqrt(jnp.mean(value * value, axis=1, keepdims=True) + 1e-06)
        for segment in range(SLOTS):
            columns = slice(segment * SEG, (segment + 1) * SEG)
            normed[:, columns] = (state[:, columns] * scale * gain[:, columns]).astype(BF16)

    rows = outgoing.shape[0]
    picks = jnp.concatenate([main[...], late[...]], axis=0)
    for segment in range(SLOTS):
        columns = slice(segment * SEG, (segment + 1) * SEG)
        picked = dot(picks, normed[:, columns])
        outgoing[:, columns] = picked[:rows].astype(BF16)
        scatter_rows(wide, segment, picked[rows:])
    outgoing[:, state.shape[1] :] = narrow(wide)


def dispatch(meta, terms, first, residual, gain, main, late):
    rows, width = main.shape[0], residual.shape[1]
    arrays = (*terms, first, residual, gain)
    return call(
        dispatch_kernel,
        "dispatch",
        [
            jax.ShapeDtypeStruct((rows, width + SEG), BF16),
            jax.ShapeDtypeStruct((TOKENS, width), F32),
        ],
        [smem()]
        + [whole(a) for a in arrays]
        + [pl.BlockSpec((count, TOKENS), lambda i: (i, 0)) for count in (ROWS, ROWS // SLOTS)],
        [
            pl.BlockSpec((ROWS, width + SEG), lambda i: (i, 0)),
            pl.BlockSpec((TOKENS, width), lambda i: (0, 0)),
        ],
        grid=(rows // ROWS,),
        scratch=[
            pltpu.VMEM((TOKENS, width), BF16),
            wide_scratch(ROWS),
        ],
        cost=pl.CostEstimate(flops=3 * 10**9, bytes_accessed=16 * 10**6, transcendentals=0),
    )(meta, *arrays, main, late)


def expert_kernel(rows_ref, over_ref, up_ref, down_hbm, out_ref, wide, spread, down_ref, mixed, done):
    step = pl.program_id(0)
    width = down_ref.shape[2]
    fetch = pltpu.make_async_copy(down_hbm, down_ref, done)

    def act(value):
        return (value / (1.0 + jnp.exp(-value))).astype(BF16)

    first = step == 0

    @pl.when(first)
    def _():
        fetch.start()
        widen(wide, over_ref)
        for segment in range(SLOTS):
            columns = slice(segment * SEG, (segment + 1) * SEG)
            mixed[:ROWS, columns] = rows_ref[:, columns]
            mixed[ROWS:, columns] = gather_rows(wide, segment)
        inner = act(dot(mixed[...], up_ref[0]))
        fetch.wait()
        for segment in range(SLOTS):
            columns = slice(segment * SEG, (segment + 1) * SEG)
            made = dot(inner, down_ref[0, :, columns])
            out_ref[:, columns] = made[:ROWS].astype(BF16)
            scatter_rows(wide, segment, made[ROWS:])
        spread[...] = narrow(wide)

    @pl.when(jnp.logical_not(first))
    def _():
        inner = act(dot(rows_ref[:, :width], up_ref[0]))
        for start in range(0, width, DOWN_COLUMNS):
            columns = slice(start, start + DOWN_COLUMNS)
            out_ref[:, columns] = dot(inner, down_ref[0, :, columns]).astype(BF16)

    mine = pl.ds(pl.multiple_of(step * ROWS, ROWS), ROWS)
    out_ref[:, width:] = spread[mine, :]


def experts(arrived, up, down):
    rows, columns = arrived.shape
    inner = up.shape[2]
    return call(
        expert_kernel,
        "experts",
        jax.ShapeDtypeStruct((rows, columns), BF16),
        [
            pl.BlockSpec((ROWS, columns), lambda i: (i, 0)),
            pl.BlockSpec((rows, SEG), lambda i: (0, SLOTS)),
            vmem(),
            pl.BlockSpec(memory_space=pl.ANY),
        ],
        pl.BlockSpec((ROWS, columns), lambda i: (i, 0)),
        grid=(rows // ROWS,),
        scratch=[
            wide_scratch(),
            pltpu.VMEM((rows, SEG), BF16),
            pltpu.VMEM(down.shape, BF16),
            pltpu.VMEM((ROWS + TOKENS, down.shape[2]), BF16),
            pltpu.SemaphoreType.DMA,
        ],
        limit=46,
        cost=pl.CostEstimate(
            flops=4 * rows * columns * inner,
            bytes_accessed=32 * 10**6,
            transcendentals=rows * inner,
        ),
    )(arrived, arrived, up, down)


def combine_kernel(main, late, rows_ref, over_ref, state, out, total, wide):
    step = pl.program_id(0)
    segments = [(i, slice(i * SEG, (i + 1) * SEG)) for i in range(SLOTS)]

    def both(value):
        return value[:TOKENS] + value[TOKENS:]

    @pl.when(step == 0)
    def _():
        widen(wide, over_ref)
        for segment, columns in segments:
            late_part = both(dot(late[...], gather_rows(wide, segment)))
            total[:, columns] = state[:, columns] + late_part

    for start in range(0, total.shape[1], COMBINE_COLUMNS):
        columns = slice(start, start + COMBINE_COLUMNS)
        total[:, columns] += both(dot(main[...], rows_ref[:, columns]))

    @pl.when(step == pl.num_programs(0) - 1)
    def _():
        out[...] = total[...].astype(BF16)


def combine(main, late, returned, state):
    rows, columns = returned.shape
    return call(
        combine_kernel,
        "combine",
        jax.ShapeDtypeStruct(state.shape, BF16),
        [
            pl.BlockSpec((2 * TOKENS, COMBINE_ROWS), lambda i: (0, i)),
            whole(late),
            pl.BlockSpec((COMBINE_ROWS, columns), lambda i: (i, 0)),
            pl.BlockSpec((rows, SEG), lambda i: (0, SLOTS), pipeline_mode=pl.Buffered(1)),
            whole(state),
        ],
        pl.BlockSpec(state.shape, lambda i: (0, 0)),
        grid=(rows // COMBINE_ROWS,),
        scratch=[pltpu.VMEM(state.shape, F32), wide_scratch()],
        cost=pl.CostEstimate(flops=4 * 10**9, bytes_accessed=13 * 10**6, transcendentals=0),
    )(main, late, returned, returned, state)


def routes_kernel(ids, weights, main, late, back_main, back_late):
    square = (TOKENS, TOKENS)
    row = lax.broadcasted_iota(jnp.int32, square, 0)
    column = lax.broadcasted_iota(jnp.int32, square, 1)
    named, weight = jnp.zeros(square, F32), jnp.zeros(square, F32)
    for choice in range(ids.shape[1]):
        chosen = column == ids[:, choice : choice + 1]
        named = named + jnp.where(chosen, 1.0, 0.0)
        weight = weight + jnp.where(chosen, weights[:, choice : choice + 1], 0.0)
    earlier = jnp.where(column < row, 1.0, 0.0).astype(BF16)
    rank = jnp.where(named > 0.0, dot(earlier, named.astype(BF16)), -1.0)
    high = weight.astype(BF16)
    low = (weight - high.astype(F32)).astype(BF16)

    tall = main.shape
    row = lax.broadcasted_iota(jnp.int32, tall, 0)
    column = lax.broadcasted_iota(jnp.int32, tall, 1)
    spread = jnp.where(row // SLOTS == column, 1.0, 0.0).astype(BF16)
    ranks = dot(spread, rank.T.astype(BF16))
    main[...] = jnp.where(ranks == (row % SLOTS).astype(F32), 1.0, 0.0).astype(BF16)
    late[...] = jnp.where(rank.T == SLOTS, 1.0, 0.0).astype(BF16)

    flat = (TOKENS, tall[0])
    hit = dot_nt(rank.astype(BF16), spread) == (
        lax.broadcasted_iota(jnp.int32, flat, 1) % SLOTS
    ).astype(F32)
    for half, part in enumerate((high, low)):
        rows = slice(half * TOKENS, (half + 1) * TOKENS)
        back_main[rows, :] = jnp.where(hit, dot_nt(part, spread), 0.0).astype(BF16)
        back_late[rows, :] = jnp.where(rank == SLOTS, part.astype(F32), 0.0).astype(BF16)


def routes(expert_ids, route_weights, n_experts):
    outs = [
        jax.ShapeDtypeStruct(shape, BF16)
        for shape in (
            (n_experts * SLOTS, TOKENS),
            (n_experts, TOKENS),
            (2 * TOKENS, n_experts * SLOTS),
            (2 * TOKENS, n_experts),
        )
    ]
    return call(
        routes_kernel,
        "routes",
        outs,
        [whole(expert_ids), whole(route_weights)],
        [pl.BlockSpec(out.shape, lambda: (0, 0)) for out in outs],
        cost=pl.CostEstimate(flops=2 * 10**8, bytes_accessed=10**6, transcendentals=0),
    )(expert_ids, route_weights)


def local(
    queries,
    key_rows,
    value_rows,
    span_order,
    out_proj,
    residual,
    norm_gain,
    expert_ids,
    route_weights,
    w_up,
    w_down,
):
    n_devices = lax.axis_size("dp") * lax.axis_size("ctx") * lax.axis_size("tp")
    core = lax.axis_index("dp") % 2
    ctx = lax.axis_index("ctx")
    x, z = lax.axis_index("tp") // SIDE, lax.axis_index("tp") % SIDE
    meta = jnp.concatenate([span_order, jnp.stack([ctx, x, z, core]).astype(jnp.int32)])

    def head_block(step):
        start = (x + step) % SIDE * HD
        return jnp.concatenate(
            [
                lax.dynamic_slice_in_dim(key_rows, start, HD, 1),
                lax.dynamic_slice_in_dim(value_rows, start, HD, 1),
            ],
            axis=1,
        )

    width = out_proj.shape[1]
    columns_z = width // 4
    columns_x = width // 2 - columns_z

    def weights_part(base, columns):
        return lax.dynamic_slice_in_dim(out_proj, base + core * columns, columns, 1)

    def after(value, *others):
        return lax.optimization_barrier((value, *others))[0]

    own = jnp.stack(exchange(shift_x, [head_block(step) for step in range(SIDE)]))
    other = swap_ctx(own)
    before_own, after_own = shift_z(own, 1), shift_z(own, -1)
    before_other, after_other = shift_z(other, 1), shift_z(other, -1)
    far_own = shift_z(before_own, 1)
    far_other = shift_z(after_other, -1)
    weights_x = gather_rows_of(shift_x, after(weights_part(0, columns_z), own))
    weights_z = gather_rows_of(shift_z, after(weights_part(2 * columns_z, columns_x), far_own, far_other))
    pieces = [
        own,
        other,
        before_own,
        before_other,
        after_own,
        after_other,
        far_own,
        far_other,
    ]


    *far, keys, values = attention(meta, queries, pieces)
    mine, *parts, weights_x, weights_z = attention_end(
        meta, queries, keys, values, far, [*weights_x, *weights_z]
    )
    context_x = exchange(shift_x, [mine, *far])
    other_x = swap_core(after(weights_x, *context_x[1:]))
    context_z = exchange(shift_z, [after(part, *context_x) for part in parts])
    terms_z = projection(6, meta, context_x, [weights_x, other_x])
    terms_z = [after(term, *context_z[1:]) for term in terms_z]
    weights_z = after(weights_z, *terms_z)
    terms_x = projection(5, meta, context_z, [weights_z, swap_core(weights_z)])
    main, late, back_main, back_late = routes(
        after(expert_ids, terms_x[0]), route_weights, n_devices
    )
    terms_z, terms_x = exchange(shift_z, terms_z), exchange(shift_x, terms_x)
    outgoing, state = dispatch(
        meta, terms_x, settle(meta, terms_z, residual), residual, norm_gain[None, :], main, late
    )

    def all_to_all(rows):
        blocks = rows.reshape(n_devices, SLOTS, rows.shape[1])
        return lax.all_to_all(
            blocks, ("dp", "ctx", "tp"), split_axis=0, concat_axis=0, tiled=True
        ).reshape(rows.shape)

    arrived = all_to_all(outgoing)
    returned = all_to_all(experts(arrived, w_up, w_down))
    return combine(back_main, back_late, returned, state)


def solution(mesh):
    return jax.shard_map(
        local,
        mesh=mesh,
        in_specs=(
            P(("dp", "ctx"), "tp"),
            P(("dp", "ctx", "tp"), None),
            P(("dp", "ctx", "tp"), None),
            P(),
            P("tp", None),
            P(("dp", "ctx", "tp"), None),
            P(),
            P(("dp", "ctx", "tp"), None),
            P(("dp", "ctx", "tp"), None),
            P(("dp", "ctx", "tp"), None, None),
            P(("dp", "ctx", "tp"), None, None),
        ),
        out_specs=P(("dp", "ctx", "tp"), None),
        check_vma=False,
    )
```
